32 devices in a mesh: wide: 8 (over z, x), narrow: 4 (over y, core).
Axes of the slice: x: 2, y: 2, z: 4, core: 2. Of those that a mesh axis runs over, the one named last changes fastest.
Arguments:
- doc_tokens: bfloat16 [8, 512, 768], P('wide', 'narrow'), may hold values from -6 to 6
- query_tokens: bfloat16 [128, 32, 768], P('wide'), may hold values from -6 to 6
- query_lengths: int32 [128], P('wide'), may hold values from 8 to 32, as said below
- positive_docs: int32 [128], P('wide'), may hold values from 0 to 7
- retrieved: int32 [128, 32, 128], P('wide'), may hold values from 0 to 4095
- attend_gain: float32 [768], replicated, may hold values from 0.5 to 1.5
- query_weight: bfloat16 [768, 768], replicated, may hold values from -0.109375 to 0.109375
- key_weight: bfloat16 [768, 768], replicated, may hold values from -0.109375 to 0.109375
- value_weight: bfloat16 [768, 768], replicated, may hold values from -0.21875 to 0.21875
- output_weight: bfloat16 [768, 768], replicated, may hold values from -0.625 to 0.625
- bias_table: float32 [32, 12], replicated, may hold values from -4 to 4
- feed_gain: float32 [768], replicated, may hold values from 0.5 to 1.5
- gate_weight: bfloat16 [768, 2048], replicated, may hold values from -0.21875 to 0.21875
- up_weight: bfloat16 [768, 2048], replicated, may hold values from -0.21875 to 0.21875
- down_weight: bfloat16 [2048, 768], replicated, may hold values from -0.125 to 0.125
- final_gain: float32 [768], replicated, may hold values from 0.5 to 1.5
- proj_weight: bfloat16 [768, 128], replicated, may hold values from -0.21875 to 0.21875
Outputs:
- losses: float32 [128], P(('wide', 'narrow'))
- doc_grad: float32 [8, 512, 768], P('wide', 'narrow')
- query_grad: float32 [128, 32, 768], P(('wide', 'narrow'))
- attend_gain_grad: float32 [768], P(('wide', 'narrow'))
- query_weight_grad: float32 [768, 768], P(('wide', 'narrow'))
- key_weight_grad: float32 [768, 768], P(('wide', 'narrow'))
- value_weight_grad: float32 [768, 768], P(('wide', 'narrow'))
- output_weight_grad: float32 [768, 768], P(('wide', 'narrow'))
- bias_table_grad: float32 [32, 12], replicated
- feed_gain_grad: float32 [768], P(('wide', 'narrow'))
- gate_weight_grad: float32 [768, 2048], P(('wide', 'narrow'))
- up_weight_grad: float32 [768, 2048], P(('wide', 'narrow'))
- down_weight_gradient: float32 [2048, 768], P(('wide', 'narrow'))
- final_gain_grad: float32 [768], P(('wide', 'narrow'))
- proj_weight_grad: float32 [768, 128], P(('wide', 'narrow'))
The draws below stay inside these ranges and needn't reach their ends.
Inputs may be any that keep to these rules, and one draw needn't show every extreme that they name: `query_lengths`: at least one slot of the batch holds exactly 32 tokens. `retrieved`: an index may repeat within a query token's list.
All inputs are finite; a program needn't handle non-finite values.
Results may differ from the reference program's by a relative error of at most 0.019.
Values may be sent and summed in bfloat16 or wider, within the bound.
No kernel may reach another device: no remote copies, remote signals or barrier semaphores. Data moves between devices by JAX's collectives and lax.ppermute only.
A program may use at most 192 MiB of HBM per device.

```python
import math
import jax
import jax.numpy as jnp
from jax import lax

D = 768
HEADS = 12
HEAD = 64
FF = 2048
BUCKETS = 32
PROJ = 128
LD = 512
QL = 32
QMIN = 8
TOPK = 128
DOCS = 8
QUESTION_COUNT = 128


def draw_query_lengths(key, part):
    key = jax.random.fold_in(key, 11)
    first_key, second_key = jax.random.split(key)
    drawn = jax.random.randint(first_key, (QUESTION_COUNT,), QMIN, QL + 1)
    longest = jax.random.randint(second_key, (), 0, QUESTION_COUNT)
    return jnp.where(jnp.arange(QUESTION_COUNT) == longest, QL, drawn).astype(jnp.int32)


def set_ends(values, rng, least, high):
    longest = values.shape.index(max(values.shape))
    spots = []
    for shift in (0, 1):
        where = [jax.random.randint(jax.random.fold_in(rng, axis), (), 0, length) for axis, length in enumerate(values.shape)]
        where[longest] = (where[longest] + shift) % values.shape[longest]
        spots.append(tuple(where))
    return values.at[spots[0]].set(least).at[spots[1]].set(high)


def block_scale(stream_key, shape, cuts, low, largest):
    factor_of = 1.0
    for dim, parts in cuts:
        steps = jax.random.uniform(jax.random.fold_in(jax.random.fold_in(stream_key, 6), dim), (parts,), jnp.float32, low / len(cuts), largest / len(cuts))
        factor_of = factor_of * jnp.repeat(jnp.exp(steps), shape[dim] // parts).reshape((-1,) + (1,) * (len(shape) - 1 - dim))
    return factor_of


def scatter_about(rng, shape, spread, reach, cuts=(), kind=jnp.bfloat16):
    entries = spread * jax.random.normal(rng, shape, jnp.float32)
    if cuts:
        entries = entries * block_scale(rng, shape, cuts, -0.22, 0.18)
    return jnp.clip(entries, -reach, reach).astype(kind)


def setup_inputs(seed: int = 0) -> dict:
    key_of = jax.random.split(jax.random.key(seed), 18)
    doc_tokens = scatter_about(key_of[0], (DOCS, LD, D), 1.0, 6.0, ((0, 8), (1, 4)))
    query_tokens = scatter_about(key_of[1], (QUESTION_COUNT, QL, D), 1.0, 6.0, ((0, 8),))
    query_lengths = draw_query_lengths(jax.random.fold_in(key_of[17], 71), 0)
    positive_docs = set_ends(jax.random.randint(key_of[3], (QUESTION_COUNT,), 0, DOCS), jax.random.fold_in(key_of[3], 1), 0, DOCS - 1).astype(jnp.int32)
    retrieved = set_ends(jax.random.randint(key_of[4], (QUESTION_COUNT, QL, TOPK), 0, DOCS * LD), jax.random.fold_in(key_of[4], 1), 0, (DOCS * LD) - 1).astype(jnp.int32)
    attend_gain = jnp.clip(1.0 + 0.1 * jax.random.normal(key_of[5], (D,), jnp.float32), 0.5, 1.5)
    query_weight = scatter_about(key_of[6], (D, D), (4 * D) ** -0.5, 0.109375)
    key_weight = scatter_about(key_of[7], (D, D), (4 * D) ** -0.5, 0.109375)
    value_weight = scatter_about(key_of[8], (D, D), D ** -0.5, 0.21875)
    output_weight = scatter_about(key_of[9], (D, D), (D // 8) ** -0.5, 0.625)
    bias_table = scatter_about(key_of[10], (BUCKETS, HEADS), 1.0, 4.0, (), jnp.float32)
    feed_gain = jnp.clip(1.0 + 0.1 * jax.random.normal(key_of[11], (D,), jnp.float32), 0.5, 1.5)
    gate_weight = scatter_about(key_of[12], (D, FF), D ** -0.5, 0.21875)
    up_weight = scatter_about(key_of[13], (D, FF), D ** -0.5, 0.21875)
    down_weight = scatter_about(key_of[14], (FF, D), FF ** -0.5, 0.125)
    final_gain = jnp.clip(1.0 + 0.1 * jax.random.normal(key_of[15], (D,), jnp.float32), 0.5, 1.5)
    proj_weight = scatter_about(key_of[16], (D, PROJ), D ** -0.5, 0.21875)
    return dict(doc_tokens=doc_tokens, query_tokens=query_tokens, query_lengths=query_lengths, positive_docs=positive_docs, retrieved=retrieved, attend_gain=attend_gain, query_weight=query_weight, key_weight=key_weight, value_weight=value_weight, output_weight=output_weight, bias_table=bias_table, feed_gain=feed_gain, gate_weight=gate_weight, up_weight=up_weight, down_weight=down_weight, final_gain=final_gain, proj_weight=proj_weight)


epsilon = 1e-06
contrastive_sharpness_factor = 0.01
masked_value = -1000000000.0
bucket_edges = (12, 16, 23, 32, 46, 64, 91)
highest = lax.Precision.HIGHEST

@jax.custom_vjp
def low(v):
    return lax.optimization_barrier(v.astype(jnp.bfloat16)).astype(jnp.float32)

@jax.custom_vjp
def low_back(v):
    return v

def low_keep(v):
    return (low(v), None)

def low_pass(kept, grad):
    return (grad,)

def back_keep(v):
    return (v, None)

def back_low(kept, grad):
    return (low(grad),)
low.defvjp(low_keep, low_pass)
low_back.defvjp(back_keep, back_low)

def both_round(value_in):
    return low(low_back(value_in))

def bucket_index(offset):
    distance = jnp.abs(offset)
    beyond = 8 + sum(((distance >= boundary).astype(jnp.int32) for boundary in bucket_edges))
    inside = jnp.where(distance < 8, distance, beyond)
    return inside + BUCKETS // 2 * (offset > 0).astype(jnp.int32)

def position_bias(length, table_f):
    places = jnp.arange(length, dtype=jnp.int32)
    buckets = bucket_index(places[None, :] - places[:, None])
    indicator_matrix = (buckets[:, :, None] == jnp.arange(BUCKETS, dtype=jnp.int32)).astype(jnp.float32)
    return jnp.einsum('ijb,bh->hij', indicator_matrix, table_f, precision=highest)

def rms_norm(values, gain_vec):
    return values * lax.rsqrt(lax.optimization_barrier(jnp.mean(values * values, -1, keepdims=True)) + epsilon) * gain_vec

def matmul_high(leftward_operand, right_side):
    return jnp.matmul(leftward_operand, right_side, precision=highest)

def encode(tokens, pos_bias, key_keep, params):
    attend_gain, query_weight, key_weight, value_weight, output_weight, feed_gain, gate_weight, up_weight, down_weight, final_gain, proj_weight = params
    batch_size = tokens.shape[0]
    length = tokens.shape[1]
    normed = low(rms_norm(tokens, attend_gain))
    query_heads = both_round(matmul_high(normed, query_weight)).reshape(batch_size, length, HEADS, HEAD)
    key_heads = both_round(matmul_high(normed, key_weight)).reshape(batch_size, length, HEADS, HEAD)
    value_heads = both_round(matmul_high(normed, value_weight)).reshape(batch_size, length, HEADS, HEAD)
    scores = low_back(jnp.einsum('bihd,bjhd->bhij', query_heads, key_heads, precision=highest) + pos_bias[None])
    scores = jnp.where(key_keep[:, None, None, :], scores, masked_value)
    probs_round = low(jax.nn.softmax(scores, axis=-1))
    mixed_heads = both_round(jnp.einsum('bhij,bjhd->bihd', probs_round, value_heads, precision=highest))
    mixed_heads = mixed_heads.reshape(batch_size, length, D)
    after_attend = tokens + low_back(matmul_high(mixed_heads, output_weight))
    normed_feed = low(rms_norm(after_attend, feed_gain))
    gate_value = low_back(matmul_high(normed_feed, gate_weight))
    upward = low_back(matmul_high(normed_feed, up_weight))
    hidden = low(jax.nn.gelu(gate_value, approximate=True) * upward)
    after_feed = after_attend + low_back(matmul_high(hidden, down_weight))
    normed_final = low(rms_norm(after_feed, final_gain))
    embedded = low_back(matmul_high(normed_final, proj_weight))
    return low(embedded * lax.rsqrt(lax.optimization_barrier(jnp.sum(embedded * embedded, -1, keepdims=True)) + epsilon))

def pooled_loss(similar, picked, lengths, positives):
    slot_count = similar.shape[0]
    owner_doc = picked // LD
    slot_ids = jnp.arange(slot_count * QL, dtype=jnp.int32).reshape(slot_count, QL, 1) * DOCS + owner_doc
    segments = slot_count * QL * DOCS
    summed = jax.ops.segment_sum(similar.reshape(-1), slot_ids.reshape(-1), num_segments=segments)
    summed = summed.reshape(slot_count, QL, DOCS)
    tallies = jax.ops.segment_sum(jnp.ones_like(similar).reshape(-1), slot_ids.reshape(-1), num_segments=segments)
    tallies = tallies.reshape(slot_count, QL, DOCS)
    pooled = summed / jnp.maximum(tallies, 1.0)
    valid_mask = (jnp.arange(QL, dtype=jnp.int32)[None, :] < lengths[:, None]).astype(jnp.float32)
    weight = jnp.minimum(tallies, 1.0) * valid_mask[:, :, None]
    passage_relevance = lax.optimization_barrier(jnp.sum(weight * pooled, 1)) / jnp.maximum(lax.optimization_barrier(jnp.sum(weight, 1)), 1.0)
    unnormalized_similarity = passage_relevance / contrastive_sharpness_factor
    chosen = lax.optimization_barrier(jnp.sum(jnp.where(jnp.arange(DOCS, dtype=jnp.int32)[None, :] == positives[:, None], unnormalized_similarity, 0.0), 1))
    return jax.nn.logsumexp(unnormalized_similarity, axis=-1) - chosen

def reference(doc_tokens, query_tokens, query_lengths, positive_docs, retrieved, attend_gain, query_weight, key_weight, value_weight, output_weight, bias_table, feed_gain, gate_weight, up_weight, down_weight, final_gain, proj_weight):
    group_size = math.gcd(QUESTION_COUNT, 32)
    blocks = QUESTION_COUNT // group_size
    params_f = (attend_gain.astype(jnp.float32), query_weight.astype(jnp.float32), key_weight.astype(jnp.float32), value_weight.astype(jnp.float32), output_weight.astype(jnp.float32), feed_gain.astype(jnp.float32), gate_weight.astype(jnp.float32), up_weight.astype(jnp.float32), down_weight.astype(jnp.float32), final_gain.astype(jnp.float32), proj_weight.astype(jnp.float32))
    grouped_integers = (query_lengths.reshape(blocks, group_size), positive_docs.reshape(blocks, group_size), retrieved.reshape(blocks, group_size, QL, TOPK))

    def forward_model(documents, queries, params, table_f):
        doc_bias = position_bias(LD, table_f)
        query_bias = position_bias(QL, table_f)
        doc_keep = jnp.ones((1, LD), dtype=bool)

        def one_doc(tokens):
            return encode(tokens[None], doc_bias, doc_keep, params)[0]
        doc_embed = lax.map(jax.checkpoint(one_doc), documents).reshape(DOCS * LD, PROJ)

        def one_group(input_rows):
            tokens, lengths, positives, picked = input_rows
            key_keep = jnp.arange(QL, dtype=jnp.int32)[None, :] < lengths[:, None]
            query_embed = encode(tokens, query_bias, key_keep, params)
            doc_rows = doc_embed[picked]
            similar = jnp.einsum('aikp,aip->aik', doc_rows, query_embed, precision=highest)
            return pooled_loss(similar, picked, lengths, positives)
        grouped = (queries.reshape(blocks, group_size, QL, D), grouped_integers[0], grouped_integers[1], grouped_integers[2])
        return lax.map(jax.checkpoint(one_group), grouped).reshape(QUESTION_COUNT)
    losses, pullback = jax.vjp(forward_model, doc_tokens.astype(jnp.float32), query_tokens.astype(jnp.float32), params_f, bias_table.astype(jnp.float32))
    doc_g, query_g, param_g, table_g = pullback(jnp.ones_like(losses))
    return (losses, doc_g, query_g, param_g[0], param_g[1], param_g[2], param_g[3], param_g[4], table_g, param_g[5], param_g[6], param_g[7], param_g[8], param_g[9], param_g[10])
```

```python
import jax
import jax.numpy as jnp
from jax import lax
from jax.experimental import pallas as pl
from jax.experimental.pallas import tpu as pltpu
from jax.sharding import PartitionSpec as P

BUCKETS = 32


epsilon = 1e-06
contrastive_sharpness_factor = 0.01
masked_value = -1000000000.0
bucket_edges = (12, 16, 23, 32, 46, 64, 91)
highest = lax.Precision.HIGHEST


def bucket_index(offset):
    distance = jnp.abs(offset)
    beyond = 8 + sum(((distance >= boundary).astype(jnp.int32) for boundary in bucket_edges))
    inside = jnp.where(distance < 8, distance, beyond)
    return inside + BUCKETS // 2 * (offset > 0).astype(jnp.int32)


def bucket_onehot(row_places, col_places):
    buckets = bucket_index(col_places[None, :] - row_places[:, None])
    return (buckets[:, :, None] == jnp.arange(BUCKETS, dtype=jnp.int32)).astype(jnp.float32)


def rms_norm(values, gain_vec):
    return values * lax.rsqrt(jnp.mean(values * values, -1, keepdims=True) + epsilon) * gain_vec


def unit_scale(values):
    return values * lax.rsqrt(jnp.sum(values * values, -1, keepdims=True) + epsilon)


def gated_unit(gate_value, up_value):
    return jax.nn.gelu(gate_value, approximate=True) * up_value


def product(leftward_operand, right_side):
    return jnp.dot(leftward_operand, right_side, preferred_element_type=jnp.float32)


def left_product(leftward_operand, right_side):
    return lax.dot_general(
        leftward_operand, right_side, (((0,), (0,)), ((), ())), preferred_element_type=jnp.float32
    )


def right_product(leftward_operand, right_side):
    return lax.dot_general(
        leftward_operand, right_side, (((1,), (1,)), ((), ())), preferred_element_type=jnp.float32
    )


def rank_bits():
    return (lax.axis_size("wide") * lax.axis_size("narrow")).bit_length() - 1


def my_bit(bit):
    rank = lax.axis_index("wide") * lax.axis_size("narrow") + lax.axis_index("narrow")
    return (rank >> bit) & 1


def swap(values, bit):
    ranks = 1 << rank_bits()
    pairs = [(rank, rank ^ (1 << bit)) for rank in range(ranks)]
    return lax.ppermute(values, ("wide", "narrow"), pairs)


def scatter_sum(values, order, last_type=jnp.float32):
    bits = sorted(order, reverse=True)
    tail = (values.shape[0] >> len(bits),) + values.shape[1:]
    values = values.reshape((2,) * len(bits) + tail)
    for step, bit in enumerate(order):
        axis = bits.index(bit)
        bits.pop(axis)
        mine = my_bit(bit)
        kept = lax.dynamic_index_in_dim(values, mine, axis, keepdims=False)
        sent = lax.dynamic_index_in_dim(values, 1 - mine, axis, keepdims=False)
        total = kept.astype(jnp.float32) + swap(sent, bit).astype(jnp.float32)
        values = total.astype(last_type if step == len(order) - 1 else values.dtype)
    return values


def gather_all(values, order):
    bits = []
    tail = values.shape
    for bit in order:
        other = swap(values, bit)
        mine = my_bit(bit)
        first = jnp.where(mine == 0, values, other)
        second = jnp.where(mine == 0, other, values)
        bits_now = sorted(bits + [bit], reverse=True)
        axis = bits_now.index(bit)
        values = jnp.stack([first, second], axis)
        bits = bits_now
    return values.reshape((-1,) + tail[1:])


def sum_all(values):
    for bit in range(rank_bits()):
        values = values + swap(values, bit)
    return values


def count_kernel(places_ref, counts_ref, scratch_ref):
    rows = places_ref.shape[0]
    blocks = counts_ref.shape[0]

    def one_row(row, carry):
        places = places_ref[pl.ds(row, 1), :]
        high = places >> 7
        low = places & 127
        picks = places.shape[1]
        high_hot = (lax.broadcasted_iota(jnp.int32, (blocks, picks), 0) == high).astype(jnp.bfloat16)
        low_hot = (lax.broadcasted_iota(jnp.int32, (128, picks), 0) == low).astype(jnp.bfloat16)
        scratch_ref[pl.ds(row, blocks, stride=rows), :] = right_product(high_hot, low_hot)
        return carry

    lax.fori_loop(0, rows, one_row, 0, unroll=8)
    for block in range(blocks):
        counts_ref[block] = scratch_ref[block * rows : (block + 1) * rows, :].astype(jnp.bfloat16)


def count_places(places, blocks):
    rows = places.shape[0]
    return pl.pallas_call(
        count_kernel,
        out_shape=jax.ShapeDtypeStruct((blocks, rows, 128), jnp.bfloat16),
        in_specs=[pl.BlockSpec(memory_space=pltpu.VMEM)],
        out_specs=pl.BlockSpec(memory_space=pltpu.VMEM),
        scratch_shapes=[pltpu.VMEM((blocks * rows, 128), jnp.float32)],
        compiler_params=pltpu.CompilerParams(vmem_limit_bytes=56 * 1024 * 1024),
    )(places)


def attend_scores(query_heads, key_heads, pos_bias, key_keep):
    scores = jnp.einsum(
        "brhe,bche->bhrc", query_heads, key_heads, preferred_element_type=jnp.float32
    )
    return jnp.where(key_keep[:, None, None, :], scores + pos_bias[None], masked_value)


def attend_forward(query_heads, key_heads, value_heads, pos_bias, key_keep):
    scores = attend_scores(query_heads, key_heads, pos_bias, key_keep)
    top_score = jnp.max(scores, -1, keepdims=True)
    weights = jnp.exp(scores - top_score)
    totals = jnp.sum(weights, -1, keepdims=True)
    probs_round = (weights / totals).astype(jnp.bfloat16)
    mixed_heads = jnp.einsum(
        "bhrc,bche->brhe", probs_round, value_heads, preferred_element_type=jnp.float32
    )
    return (mixed_heads.astype(jnp.bfloat16), top_score + jnp.log(totals))


def attention_pullback_pass(
    query_heads, key_heads, value_heads, pos_bias, key_keep, log_total, grad_mixed
):
    probs = jnp.exp(attend_scores(query_heads, key_heads, pos_bias, key_keep) - log_total)
    grad_probs = jnp.einsum(
        "brhe,bche->bhrc", grad_mixed, value_heads, preferred_element_type=jnp.float32
    )
    grad_values = jnp.einsum(
        "bhrc,brhe->bche",
        probs.astype(jnp.bfloat16),
        grad_mixed,
        preferred_element_type=jnp.float32,
    )
    grad_scores = (probs * (grad_probs - jnp.sum(probs * grad_probs, -1, keepdims=True))).astype(
        jnp.bfloat16
    )
    query_gradients = jnp.einsum(
        "bhrc,bche->brhe", grad_scores, key_heads, preferred_element_type=jnp.float32
    )
    grad_keys = jnp.einsum(
        "bhrc,brhe->bche", grad_scores, query_heads, preferred_element_type=jnp.float32
    )
    return (query_gradients, grad_keys, grad_values, grad_scores)


def pooled_loss(summed, tallies, lengths, positives):
    slot_length = summed.shape[1]
    doc_total = summed.shape[2]
    pooled = summed / jnp.maximum(tallies, 1.0)
    valid_mask = (jnp.arange(slot_length, dtype=jnp.int32)[None, :] < lengths[:, None]).astype(
        jnp.float32
    )
    weight = jnp.minimum(tallies, 1.0) * valid_mask[:, :, None]
    passage_relevance = jnp.sum(weight * pooled, 1) / jnp.maximum(jnp.sum(weight, 1), 1.0)
    unnormalized_similarity = passage_relevance / contrastive_sharpness_factor
    chosen = jnp.sum(
        jnp.where(
            jnp.arange(doc_total, dtype=jnp.int32)[None, :] == positives[:, None],
            unnormalized_similarity,
            0.0,
        ),
        1,
    )
    return jax.nn.logsumexp(unnormalized_similarity, axis=-1) - chosen


def on_device(
    doc_tokens,
    query_tokens,
    query_lengths,
    positive_docs,
    retrieved,
    attend_gain,
    query_weight,
    key_weight,
    value_weight,
    output_weight,
    bias_table,
    feed_gain,
    gate_weight,
    up_weight,
    down_weight,
    final_gain,
    proj_weight,
):
    narrow_size = lax.axis_size("narrow")
    narrow_rank = lax.axis_index("narrow")
    wide_size = lax.axis_size("wide")
    doc_count = doc_tokens.shape[0]
    doc_rows = doc_tokens.shape[1]
    width = doc_tokens.shape[2]
    doc_length = doc_rows * narrow_size
    doc_total = doc_count * wide_size
    own_slots = query_tokens.shape[0] // narrow_size
    slot_length = query_tokens.shape[1]
    head_count = bias_table.shape[1]
    head_size = width // head_count
    doc_flat = doc_count * doc_rows
    query_flat = own_slots * slot_length
    first_slot = narrow_rank * own_slots
    my_queries = lax.dynamic_slice_in_dim(query_tokens, first_slot, own_slots, 0)
    my_lengths = lax.dynamic_slice_in_dim(query_lengths, first_slot, own_slots, 0)
    my_positives = lax.dynamic_slice_in_dim(positive_docs, first_slot, own_slots, 0)
    my_picked = lax.dynamic_slice_in_dim(retrieved, first_slot, own_slots, 0)
    input_rows = jnp.concatenate(
        [doc_tokens.reshape(doc_flat, width), my_queries.reshape(query_flat, width)], 0
    ).astype(jnp.float32)
    attend_normed, attend_back = jax.vjp(rms_norm, input_rows, attend_gain)
    normed = attend_normed.astype(jnp.bfloat16)
    query_heads = product(normed, query_weight).astype(jnp.bfloat16)
    key_heads = product(normed[doc_flat:], key_weight).astype(jnp.bfloat16)
    value_heads = product(normed[doc_flat:], value_weight).astype(jnp.bfloat16)
    whole_doc = lax.all_gather(doc_tokens[0], "narrow", axis=0, tiled=True).astype(jnp.float32)
    whole_normed = rms_norm(whole_doc, attend_gain).astype(jnp.bfloat16)
    key_all = product(whole_normed, key_weight).astype(jnp.bfloat16)
    value_all = product(whole_normed, value_weight).astype(jnp.bfloat16)
    key_all = key_all.reshape(doc_count, doc_length, head_count, head_size)
    value_all = value_all.reshape(doc_count, doc_length, head_count, head_size)
    row_places = narrow_rank * doc_rows + jnp.arange(doc_rows, dtype=jnp.int32)
    doc_onehot = bucket_onehot(row_places, jnp.arange(doc_length, dtype=jnp.int32))
    doc_bias = jnp.einsum("rcu,uh->hrc", doc_onehot, bias_table, precision=highest)
    slot_places = jnp.arange(slot_length, dtype=jnp.int32)
    slot_onehot = bucket_onehot(slot_places, slot_places)
    slot_bias = jnp.einsum("rcu,uh->hrc", slot_onehot, bias_table, precision=highest)
    doc_keep = jnp.ones((doc_count, doc_length), dtype=bool)
    slot_keep = slot_places[None, :] < my_lengths[:, None]
    doc_query = query_heads[:doc_flat].reshape(doc_count, doc_rows, head_count, head_size)
    doc_mixed, doc_logsum = attend_forward(doc_query, key_all, value_all, doc_bias, doc_keep)
    slot_query = query_heads[doc_flat:].reshape(own_slots, slot_length, head_count, head_size)
    slot_key = key_heads.reshape(own_slots, slot_length, head_count, head_size)
    slot_value = value_heads.reshape(own_slots, slot_length, head_count, head_size)
    slot_mixed, slot_logsum = attend_forward(slot_query, slot_key, slot_value, slot_bias, slot_keep)
    mixed = jnp.concatenate(
        [doc_mixed.reshape(doc_flat, width), slot_mixed.reshape(query_flat, width)], 0
    )
    after_attend = input_rows + product(mixed, output_weight)
    feed_normed, feed_back = jax.vjp(rms_norm, after_attend, feed_gain)
    normed_feed = feed_normed.astype(jnp.bfloat16)
    gate_value = product(normed_feed, gate_weight)
    upward = product(normed_feed, up_weight)
    gated_value, gated_back = jax.vjp(gated_unit, gate_value, upward)
    hidden = gated_value.astype(jnp.bfloat16)
    after_feed = after_attend + product(hidden, down_weight)
    final_normed, final_back = jax.vjp(rms_norm, after_feed, final_gain)
    normed_final = final_normed.astype(jnp.bfloat16)
    embedded = product(normed_final, proj_weight)
    unit_value, unit_back = jax.vjp(unit_scale, embedded)
    unit_round = unit_value.astype(jnp.bfloat16)
    passage_normalized_vector = unit_round[:doc_flat]
    slot_unit = unit_round[doc_flat:]
    columns = slot_unit.shape[-1]
    bits = rank_bits()
    every_unit = gather_all(passage_normalized_vector, list(range(bits))[::-1])
    blocks = doc_total * doc_length // 128
    places = my_picked.reshape(query_flat, -1)
    counts = count_places(places, blocks)
    per_doc = doc_length // 128
    block_sum = jnp.einsum(
        "brl,blp->brp",
        counts,
        every_unit.reshape(blocks, 128, columns),
        preferred_element_type=jnp.float32,
    )
    doc_sum = jnp.sum(block_sum.reshape(doc_total, per_doc, query_flat, columns), 1)
    slot_unit_f = slot_unit.astype(jnp.float32)
    summed = jnp.sum(doc_sum * slot_unit_f[None], -1).T.reshape(own_slots, slot_length, doc_total)
    tallies = jnp.sum(
        (places[:, None, :] // doc_length == jnp.arange(doc_total, dtype=jnp.int32)[:, None]).astype(
            jnp.float32
        ),
        -1,
    ).reshape(own_slots, slot_length, doc_total)

    def loss_of(summed_values):
        return pooled_loss(summed_values, tallies, my_lengths, my_positives)

    losses, loss_back = jax.vjp(loss_of, summed)
    grad_summed = loss_back(jnp.ones_like(losses))[0].reshape(query_flat, doc_total)
    grad_slot_unit = jnp.sum(doc_sum * grad_summed.T[:, :, None], 0)
    scaled_unit = (grad_summed.T[:, :, None] * slot_unit_f[None]).astype(jnp.bfloat16)
    scaled_blocks = jnp.broadcast_to(
        scaled_unit[:, None], (doc_total, per_doc, query_flat, columns)
    ).reshape(blocks, query_flat, columns)
    whole_term = jnp.einsum(
        "brl,brp->blp", counts, scaled_blocks, preferred_element_type=jnp.float32
    ).astype(jnp.bfloat16)
    grad_doc_unit = scatter_sum(whole_term.reshape(blocks * 128, columns), range(bits))
    grad_unit = jnp.concatenate([grad_doc_unit, grad_slot_unit.reshape(query_flat, -1)], 0)
    grad_embed = unit_back(grad_unit)[0].astype(jnp.bfloat16)
    proj_grad = left_product(normed_final, grad_embed).astype(jnp.bfloat16)
    grad_after_feed, final_gain_grad = final_back(right_product(grad_embed, proj_weight))
    grad_feed_out = grad_after_feed.astype(jnp.bfloat16)
    down_grad = left_product(hidden, grad_feed_out).astype(jnp.bfloat16)
    grad_gate, grad_upward = gated_back(right_product(grad_feed_out, down_weight))
    grad_gate = grad_gate.astype(jnp.bfloat16)
    grad_upward = grad_upward.astype(jnp.bfloat16)
    gate_grad = left_product(normed_feed, grad_gate).astype(jnp.bfloat16)
    up_grad = left_product(normed_feed, grad_upward).astype(jnp.bfloat16)
    grad_normed_feed = right_product(grad_gate, gate_weight) + right_product(grad_upward, up_weight)
    grad_feed_part, feed_gain_grad = feed_back(grad_normed_feed)
    grad_after_attend = grad_after_feed + grad_feed_part
    grad_attend_out = grad_after_attend.astype(jnp.bfloat16)
    output_grad = left_product(mixed, grad_attend_out).astype(jnp.bfloat16)
    grad_mixed = right_product(grad_attend_out, output_weight).astype(jnp.bfloat16)
    grad_doc_query, grad_key_all, grad_value_all, grad_doc_scores = attention_pullback_pass(
        doc_query,
        key_all,
        value_all,
        doc_bias,
        doc_keep,
        doc_logsum,
        grad_mixed[:doc_flat].reshape(doc_count, doc_rows, head_count, head_size),
    )
    grad_pair = jnp.concatenate(
        [grad_key_all.reshape(doc_length, width), grad_value_all.reshape(doc_length, width)], 1
    ).astype(jnp.bfloat16)
    grad_pair = scatter_sum(grad_pair, range(narrow_size.bit_length() - 1))
    grad_doc_keys = grad_pair[:, :width]
    grad_doc_values = grad_pair[:, width:]
    grad_slot_query, grad_slot_key, grad_slot_value, grad_slot_scores = attention_pullback_pass(
        slot_query,
        slot_key,
        slot_value,
        slot_bias,
        slot_keep,
        slot_logsum,
        grad_mixed[doc_flat:].reshape(own_slots, slot_length, head_count, head_size),
    )
    table_term = jnp.einsum(
        "nhrc,rcu->uh", grad_doc_scores.astype(jnp.float32), doc_onehot, precision=highest
    )
    table_term = table_term + jnp.einsum(
        "nhrc,rcu->uh", grad_slot_scores.astype(jnp.float32), slot_onehot, precision=highest
    )
    query_gradients = jnp.concatenate(
        [grad_doc_query.reshape(doc_flat, width), grad_slot_query.reshape(query_flat, width)], 0
    ).astype(jnp.bfloat16)
    grad_keys = jnp.concatenate(
        [grad_doc_keys.reshape(doc_flat, width), grad_slot_key.reshape(query_flat, width)], 0
    ).astype(jnp.bfloat16)
    grad_values = jnp.concatenate(
        [grad_doc_values.reshape(doc_flat, width), grad_slot_value.reshape(query_flat, width)], 0
    ).astype(jnp.bfloat16)
    both_grads = jnp.concatenate([query_gradients, grad_keys, grad_values], 1)
    attend_grad_w = left_product(normed, both_grads).astype(jnp.bfloat16)
    grad_normed = (
        right_product(query_gradients, query_weight)
        + right_product(grad_keys, key_weight)
        + right_product(grad_values, value_weight)
    )
    grad_input_part, attend_gain_grad = attend_back(grad_normed)
    grad_inputs = grad_after_attend + grad_input_part
    doc_grad = grad_inputs[:doc_flat].reshape(doc_count, doc_rows, width)
    query_grad = grad_inputs[doc_flat:].reshape(own_slots, slot_length, width)
    over_y = [0, 1, 2] + list(range(3, bits))
    over_x = [0, 2, 1] + list(range(3, bits))
    over_z = [0] + list(range(3, bits)) + [1, 2]
    hidden_units = gate_grad.shape[1]
    first_sum = scatter_sum(jnp.concatenate([gate_grad, output_grad], 1), over_y)
    second_sum = scatter_sum(jnp.concatenate([up_grad, proj_grad], 1), over_x)
    third_sum = scatter_sum(down_grad, over_z)
    middle = 3 * width // 2
    attend_sum = jnp.concatenate(
        [scatter_sum(attend_grad_w[:, :middle], over_y), scatter_sum(attend_grad_w[:, middle:], over_x)], 1
    )
    small = jnp.concatenate(
        [attend_gain_grad, feed_gain_grad, final_gain_grad, table_term.reshape(-1)]
    )
    small = sum_all(small.reshape(-1, 128)).reshape(-1)
    rank = lax.axis_index("wide") * narrow_size + narrow_rank
    gain_rows = width >> bits
    gains = [
        lax.dynamic_slice_in_dim(small, place * width + rank * gain_rows, gain_rows, 0)
        for place in range(3)
    ]
    bias_table_grad = small[3 * width :].reshape(table_term.shape)
    return (
        losses,
        doc_grad,
        query_grad,
        gains[0],
        attend_sum[:, :width],
        attend_sum[:, width : 2 * width],
        attend_sum[:, 2 * width :],
        first_sum[:, hidden_units:],
        bias_table_grad,
        gains[1],
        first_sum[:, :hidden_units],
        second_sum[:, :hidden_units],
        third_sum,
        gains[2],
        second_sum[:, hidden_units:],
    )


def solution(mesh):
    return jax.shard_map(
        on_device,
        mesh=mesh,
        in_specs=(
            P("wide", "narrow", None),
            P("wide", None, None),
            P("wide"),
            P("wide"),
            P("wide", None, None),
            P(),
            P(),
            P(),
            P(),
            P(),
            P(),
            P(),
            P(),
            P(),
            P(),
            P(),
            P(),
        ),
        out_specs=(
            P(("wide", "narrow")),
            P("wide", "narrow", None),
            P(("wide", "narrow"), None, None),
            P(("wide", "narrow")),
            P(("wide", "narrow"), None),
            P(("wide", "narrow"), None),
            P(("wide", "narrow"), None),
            P(("wide", "narrow"), None),
            P(),
            P(("wide", "narrow")),
            P(("wide", "narrow"), None),
            P(("wide", "narrow"), None),
            P(("wide", "narrow"), None),
            P(("wide", "narrow")),
            P(("wide", "narrow"), None),
        ),
        check_vma=False,
    )
```

```python
import functools

import jax
import jax.numpy as jnp
from jax import lax
from jax.experimental import pallas as pl
from jax.experimental.pallas import tpu as pltpu
from jax.sharding import PartitionSpec as P

BUCKETS = 32
LANES = 128
CHUNK = 512

epsilon = 1e-06
contrastive_sharpness_factor = 0.01
masked_value = -1000000000.0
bucket_edges = (12, 16, 23, 32, 46, 64, 91)
highest = lax.Precision.HIGHEST
f32 = jnp.float32
bf16 = jnp.bfloat16


def bucket_index(offset):
    distance = jnp.abs(offset)
    beyond = 8 + sum(((distance >= boundary).astype(jnp.int32) for boundary in bucket_edges))
    inside = jnp.where(distance < 8, distance, beyond)
    return inside + BUCKETS // 2 * (offset > 0).astype(jnp.int32)


def product(left, right):
    return jnp.dot(left, right, preferred_element_type=f32)


def left_product(left, right):
    return lax.dot_general(left, right, (((0,), (0,)), ((), ())), preferred_element_type=f32)


def right_product(left, right):
    return lax.dot_general(left, right, (((1,), (1,)), ((), ())), preferred_element_type=f32)


def rank_bits():
    return (lax.axis_size("wide") * lax.axis_size("narrow")).bit_length() - 1


def my_rank():
    return lax.axis_index("wide") * lax.axis_size("narrow") + lax.axis_index("narrow")


def swap(values, bit):
    ranks = 1 << rank_bits()
    pairs = [(rank, rank ^ (1 << bit)) for rank in range(ranks)]
    return lax.ppermute(values, ("wide", "narrow"), pairs)


def scatter_order(position, order):
    count = len(order)
    return sum(((position >> (count - 1 - step)) & 1) << bit for step, bit in enumerate(order))


def gather_order(position, order):
    return sum(((position >> step) & 1) << bit for step, bit in enumerate(order))


def halve(kept, sent, order, last_type=f32):
    for step, bit in enumerate(order):
        came = swap(sent, bit)
        if step == len(order) - 1:
            return kept.astype(f32) + came.astype(f32)
        half = kept.shape[0] // 2
        sent = (kept[half:].astype(f32) + came[half:].astype(f32)).astype(kept.dtype)
        kept = (kept[:half].astype(f32) + came[:half].astype(f32)).astype(kept.dtype)


def sum_all(values):
    for bit in range(rank_bits()):
        values = values + swap(values, bit)
    return values


def call(kernel, outs, args, scratch=(), smem=0, flops=0):
    vmem = pl.BlockSpec(memory_space=pltpu.VMEM)
    specs = [pl.BlockSpec(memory_space=pltpu.SMEM)] * smem + [vmem] * (len(args) - smem)
    moved = sum(a.size * a.dtype.itemsize for a in args)
    moved += sum(o.size * o.dtype.itemsize for o in outs)
    return pl.pallas_call(
        kernel,
        out_shape=tuple(outs),
        in_specs=specs,
        out_specs=tuple([vmem] * len(outs)),
        scratch_shapes=list(scratch),
        compiler_params=pltpu.CompilerParams(vmem_limit_bytes=60 * 1024 * 1024),
        cost_estimate=pl.CostEstimate(flops=flops, bytes_accessed=moved, transcendentals=0),
    )(*args)


def shape(dims, kind=f32):
    return jax.ShapeDtypeStruct(tuple(dims), kind)


def prepare_kernel(
    doc_length, slot_length, doc_total, rank_ref, places_ref, table_ref, counts_ref, tally_ref, doc_bias_ref,
    slot_bias_ref, scratch_ref,
):
    rows, picks = places_ref.shape
    blocks = counts_ref.shape[0]
    heads = doc_bias_ref.shape[0]
    parts = doc_length // LANES

    def one_row(row, carry):
        places = places_ref[pl.ds(row, 1), :]
        high = places >> 7
        low = places & 127
        high_hot = (lax.broadcasted_iota(jnp.int32, (blocks, picks), 0) == high).astype(bf16)
        low_hot = (lax.broadcasted_iota(jnp.int32, (LANES, picks), 0) == low).astype(bf16)
        scratch_ref[pl.ds(row, blocks, stride=rows), :] = right_product(high_hot, low_hot)
        return carry

    lax.fori_loop(0, rows, one_row, 0, unroll=8)

    def one_block(block, carry):
        start = pl.multiple_of(block * rows, rows)
        counts_ref[block] = scratch_ref[pl.ds(start, rows), :].astype(bf16)
        return carry

    lax.fori_loop(0, blocks, one_block, 0, unroll=4)

    owner = places_ref[...] // doc_length
    lane = lax.broadcasted_iota(jnp.int32, (rows, LANES), 1)
    tally = jnp.zeros((rows, LANES), f32)
    for doc in range(doc_total):
        number = jnp.sum((owner == doc).astype(f32), 1, keepdims=True)
        tally = jnp.where(lane == doc, number, tally)
    tally_ref[...] = tally

    narrow = rank_ref[0] & (parts - 1)

    def spread(head, offset):
        line = table_ref[pl.ds(head, 1), pl.ds(pl.multiple_of(offset, LANES), 2 * LANES)]
        rolled = pltpu.roll(jnp.broadcast_to(line, (LANES, 2 * LANES)), 0, 1, stride=1, stride_axis=0)
        return rolled[:, LANES:]

    def one_head(head, carry):
        for part in range(parts):
            distance = (narrow ^ part) - narrow
            doc_bias_ref[head, :, part * LANES : (part + 1) * LANES] = spread(
                head, doc_length - LANES + distance * LANES
            )
        slot_bias_ref[head] = spread(head, doc_length - LANES)
        return carry

    lax.fori_loop(0, heads, one_head, 0)


def rms_scale(values):
    return lax.rsqrt(jnp.mean(values * values, -1, keepdims=True) + epsilon)


def rms_back(values, gain, grad):
    scale = rms_scale(values)
    weighted = grad * gain
    inner = jnp.mean(weighted * values, -1, keepdims=True)
    back = scale * weighted - values * (scale * scale * scale * inner)
    return back, jnp.sum(grad * values * scale, 0, keepdims=True)


def forward_kernel(
    slot_length, slot_ref, own_ref, near_ref, far_ref, last_ref, key_valid_ref, doc_bias_ref, slot_bias_ref,
    attend_gain_ref, feed_gain_ref, final_gain_ref, wq_ref, wk_ref, wv_ref, wo_ref, wg_ref, wu_ref, wd_ref, wp_ref,
    normed_ref, query_ref, key_ref, value_ref, doc_probs_ref, slot_probs_ref, mixed_ref, after_attend_ref,
    normed_feed_ref, hidden_ref, gate_slope_ref, up_slope_ref, after_feed_ref, normed_final_ref, embed_ref,
    slot_unit_ref, doc_unit_ref, all_ref,
):
    rows, width = normed_ref.shape
    head_count = doc_probs_ref.shape[0]
    half = LANES // 2
    slots = slot_ref.shape[0]
    gain = attend_gain_ref[...]
    place = 0
    for ref in (slot_ref, own_ref, near_ref, far_ref, last_ref):
        tokens = ref[...].astype(f32)
        all_ref[place : place + ref.shape[0], :] = (tokens * rms_scale(tokens) * gain).astype(bf16)
        place += ref.shape[0]
    normed = all_ref[:rows, :]
    normed_ref[...] = normed
    query_ref[...] = product(normed, wq_ref[...]).astype(bf16)
    key_ref[...] = product(all_ref[...], wk_ref[...]).astype(bf16)
    value_ref[...] = product(all_ref[...], wv_ref[...]).astype(bf16)

    lane = lax.broadcasted_iota(jnp.int32, (slots, LANES), 1)
    row_slot = lax.broadcasted_iota(jnp.int32, (slots, slots), 0) // slot_length
    col_slot = lax.broadcasted_iota(jnp.int32, (slots, slots), 1) // slot_length
    slot_keep = (row_slot == col_slot) & (key_valid_ref[...] > 0.0)

    def softmax(scores):
        weights = jnp.exp(scores - jnp.max(scores, -1, keepdims=True))
        return (weights * (1.0 / jnp.sum(weights, -1, keepdims=True))).astype(bf16)

    for pair in range(head_count // 2):
        lanes = slice(pair * LANES, (pair + 1) * LANES)
        slot_mixed, doc_mixed = [], []
        for side in range(2):
            head = 2 * pair + side
            mine = (lane < half) if side == 0 else (lane >= half)
            slot_query = jnp.where(mine, query_ref[:slots, lanes], jnp.zeros((), bf16))
            doc_query = jnp.where(mine, query_ref[slots:, lanes], jnp.zeros((), bf16))
            scores = right_product(slot_query, key_ref[:slots, lanes]) + slot_bias_ref[head]
            probs = softmax(jnp.where(slot_keep, scores, masked_value))
            slot_probs_ref[head] = probs
            slot_mixed.append(product(probs, value_ref[:slots, lanes]))
            scores = right_product(doc_query, key_ref[slots:, lanes]) + doc_bias_ref[head]
            probs = softmax(scores)
            doc_probs_ref[head] = probs
            doc_mixed.append(product(probs, value_ref[slots:, lanes]))
        mixed_ref[:slots, lanes] = jnp.where(lane < half, slot_mixed[0], slot_mixed[1]).astype(bf16)
        mixed_ref[slots:, lanes] = jnp.where(lane < half, doc_mixed[0], doc_mixed[1]).astype(bf16)

    attended = product(mixed_ref[...], wo_ref[...])
    after_attend_ref[:slots, :] = slot_ref[...].astype(f32) + attended[:slots]
    after_attend_ref[slots:, :] = own_ref[...].astype(f32) + attended[slots:]
    after_attend = after_attend_ref[...]
    normed_feed = (after_attend * rms_scale(after_attend) * feed_gain_ref[...]).astype(bf16)
    normed_feed_ref[...] = normed_feed
    for start in range(0, hidden_ref.shape[1], CHUNK):
        part = slice(start, start + CHUNK)
        gate = product(normed_feed_ref[...], wg_ref[:, part])
        upward = product(normed_feed_ref[...], wu_ref[:, part])
        factor = 0.7978845608028654
        square = gate * gate
        bent = jnp.tanh(factor * gate * (1.0 + 0.044715 * square))
        curve = 0.5 * gate * (1.0 + bent)
        slope = 0.5 * (1.0 + bent) + 0.5 * factor * gate * (1.0 - bent * bent) * (1.0 + 3 * 0.044715 * square)
        hidden_ref[:, part] = (curve * upward).astype(bf16)
        gate_slope_ref[:, part] = (upward * slope).astype(bf16)
        up_slope_ref[:, part] = curve.astype(bf16)
    after_feed = after_attend_ref[...] + product(hidden_ref[...], wd_ref[...])
    after_feed_ref[...] = after_feed
    normed_final = (after_feed * rms_scale(after_feed) * final_gain_ref[...]).astype(bf16)
    normed_final_ref[...] = normed_final
    embed = product(normed_final, wp_ref[...])
    embed_ref[...] = embed
    unit = (embed * lax.rsqrt(jnp.sum(embed * embed, -1, keepdims=True) + epsilon)).astype(bf16)
    slot_unit_ref[...] = unit[:slots]
    doc_unit_ref[...] = unit[slots:]


def loss_kernel(
    order, gathered, doc_total, slots, rank_ref, counts_ref, near_ref, far_ref, unit_ref, tally_ref, row_valid_ref,
    positive_ref, losses_ref, grad_ref, kept_ref, sent_ref, sum_ref, scaled_ref,
):
    rows = unit_ref.shape[0]
    blocks = counts_ref.shape[0]
    per_doc = blocks // doc_total
    rank = rank_ref[0]
    half = blocks // 2
    sum_ref[...] = jnp.zeros_like(sum_ref)

    def gather_step(place, carry):
        near = rank ^ gather_order(place, gathered)
        far = near ^ (1 << gathered[-1])
        sum_ref[near // per_doc] += product(counts_ref[near], near_ref[place])
        sum_ref[far // per_doc] += product(counts_ref[far], far_ref[place])
        return carry

    lax.fori_loop(0, half, gather_step, 0, unroll=4)

    unit = unit_ref[...].astype(f32)
    lane = lax.broadcasted_iota(jnp.int32, (rows, LANES), 1)
    summed = jnp.zeros((rows, LANES), f32)
    for doc in range(doc_total):
        number = jnp.sum(sum_ref[doc] * unit, 1, keepdims=True)
        summed = jnp.where(lane == doc, number, summed)
    tally = tally_ref[...]
    most = jnp.maximum(tally, 1.0)
    weight = jnp.minimum(tally, 1.0) * row_valid_ref[...]
    slot_length = rows // slots
    pooled = (weight * (summed / most)).reshape(slots, slot_length, LANES)
    weight_sum = jnp.maximum(jnp.sum(weight.reshape(slots, slot_length, LANES), 1), 1.0)
    scores = jnp.sum(pooled, 1) / weight_sum / contrastive_sharpness_factor
    slot_lane = lax.broadcasted_iota(jnp.int32, (slots, LANES), 1)
    inside = slot_lane < doc_total
    scores = jnp.where(inside, scores, -jnp.inf)
    top = jnp.max(scores, -1, keepdims=True)
    powers = jnp.exp(scores - top)
    total = jnp.sum(powers, -1, keepdims=True)
    chosen = (slot_lane == positive_ref[...]).astype(f32)
    picked = jnp.sum(jnp.where(slot_lane == positive_ref[...], scores, 0.0), -1, keepdims=True)
    losses_ref[...] = jnp.broadcast_to(top + jnp.log(total) - picked, (slots, LANES))
    slope = (powers / total - chosen) / contrastive_sharpness_factor / weight_sum
    slope = jnp.where(inside, slope, 0.0)
    slope = jnp.broadcast_to(slope[:, None, :], (slots, slot_length, LANES)).reshape(rows, LANES)
    slope = slope * weight / most

    grad = jnp.zeros((rows, unit.shape[1]), f32)
    for doc in range(doc_total):
        column = jnp.sum(jnp.where(lane == doc, slope, 0.0), 1, keepdims=True)
        grad = grad + column * sum_ref[doc]
        scaled_ref[doc] = (column * unit).T.astype(bf16)
    grad_ref[...] = grad

    def scatter_step(place, carry):
        kept = rank ^ scatter_order(place, order)
        sent = kept ^ (1 << order[0])
        kept_ref[place] = product(scaled_ref[kept // per_doc], counts_ref[kept]).astype(bf16)
        sent_ref[place] = product(scaled_ref[sent // per_doc], counts_ref[sent]).astype(bf16)
        return carry

    lax.fori_loop(0, half, scatter_step, 0, unroll=4)


def feed_back(
    part, grad_unit, embed_ref, after_feed_ref, after_attend_ref, gate_slope_ref, up_slope_ref, feed_gain_ref,
    final_gain_ref, wo_ref, wg_ref, wu_ref, wd_ref, wp_ref, embed_out, feed_out, gate_out, up_out, after_out,
    attend_out, mixed_out, final_gain_out, feed_gain_out,
):
    embed = embed_ref[part, :]
    scale = lax.rsqrt(jnp.sum(embed * embed, -1, keepdims=True) + epsilon)
    inner = jnp.sum(grad_unit * embed, -1, keepdims=True)
    grad_embed = (scale * grad_unit - embed * (scale * scale * scale * inner)).astype(bf16)
    embed_out[...] = grad_embed
    grad_after_feed, final_gain_out[...] = rms_back(
        after_feed_ref[part, :], final_gain_ref[...], right_product(grad_embed, wp_ref[...])
    )
    after_out[...] = grad_after_feed
    feed_out[...] = grad_after_feed.astype(bf16)
    total = jnp.zeros(after_out.shape, f32)
    for start in range(0, gate_out.shape[1], CHUNK):
        cols = slice(start, start + CHUNK)
        grad_hidden = right_product(feed_out[...], wd_ref[cols, :])
        grad_gate = (grad_hidden * gate_slope_ref[part, cols].astype(f32)).astype(bf16)
        grad_up = (grad_hidden * up_slope_ref[part, cols].astype(f32)).astype(bf16)
        gate_out[:, cols] = grad_gate
        up_out[:, cols] = grad_up
        total = total + right_product(grad_gate, wg_ref[:, cols]) + right_product(grad_up, wu_ref[:, cols])
    more, feed_gain_out[...] = rms_back(after_attend_ref[part, :], feed_gain_ref[...], total)
    grad_after_attend = after_out[...] + more
    after_out[...] = grad_after_attend
    attend_out[...] = grad_after_attend.astype(bf16)
    mixed_out[...] = right_product(attend_out[...], wo_ref[...]).astype(bf16)


def diagonal_sums(grads, flip):
    size = grads.shape[0]
    turned = product(flip, grads)
    lines = []
    for start in range(0, grads.shape[1], LANES):
        part = turned[:, start : start + LANES]
        wide = jnp.concatenate([part, jnp.zeros_like(part)], 1)
        rolled = pltpu.roll(wide, 0, 1, stride=1, stride_axis=0)
        lines.append(jnp.sum(rolled.reshape(size // 8, 8, 2 * LANES), 0))
    return jnp.concatenate(lines, 1)


def attend_back(queries, keys, query_ref, key_ref, value_ref, probs_ref, mixed_ref, query_out, key_out, value_out, sums_out):
    size = query_out.shape[0]
    length = probs_ref.shape[2]
    half = LANES // 2
    lane = lax.broadcasted_iota(jnp.int32, (size, LANES), 1)
    key_lane = lax.broadcasted_iota(jnp.int32, (length, LANES), 1)
    row = lax.broadcasted_iota(jnp.int32, (size, size), 0)
    col = lax.broadcasted_iota(jnp.int32, (size, size), 1)
    flip = (row + col == size - 1).astype(bf16)
    for pair in range(probs_ref.shape[0] // 2):
        lanes = slice(pair * LANES, (pair + 1) * LANES)
        sides = []
        for side in range(2):
            head = 2 * pair + side
            mine = (lane < half) if side == 0 else (lane >= half)
            grad_mixed = jnp.where(mine, mixed_ref[:, lanes], jnp.zeros((), bf16))
            probs = probs_ref[head]
            grad_probs = right_product(grad_mixed, value_ref[keys, lanes])
            exact = probs.astype(f32)
            inner = jnp.sum(exact * grad_probs, -1, keepdims=True)
            grad_scores = (exact * (grad_probs - inner)).astype(bf16)
            sums_out[head * 8 : (head + 1) * 8, :] = diagonal_sums(grad_scores, flip)
            sides.append(
                (
                    product(grad_scores, key_ref[keys, lanes]),
                    left_product(grad_scores, query_ref[queries, lanes]),
                    left_product(probs, mixed_ref[:, lanes]),
                )
            )
        query_out[:, lanes] = jnp.where(lane < half, sides[0][0], sides[1][0]).astype(bf16)
        key_out[:, lanes] = jnp.where(key_lane < half, sides[0][1], sides[1][1]).astype(bf16)
        value_out[:, lanes] = jnp.where(key_lane < half, sides[0][2], sides[1][2]).astype(bf16)


def input_back(tokens, gain_ref, after_ref, query, key, value, wq_ref, wk_ref, wv_ref):
    grad_normed = right_product(query, wq_ref[...])
    grad_normed = grad_normed + right_product(key, wk_ref[...])
    grad_normed = grad_normed + right_product(value, wv_ref[...])
    back, gain_grad = rms_back(tokens, gain_ref[...], grad_normed)
    return after_ref[...] + back, gain_grad


def slot_back_kernel(
    grad_unit_ref, embed_ref, after_feed_ref, after_attend_ref, gate_slope_ref, up_slope_ref, tokens_ref, query_ref,
    key_ref, value_ref, probs_ref, attend_gain_ref, feed_gain_ref, final_gain_ref, wq_ref, wk_ref, wv_ref, wo_ref,
    wg_ref, wu_ref, wd_ref, wp_ref,
    embed_out, feed_out, gate_out, up_out, attend_out, query_out, key_out, value_out, tokens_out, gains_out, sums_out,
    after_ref, mixed_ref, final_gain_out, feed_gain_out,
):
    part = slice(0, tokens_ref.shape[0])
    feed_back(
        part, grad_unit_ref[...], embed_ref, after_feed_ref, after_attend_ref, gate_slope_ref, up_slope_ref,
        feed_gain_ref, final_gain_ref, wo_ref, wg_ref, wu_ref, wd_ref, wp_ref, embed_out, feed_out, gate_out, up_out,
        after_ref, attend_out, mixed_ref, final_gain_out, feed_gain_out,
    )
    attend_back(
        part, part, query_ref, key_ref, value_ref, probs_ref, mixed_ref, query_out, key_out, value_out, sums_out
    )
    grads, gain_grad = input_back(
        tokens_ref[...].astype(f32), attend_gain_ref, after_ref, query_out[...], key_out[...], value_out[...], wq_ref,
        wk_ref, wv_ref,
    )
    tokens_out[...] = grads
    gains_out[0:1, :] = gain_grad
    gains_out[1:2, :] = feed_gain_out[...]
    gains_out[2:3, :] = final_gain_out[...]


def doc_feed_kernel(
    kept_ref, came_ref, embed_ref, after_feed_ref, after_attend_ref, gate_slope_ref, up_slope_ref, feed_gain_ref,
    final_gain_ref, wo_ref, wg_ref, wu_ref, wd_ref, wp_ref,
    embed_out, feed_out, gate_out, up_out, after_out, attend_out, mixed_out, gains_out, final_gain_out, feed_gain_out,
):
    rows = kept_ref.shape[1]
    grad_unit = (kept_ref[0].astype(f32) + came_ref[0].astype(f32)).T
    feed_back(
        slice(embed_ref.shape[0] - rows, embed_ref.shape[0]), grad_unit, embed_ref, after_feed_ref, after_attend_ref,
        gate_slope_ref, up_slope_ref, feed_gain_ref, final_gain_ref, wo_ref, wg_ref, wu_ref, wd_ref, wp_ref, embed_out,
        feed_out, gate_out, up_out, after_out, attend_out, mixed_out, final_gain_out, feed_gain_out,
    )
    gains_out[0:1, :] = feed_gain_out[...]
    gains_out[1:2, :] = final_gain_out[...]


def doc_attend_kernel(
    query_ref, key_ref, value_ref, probs_ref, mixed_ref, query_out, key_kept, value_kept, key_sent, value_sent,
    sums_out, key_out, value_out,
):
    rows = query_out.shape[0]
    first = key_ref.shape[0] - probs_ref.shape[2]
    attend_back(
        slice(first, first + rows), slice(first, key_ref.shape[0]), query_ref, key_ref, value_ref, probs_ref, mixed_ref,
        query_out, key_out, value_out, sums_out,
    )
    for place in range(2):
        here = slice(place * rows, (place + 1) * rows)
        key_kept[here, :] = key_out[2 * place * rows : (2 * place + 1) * rows, :]
        value_kept[here, :] = value_out[2 * place * rows : (2 * place + 1) * rows, :]
        key_sent[here, :] = key_out[(2 * place + 1) * rows : (2 * place + 2) * rows, :]
        value_sent[here, :] = value_out[(2 * place + 1) * rows : (2 * place + 2) * rows, :]


def turn(values, scratch, target, order, rank):
    scratch[...] = values.astype(f32).T
    count = 1 << len(order)
    size = scratch.shape[0] // count
    if size % 8:
        row = lax.broadcasted_iota(jnp.int32, (scratch.shape[0], scratch.shape[0]), 0)
        col = lax.broadcasted_iota(jnp.int32, (scratch.shape[0], scratch.shape[0]), 1)
        source = (scatter_order(row // size, order) ^ rank) * size + row % size
        target[...] = product((col == source).astype(bf16), scratch[...].astype(bf16))
        return
    for place in range(count):
        source = (rank ^ scatter_order(place, order)) * size
        target[place * size : (place + 1) * size, :] = scratch[pl.ds(pl.multiple_of(source, 8), size), :]


def store_product(turned, right, kept_ref, sent_ref, start):
    half = kept_ref.shape[0]
    for first in range(0, right.shape[1], CHUNK):
        last = min(first + CHUNK, right.shape[1])
        result = product(turned, right[:, first:last]).astype(bf16)
        kept_ref[:, start + first : start + last] = result[:half]
        sent_ref[:, start + first : start + last] = result[half:]


def both(slot_ref, doc_ref):
    return jnp.concatenate([slot_ref[...], doc_ref[...]], 0)


def feed_weight_kernel(
    first_order, second_order, rank_ref, normed_feed_ref, mixed_ref, normed_final_ref, hidden_ref, slot_gate, doc_gate,
    slot_up, doc_up, slot_attend, doc_attend, slot_embed, doc_embed, slot_feed, doc_feed,
    first_kept, first_sent, second_kept, second_sent, third_kept, third_sent, narrow_ref, narrow_target, wide_ref,
    wide_target,
):
    rank = rank_ref[0]
    units = slot_gate.shape[1]
    turn(hidden_ref[...], wide_ref, wide_target, second_order, rank)
    store_product(wide_target[...].astype(bf16), both(slot_feed, doc_feed), third_kept, third_sent, 0)
    turn(normed_feed_ref[...], narrow_ref, narrow_target, first_order, rank)
    store_product(narrow_target[...].astype(bf16), both(slot_gate, doc_gate), first_kept, first_sent, 0)
    turn(normed_feed_ref[...], narrow_ref, narrow_target, second_order, rank)
    store_product(narrow_target[...].astype(bf16), both(slot_up, doc_up), second_kept, second_sent, 0)
    turn(mixed_ref[...], narrow_ref, narrow_target, first_order, rank)
    store_product(narrow_target[...].astype(bf16), both(slot_attend, doc_attend), first_kept, first_sent, units)
    turn(normed_final_ref[...], narrow_ref, narrow_target, second_order, rank)
    store_product(narrow_target[...].astype(bf16), both(slot_embed, doc_embed), second_kept, second_sent, units)


def attend_weight_kernel(
    first_order, second_order, rank_ref, normed_ref, tokens_ref, gain_ref, after_ref, slot_query, slot_key, slot_value,
    doc_query, key_kept, key_came, value_kept, value_came, wq_ref, wk_ref, wv_ref,
    first_kept, first_sent, second_kept, second_sent, tokens_out, gain_out, grads_ref, narrow_ref, narrow_target,
):
    rank = rank_ref[0]
    slots, width = slot_query.shape
    middle = first_kept.shape[1]
    key = (key_kept[...].astype(f32) + key_came[...].astype(f32)).astype(bf16)
    value = (value_kept[...].astype(f32) + value_came[...].astype(f32)).astype(bf16)
    grads_ref[:slots, :width] = slot_query[...]
    grads_ref[:slots, width : 2 * width] = slot_key[...]
    grads_ref[:slots, 2 * width :] = slot_value[...]
    grads_ref[slots:, :width] = doc_query[...]
    grads_ref[slots:, width : 2 * width] = key
    grads_ref[slots:, 2 * width :] = value
    turn(normed_ref[...], narrow_ref, narrow_target, first_order, rank)
    store_product(narrow_target[...].astype(bf16), grads_ref[:, :middle], first_kept, first_sent, 0)
    turn(normed_ref[...], narrow_ref, narrow_target, second_order, rank)
    store_product(narrow_target[...].astype(bf16), grads_ref[:, middle:], second_kept, second_sent, 0)
    tokens_out[...], gain_out[...] = input_back(
        tokens_ref[...].astype(f32), gain_ref, after_ref, doc_query[...], key, value, wq_ref, wk_ref, wv_ref
    )


def on_device(
    doc_tokens, query_tokens, query_lengths, positive_docs, retrieved, attend_gain, query_weight, key_weight,
    value_weight, output_weight, bias_table, feed_gain, gate_weight, up_weight, down_weight, final_gain, proj_weight,
):
    narrow_size = lax.axis_size("narrow")
    narrow_rank = lax.axis_index("narrow")
    bits = rank_bits()
    rank = my_rank()
    rank_word = rank.astype(jnp.int32).reshape(1)
    doc_rows, width = doc_tokens.shape[1:]
    doc_length = doc_rows * narrow_size
    doc_total = doc_tokens.shape[0] * lax.axis_size("wide")
    slots = query_tokens.shape[0] // narrow_size
    slot_length = query_tokens.shape[1]
    heads = bias_table.shape[1]
    units = gate_weight.shape[1]
    columns = proj_weight.shape[1]
    slot_rows = slots * slot_length
    rows = slot_rows + doc_rows
    blocks = doc_total * doc_length // LANES
    assert doc_tokens.shape[0] == 1 and doc_rows == LANES and slot_rows == LANES and narrow_size == 4
    assert columns == LANES and doc_total <= LANES and blocks == 1 << bits

    def own(values):
        return lax.dynamic_slice_in_dim(values, narrow_rank * slots, slots, 0)

    own_tokens = doc_tokens[0]
    y_tokens = swap(own_tokens, 1)
    slot_tokens = own(query_tokens).reshape(slot_rows, width)
    places = own(retrieved).reshape(slot_rows, -1)
    lengths = own(query_lengths)
    positives = own(positive_docs).reshape(slots, 1)
    valid = (jnp.arange(slot_length, dtype=jnp.int32)[None, :] < lengths[:, None]).astype(f32)
    key_valid = valid.reshape(1, slot_rows)
    row_valid = valid.reshape(slot_rows, 1)
    reach = doc_length + LANES
    offsets = jnp.arange(-doc_length, reach, dtype=jnp.int32)
    offset_hot = (bucket_index(offsets)[:, None] == jnp.arange(BUCKETS, dtype=jnp.int32)).astype(f32)
    offset_bias = jnp.einsum("mu,uh->hm", offset_hot, bias_table, precision=highest)

    counts, tally, doc_bias, slot_bias = call(
        functools.partial(prepare_kernel, doc_length, slot_length, doc_total),
        [
            shape((blocks, slot_rows, LANES), bf16),
            shape((slot_rows, LANES)),
            shape((heads, doc_rows, doc_length)),
            shape((heads, slot_rows, slot_rows)),
        ],
        [rank_word, places, offset_bias],
        scratch=[pltpu.VMEM((blocks * slot_rows, LANES), f32)],
        smem=1,
    )
    core_tokens = swap(own_tokens, 0)
    both_tokens = swap(y_tokens, 0)

    gains = (attend_gain.reshape(1, width), feed_gain.reshape(1, width), final_gain.reshape(1, width))
    all_rows = slot_rows + doc_length
    (
        normed, query, key, value, doc_probs, slot_probs, mixed, after_attend, normed_feed, hidden, gate_slope, up_slope,
        after_feed, normed_final, embed, slot_unit, doc_unit,
    ) = call(
        functools.partial(forward_kernel, slot_length),
        [
            shape((rows, width), bf16),
            shape((rows, width), bf16),
            shape((all_rows, width), bf16),
            shape((all_rows, width), bf16),
            shape((heads, doc_rows, doc_length), bf16),
            shape((heads, slot_rows, slot_rows), bf16),
            shape((rows, width), bf16),
            shape((rows, width)),
            shape((rows, width), bf16),
            shape((rows, units), bf16),
            shape((rows, units), bf16),
            shape((rows, units), bf16),
            shape((rows, width)),
            shape((rows, width), bf16),
            shape((rows, columns)),
            shape((slot_rows, columns), bf16),
            shape((doc_rows, columns), bf16),
        ],
        [
            slot_tokens, own_tokens, core_tokens, y_tokens, both_tokens, key_valid, doc_bias, slot_bias, *gains,
            query_weight, key_weight, value_weight, output_weight, gate_weight, up_weight, down_weight, proj_weight,
        ],
        scratch=[pltpu.VMEM((all_rows, width), bf16)],
    )

    gathered = list(range(bits))[::-1]
    gathered_units = doc_unit[None]
    for bit in gathered[:-1]:
        gathered_units = jnp.concatenate([gathered_units, swap(gathered_units, bit)], 0)
    far_units = swap(gathered_units, gathered[-1])

    order = list(range(bits))
    half = blocks // 2
    losses, grad_slot_unit, kept, sent = call(
        functools.partial(loss_kernel, order, gathered, doc_total, slots),
        [
            shape((slots, LANES)),
            shape((slot_rows, columns)),
            shape((half, columns, LANES), bf16),
            shape((half, columns, LANES), bf16),
        ],
        [rank_word, counts, gathered_units, far_units, slot_unit, tally, row_valid, positives],
        scratch=[
            pltpu.VMEM((doc_total, slot_rows, columns), f32),
            pltpu.VMEM((doc_total, columns, slot_rows), bf16),
        ],
        smem=1,
    )
    for step, bit in enumerate(order):
        came = swap(sent, bit)
        if step < bits - 1:
            cut = kept.shape[0] // 2
            sent = (kept[cut:].astype(f32) + came[cut:].astype(f32)).astype(bf16)
            kept = (kept[:cut].astype(f32) + came[:cut].astype(f32)).astype(bf16)

    feed_shapes = [
        shape((LANES, columns), bf16),
        shape((LANES, width), bf16),
        shape((LANES, units), bf16),
        shape((LANES, units), bf16),
    ]
    row_shape = shape((LANES, width), bf16)
    gain_scratch = [pltpu.VMEM((1, width), f32), pltpu.VMEM((1, width), f32)]
    (
        slot_embed, slot_feed, slot_gate, slot_up, slot_attend, slot_grad_query, slot_grad_key, slot_grad_value,
        query_grad, slot_gains, slot_sums,
    ) = call(
        slot_back_kernel,
        feed_shapes
        + [row_shape] * 4
        + [shape((slot_rows, width)), shape((3, width)), shape((heads * 8, 2 * LANES))],
        [
            grad_slot_unit, embed, after_feed, after_attend, gate_slope, up_slope, slot_tokens, query, key, value,
            slot_probs, *gains, query_weight, key_weight, value_weight, output_weight, gate_weight, up_weight,
            down_weight, proj_weight,
        ],
        scratch=[pltpu.VMEM((slot_rows, width), f32), pltpu.VMEM((slot_rows, width), bf16)] + gain_scratch,
    )
    doc_embed, doc_feed, doc_gate, doc_up, doc_after, doc_attend, doc_mixed, doc_gains = call(
        doc_feed_kernel,
        feed_shapes + [shape((doc_rows, width)), row_shape, row_shape, shape((2, width))],
        [
            kept, came, embed, after_feed, after_attend, gate_slope, up_slope, gains[1], gains[2], output_weight,
            gate_weight, up_weight, down_weight, proj_weight,
        ],
        scratch=gain_scratch,
    )

    over_y = [0, 1, 2] + list(range(3, bits))
    over_x = [0, 2, 1] + list(range(3, bits))
    first_cols, second_cols = units + width, units + columns
    first_kept, first_sent, second_kept, second_sent, third_kept, third_sent = call(
        functools.partial(feed_weight_kernel, over_y, over_x),
        [shape((width // 2, first_cols), bf16)] * 2
        + [shape((width // 2, second_cols), bf16)] * 2
        + [shape((units // 2, width), bf16)] * 2,
        [
            rank_word, normed_feed, mixed, normed_final, hidden, slot_gate, doc_gate, slot_up, doc_up, slot_attend,
            doc_attend, slot_embed, doc_embed, slot_feed, doc_feed,
        ],
        scratch=[
            pltpu.VMEM((width, rows), f32),
            pltpu.VMEM((width, rows), f32),
            pltpu.VMEM((units, rows), f32),
            pltpu.VMEM((units, rows), f32),
        ],
        smem=1,
    )

    doc_grad_query, key_kept, value_kept, key_sent, value_sent, doc_sums = call(
        doc_attend_kernel,
        [row_shape] + [shape((doc_length // 2, width), bf16)] * 4 + [shape((heads * 8, 2 * doc_length))],
        [query, key, value, doc_probs, doc_mixed],
        scratch=[pltpu.VMEM((doc_length, width), bf16), pltpu.VMEM((doc_length, width), bf16)],
    )
    key_came, value_came = swap(key_sent, 0), swap(value_sent, 0)
    pair_sum = []
    for one_kept, one_came in ((key_kept, key_came), (value_kept, value_came)):
        total = one_kept.astype(f32) + one_came.astype(f32)
        pair_sum.append((total[:doc_rows].astype(bf16), total[doc_rows:].astype(bf16)))
    came_pair = swap(jnp.concatenate([pair_sum[0][1], pair_sum[1][1]], 0), 1)

    middle = 3 * width // 2
    fourth_kept, fourth_sent, fifth_kept, fifth_sent, doc_grad, doc_attend_gain = call(
        functools.partial(attend_weight_kernel, over_y, over_x),
        [shape((width // 2, middle), bf16)] * 4 + [shape((doc_rows, width)), shape((1, width))],
        [
            rank_word, normed, own_tokens, gains[0], doc_after, slot_grad_query, slot_grad_key, slot_grad_value,
            doc_grad_query, pair_sum[0][0], came_pair[:doc_rows], pair_sum[1][0], came_pair[doc_rows:], query_weight,
            key_weight, value_weight,
        ],
        scratch=[
            pltpu.VMEM((rows, 3 * width), bf16),
            pltpu.VMEM((width, rows), f32),
            pltpu.VMEM((width, rows), f32),
        ],
        smem=1,
    )

    lines = doc_sums.reshape(heads, 8, narrow_size, 2 * LANES).sum(1)
    span = jnp.arange(2 * LANES, dtype=jnp.int32) - (LANES - 1)
    parts = jnp.arange(narrow_size, dtype=jnp.int32)
    doc_offsets = ((narrow_rank ^ parts) - narrow_rank)[:, None] * LANES + span[None, :]
    places_hot = jnp.arange(BUCKETS, dtype=jnp.int32)
    doc_hot = (bucket_index(doc_offsets)[..., None] == places_hot).astype(f32)
    slot_hot = (bucket_index(span)[:, None] == places_hot).astype(f32)
    table_term = jnp.einsum("hpm,pmu->uh", lines, doc_hot, precision=highest)
    table_term = table_term + jnp.einsum(
        "hm,mu->uh", slot_sums.reshape(heads, 8, 2 * LANES).sum(1), slot_hot, precision=highest
    )

    first_sum = halve(first_kept, first_sent, over_y)
    second_sum = halve(second_kept, second_sent, over_x)
    third_sum = halve(third_kept, third_sent, over_x)
    fourth_sum = halve(fourth_kept, fourth_sent, over_y)
    fifth_sum = halve(fifth_kept, fifth_sent, over_x)
    gain_grads = slot_gains + jnp.concatenate([doc_attend_gain, doc_gains], 0)
    small = jnp.concatenate([gain_grads.reshape(-1), table_term.reshape(-1)])
    small = sum_all(small.reshape(-1, LANES)).reshape(-1)
    gain_rows = width >> bits
    gain_out = [
        lax.dynamic_slice_in_dim(small, place * width + rank * gain_rows, gain_rows, 0) for place in range(3)
    ]
    bias_table_grad = small[3 * width :].reshape(BUCKETS, heads)
    return (
        losses[:, 0],
        doc_grad[None],
        query_grad.reshape(slots, slot_length, width),
        gain_out[0],
        fourth_sum[:, :width],
        jnp.concatenate([fourth_sum[:, width:], fifth_sum[:, : 2 * width - middle]], 1),
        fifth_sum[:, 2 * width - middle :],
        first_sum[:, units:],
        bias_table_grad,
        gain_out[1],
        first_sum[:, :units],
        second_sum[:, :units],
        third_sum,
        gain_out[2],
        second_sum[:, units:],
    )


def solution(mesh):
    return jax.shard_map(
        on_device,
        mesh=mesh,
        in_specs=(
            P("wide", "narrow", None),
            P("wide", None, None),
            P("wide"),
            P("wide"),
            P("wide", None, None),
            P(),
            P(),
            P(),
            P(),
            P(),
            P(),
            P(),
            P(),
            P(),
            P(),
            P(),
            P(),
        ),
        out_specs=(
            P(("wide", "narrow")),
            P("wide", "narrow", None),
            P(("wide", "narrow"), None, None),
            P(("wide", "narrow")),
            P(("wide", "narrow"), None),
            P(("wide", "narrow"), None),
            P(("wide", "narrow"), None),
            P(("wide", "narrow"), None),
            P(),
            P(("wide", "narrow")),
            P(("wide", "narrow"), None),
            P(("wide", "narrow"), None),
            P(("wide", "narrow"), None),
            P(("wide", "narrow")),
            P(("wide", "narrow"), None),
        ),
        check_vma=False,
    )
```

```python
import functools

import jax
import jax.numpy as jnp
from jax import lax
from jax.experimental import pallas as pl
from jax.experimental.pallas import tpu as pltpu
from jax.sharding import PartitionSpec as P

BUCKETS = 32
LANES = 128
CHUNK = 512

epsilon = 1e-06
contrastive_sharpness_factor = 0.01
masked_value = -1000000000.0
bucket_edges = (12, 16, 23, 32, 46, 64, 91)
highest = lax.Precision.HIGHEST
f32 = jnp.float32
bf16 = jnp.bfloat16


def bucket_index(offset):
    distance = jnp.abs(offset)
    beyond = 8 + sum(((distance >= boundary).astype(jnp.int32) for boundary in bucket_edges))
    inside = jnp.where(distance < 8, distance, beyond)
    return inside + BUCKETS // 2 * (offset > 0).astype(jnp.int32)


def product(left, right):
    return jnp.dot(left, right, preferred_element_type=f32)


def left_product(left, right):
    return lax.dot_general(left, right, (((0,), (0,)), ((), ())), preferred_element_type=f32)


def right_product(left, right):
    return lax.dot_general(left, right, (((1,), (1,)), ((), ())), preferred_element_type=f32)


def rank_bits():
    return (lax.axis_size("wide") * lax.axis_size("narrow")).bit_length() - 1


def my_rank():
    return lax.axis_index("wide") * lax.axis_size("narrow") + lax.axis_index("narrow")


def swap(values, mask):
    ranks = 1 << rank_bits()
    pairs = [(rank, rank ^ mask) for rank in range(ranks)]
    return lax.ppermute(values, ("wide", "narrow"), pairs)


def scatter_order(position, order):
    count = len(order)
    return sum(((position >> (count - 1 - step)) & 1) << bit for step, bit in enumerate(order))


def gather_order(position, order):
    return sum(((position >> step) & 1) << bit for step, bit in enumerate(order))


def after(values, *others):
    flat, tree = jax.tree.flatten(values)
    done = lax.optimization_barrier(tuple(flat) + tuple(others))
    return jax.tree.unflatten(tree, done[: len(flat)])


def add(*values):
    total = values[0].astype(f32)
    for value in values[1:]:
        total = total + value.astype(f32)
    return total


def cut_kernel(kept_ref, came_ref, kept_out, sent_out):
    half = kept_out.shape[0]
    kept_out[...] = add(kept_ref[:half, :], came_ref[:half, :]).astype(bf16)
    sent_out[...] = add(kept_ref[half:, :], came_ref[half:, :]).astype(bf16)


def cut(kept, came):
    half = kept.shape[0] // 2
    if half % 16 == 0:
        return call(cut_kernel, [shape((half, kept.shape[1]), bf16)] * 2, [kept, came])
    return add(kept[:half], came[:half]).astype(bf16), add(kept[half:], came[half:]).astype(bf16)


def call(kernel, outs, args, spaces="", scratch=(), flops=0):
    kinds = {"s": pltpu.SMEM, "v": pltpu.VMEM, "a": pl.ANY}
    spaces = spaces.ljust(len(args) + len(outs), "v")
    specs = [pl.BlockSpec(memory_space=kinds[kind]) for kind in spaces]
    return pl.pallas_call(
        kernel,
        out_shape=tuple(outs),
        in_specs=specs[: len(args)],
        out_specs=tuple(specs[len(args) :]),
        scratch_shapes=list(scratch),
        compiler_params=pltpu.CompilerParams(vmem_limit_bytes=60 * 1024 * 1024),
        cost_estimate=pl.CostEstimate(flops=flops, bytes_accessed=0, transcendentals=0),
    )(*args)


def shape(dims, kind=f32):
    return jax.ShapeDtypeStruct(tuple(dims), kind)


def room(values):
    return pltpu.VMEM(values.shape, values.dtype)


def loads(refs, rooms, sems):
    return [pltpu.make_async_copy(ref, place, sems.at[i]) for i, (ref, place) in enumerate(zip(refs, rooms))]


def bias_kernel(doc_length, rank_ref, table_ref, doc_bias_ref, slot_bias_ref, line_ref):
    pairs = doc_bias_ref.shape[0]
    parts = doc_length // LANES
    length = line_ref.shape[1]
    offset = lax.broadcasted_iota(jnp.int32, (BUCKETS, length), 1) - doc_length
    hot = (bucket_index(offset) == lax.broadcasted_iota(jnp.int32, (BUCKETS, length), 0)).astype(f32)
    line_ref[...] = lax.dot_general(
        table_ref[...], hot, (((0,), (0,)), ((), ())), precision=highest, preferred_element_type=f32
    )
    narrow = rank_ref[0] & (parts - 1)

    def spread(head, start):
        line = line_ref[pl.ds(head, 1), pl.ds(pl.multiple_of(start, LANES), 2 * LANES)]
        rolled = pltpu.roll(jnp.broadcast_to(line, (LANES, 2 * LANES)), 0, 1, stride=1, stride_axis=0)
        return rolled[:, LANES:]

    def one_pair(pair, carry):
        for side in range(2):
            rows = slice(side * LANES, (side + 1) * LANES)
            head = 2 * pair + side
            for part in range(parts):
                distance = (narrow ^ part) - narrow
                doc_bias_ref[pair, rows, part * LANES : (part + 1) * LANES] = spread(
                    head, doc_length - LANES + distance * LANES
                )
            slot_bias_ref[pair, rows, :] = spread(head, doc_length - LANES)
        return carry

    lax.fori_loop(0, pairs, one_pair, 0)


def count_kernel(doc_length, doc_total, rank_ref, picked_ref, counts_ref, tally_ref, load_ref, places_ref, scratch_ref, sem):
    slots, slot_length, picks = load_ref.shape
    rows = slots * slot_length
    blocks = counts_ref.shape[0]
    narrow_size = picked_ref.shape[0] // slots
    first = (rank_ref[0] & (narrow_size - 1)) * slots
    load = pltpu.make_async_copy(picked_ref.at[pl.ds(first, slots)], load_ref, sem)
    load.start()
    load.wait()

    places_ref[...] = load_ref[...].reshape(rows, picks)

    def one_row(row, carry):
        places = places_ref[pl.ds(row, 1), :]
        high = places >> 7
        low = places & 127
        high_hot = (lax.broadcasted_iota(jnp.int32, (blocks, picks), 0) == high).astype(bf16)
        low_hot = (lax.broadcasted_iota(jnp.int32, (LANES, picks), 0) == low).astype(bf16)
        scratch_ref[pl.ds(row, blocks, stride=rows), :] = right_product(high_hot, low_hot)
        return carry

    lax.fori_loop(0, rows, one_row, 0, unroll=8)

    def one_block(block, carry):
        start = pl.multiple_of(block * rows, rows)
        counts_ref[block] = scratch_ref[pl.ds(start, rows), :].astype(bf16)
        return carry

    lax.fori_loop(0, blocks, one_block, 0, unroll=4)

    owner = places_ref[...] // doc_length
    lane = lax.broadcasted_iota(jnp.int32, (rows, LANES), 1)
    tally = jnp.zeros((rows, LANES), f32)
    for doc in range(doc_total):
        number = jnp.sum((owner == doc).astype(f32), 1, keepdims=True)
        tally = jnp.where(lane == doc, number, tally)
    tally_ref[...] = tally


def rms_scale(values):
    return lax.rsqrt(jnp.mean(values * values, -1, keepdims=True) + epsilon)


def rms_back(values, gain, grad):
    scale = rms_scale(values)
    weighted = grad * gain
    inner = jnp.mean(weighted * values, -1, keepdims=True)
    return scale * weighted - values * (scale * scale * scale * inner)


def tile(index, size=LANES):
    return pl.ds(pl.multiple_of(index * size, size), size)


def halves(values, zero_row):
    return jnp.concatenate([jnp.where(zero_row, values, jnp.zeros((), values.dtype)),
                            jnp.where(zero_row, jnp.zeros((), values.dtype), values)], 0)


def joined(values, first_lanes):
    rows = values.shape[0] // 2
    return jnp.where(first_lanes, values[:rows], values[rows:])


def forward_kernel(
    slots, slot_length, rank_ref, lengths_ref, queries_ref, own_ref, near_ref, far_ref, last_ref, doc_bias_ref,
    slot_bias_ref, attend_gain_ref, feed_gain_ref, final_gain_ref,
    wq_any, wk_any, wv_any, wo_any, wg_any, wu_any, wd_any, wp_any,
    all_any, query_any, key_any, value_any, doc_probs_any, slot_probs_any, mixed_any, after_attend_any,
    normed_feed_any, hidden_any, gate_slope_any, up_slope_any, after_feed_any, normed_final_any, embed_any,
    slot_unit_any, doc_unit_any,
    all_ref, query_ref, key_ref, value_ref, doc_probs_ref, slot_probs_ref, mixed_ref, after_attend_ref,
    normed_feed_ref, hidden_ref, gate_slope_ref, up_slope_ref, after_feed_ref, normed_final_ref, embed_ref,
    slot_unit_ref, doc_unit_ref,
    wq_ref, wk_ref, wv_ref, wo_ref, wg_ref, wu_ref, wd_ref, wp_ref, slot_ref, load_sems, store_sems, slot_sem,
):
    slot_rows = slots * slot_length
    rows, width = query_ref.shape
    pairs = doc_probs_ref.shape[0]
    half = LANES // 2
    narrow_size = queries_ref.shape[0] // slots
    first = (rank_ref[0] & (narrow_size - 1)) * slots
    load_slots = pltpu.make_async_copy(queries_ref.at[pl.ds(first, slots)], slot_ref, slot_sem)
    load_slots.start()
    weights = loads(
        (wq_any, wk_any, wv_any, wo_any, wg_any, wu_any, wd_any, wp_any),
        (wq_ref, wk_ref, wv_ref, wo_ref, wg_ref, wu_ref, wd_ref, wp_ref),
        load_sems,
    )
    stores = loads(
        (all_ref, query_ref, key_ref, value_ref, doc_probs_ref, slot_probs_ref, mixed_ref, after_attend_ref,
         normed_feed_ref, hidden_ref, gate_slope_ref, up_slope_ref, after_feed_ref, normed_final_ref, embed_ref,
         slot_unit_ref, doc_unit_ref),
        (all_any, query_any, key_any, value_any, doc_probs_any, slot_probs_any, mixed_any, after_attend_any,
         normed_feed_any, hidden_any, gate_slope_any, up_slope_any, after_feed_any, normed_final_any, embed_any,
         slot_unit_any, doc_unit_any),
        store_sems,
    )
    for weight in weights[:3]:
        weight.start()
    gain = attend_gain_ref[...].reshape(1, width)
    place = slot_rows
    for ref in (own_ref, near_ref, far_ref, last_ref):
        tokens = ref[...].astype(f32)
        all_ref[place : place + ref.shape[0], :] = (tokens * rms_scale(tokens) * gain).astype(bf16)
        place += ref.shape[0]
    load_slots.wait()
    slot_tokens = slot_ref[...].reshape(slot_rows, width).astype(f32)
    all_ref[:slot_rows, :] = (slot_tokens * rms_scale(slot_tokens) * gain).astype(bf16)
    normed = all_ref[:rows, :]
    stores[0].start()
    weights[0].wait()
    for weight in weights[3:]:
        weight.start()
    query_ref[...] = product(normed, wq_ref[...]).astype(bf16)
    stores[1].start()
    weights[1].wait()
    key_ref[...] = product(all_ref[...], wk_ref[...]).astype(bf16)
    stores[2].start()
    weights[2].wait()
    value_ref[...] = product(all_ref[...], wv_ref[...]).astype(bf16)
    stores[3].start()

    lane = lax.broadcasted_iota(jnp.int32, (slot_rows, LANES), 1)
    row = lax.broadcasted_iota(jnp.int32, (slot_rows, slot_rows), 0)
    col = lax.broadcasted_iota(jnp.int32, (slot_rows, slot_rows), 1)
    slot_keep = row < 0
    for slot in range(slots):
        start = slot * slot_length
        inside = (row >= start) & (row < start + slot_length) & (col >= start)
        slot_keep = slot_keep | (inside & (col < start + lengths_ref[first + slot]))

    def softmax(scores):
        weights = jnp.exp(scores - jnp.max(scores, -1, keepdims=True))
        return (weights * (1.0 / jnp.sum(weights, -1, keepdims=True))).astype(bf16)

    first_lanes = lane < half
    pair_keep = jnp.concatenate([slot_keep, slot_keep], 0)

    def one_pair(pair, carry):
        lanes = tile(pair)
        slot_query = halves(query_ref[:slot_rows, lanes], first_lanes)
        scores = right_product(slot_query, key_ref[:slot_rows, lanes]) + slot_bias_ref[pair]
        probs = softmax(jnp.where(pair_keep, scores, masked_value))
        slot_probs_ref[pair] = probs
        slot_mixed = product(probs, value_ref[:slot_rows, lanes])
        mixed_ref[:slot_rows, lanes] = joined(slot_mixed, first_lanes).astype(bf16)
        doc_query = halves(query_ref[slot_rows:, lanes], first_lanes)
        scores = right_product(doc_query, key_ref[slot_rows:, lanes]) + doc_bias_ref[pair]
        probs = softmax(scores)
        doc_probs_ref[pair] = probs
        doc_mixed = product(probs, value_ref[slot_rows:, lanes])
        mixed_ref[slot_rows:, lanes] = joined(doc_mixed, first_lanes).astype(bf16)
        return carry

    lax.fori_loop(0, pairs, one_pair, 0)
    for store in stores[4:7]:
        store.start()

    weights[3].wait()
    attended = product(mixed_ref[...], wo_ref[...])
    after_attend_ref[:slot_rows, :] = slot_ref[...].reshape(slot_rows, width).astype(f32) + attended[:slot_rows]
    after_attend_ref[slot_rows:, :] = own_ref[...].astype(f32) + attended[slot_rows:]
    stores[7].start()
    after_attend = after_attend_ref[...]
    feed_gain = feed_gain_ref[...].reshape(1, width)
    normed_feed_ref[...] = (after_attend * rms_scale(after_attend) * feed_gain).astype(bf16)
    stores[8].start()
    weights[4].wait()
    weights[5].wait()

    def one_part(step, carry):
        part = tile(step, CHUNK)
        gate = product(normed_feed_ref[...], wg_ref[:, part])
        upward = product(normed_feed_ref[...], wu_ref[:, part])
        factor = 0.7978845608028654
        square = gate * gate
        bent = jnp.tanh(factor * gate * (1.0 + 0.044715 * square))
        curve = 0.5 * gate * (1.0 + bent)
        slope = 0.5 * (1.0 + bent) + 0.5 * factor * gate * (1.0 - bent * bent) * (1.0 + 3 * 0.044715 * square)
        hidden_ref[:, part] = (curve * upward).astype(bf16)
        gate_slope_ref[:, part] = (upward * slope).astype(bf16)
        up_slope_ref[:, part] = curve.astype(bf16)
        return carry

    lax.fori_loop(0, hidden_ref.shape[1] // CHUNK, one_part, 0)
    for store in stores[9:12]:
        store.start()
    weights[6].wait()
    after_feed = after_attend_ref[...] + product(hidden_ref[...], wd_ref[...])
    after_feed_ref[...] = after_feed
    stores[12].start()
    final_gain = final_gain_ref[...].reshape(1, width)
    normed_final = (after_feed * rms_scale(after_feed) * final_gain).astype(bf16)
    normed_final_ref[...] = normed_final
    stores[13].start()
    weights[7].wait()
    embed = product(normed_final, wp_ref[...])
    embed_ref[...] = embed
    unit = (embed * lax.rsqrt(jnp.sum(embed * embed, -1, keepdims=True) + epsilon)).astype(bf16)
    slot_unit_ref[...] = unit[:slot_rows]
    doc_unit_ref[...] = unit[slot_rows:]
    for store in stores[14:]:
        store.start()
    for store in stores:
        store.wait()


def loss_kernel(
    order, gathered, doc_total, slots, rank_ref, lengths_ref, positives_ref, counts_ref, near_ref, far_ref, unit_ref,
    tally_ref, losses_ref, grad_ref, kept_ref, sent_ref, sum_ref, scaled_ref,
):
    rows = unit_ref.shape[0]
    blocks = counts_ref.shape[0]
    per_doc = blocks // doc_total
    rank = rank_ref[0]
    half = blocks // 2
    sum_ref[...] = jnp.zeros_like(sum_ref)

    def gather_step(place, carry):
        near = rank ^ gather_order(place, gathered)
        far = near ^ (1 << gathered[-1])
        sum_ref[near // per_doc] += product(counts_ref[near], near_ref[place])
        sum_ref[far // per_doc] += product(counts_ref[far], far_ref[place])
        return carry

    lax.fori_loop(0, half, gather_step, 0, unroll=4)

    unit = unit_ref[...].astype(f32)
    lane = lax.broadcasted_iota(jnp.int32, (rows, LANES), 1)
    summed = jnp.zeros((rows, LANES), f32)
    for doc in range(doc_total):
        number = jnp.sum(sum_ref[doc] * unit, 1, keepdims=True)
        summed = jnp.where(lane == doc, number, summed)
    tally = tally_ref[...]
    most = jnp.maximum(tally, 1.0)
    slot_length = rows // slots
    narrow_size = lengths_ref.shape[0] // slots
    first = (rank & (narrow_size - 1)) * slots
    row = lax.broadcasted_iota(jnp.int32, (rows, LANES), 0)
    slot_row = lax.broadcasted_iota(jnp.int32, (slots, LANES), 0)
    valid = row < 0
    positive = jnp.zeros((slots, LANES), jnp.int32)
    for slot in range(slots):
        start = slot * slot_length
        valid = valid | ((row >= start) & (row < start + lengths_ref[first + slot]))
        positive = jnp.where(slot_row == slot, positives_ref[first + slot], positive)
    weight = jnp.where(valid, jnp.minimum(tally, 1.0), 0.0)
    pooled = (weight * (summed / most)).reshape(slots, slot_length, LANES)
    weight_sum = jnp.maximum(jnp.sum(weight.reshape(slots, slot_length, LANES), 1), 1.0)
    scores = jnp.sum(pooled, 1) / weight_sum / contrastive_sharpness_factor
    slot_lane = lax.broadcasted_iota(jnp.int32, (slots, LANES), 1)
    inside = slot_lane < doc_total
    scores = jnp.where(inside, scores, -jnp.inf)
    top = jnp.max(scores, -1, keepdims=True)
    powers = jnp.exp(scores - top)
    total = jnp.sum(powers, -1, keepdims=True)
    chosen = (slot_lane == positive).astype(f32)
    picked = jnp.sum(jnp.where(slot_lane == positive, scores, 0.0), -1, keepdims=True)
    losses_ref[...] = jnp.broadcast_to(top + jnp.log(total) - picked, (slots, LANES))
    slope = (powers / total - chosen) / contrastive_sharpness_factor / weight_sum
    slope = jnp.where(inside, slope, 0.0)
    slope = jnp.broadcast_to(slope[:, None, :], (slots, slot_length, LANES)).reshape(rows, LANES)
    slope = slope * weight / most

    grad = jnp.zeros((rows, unit.shape[1]), f32)
    for doc in range(doc_total):
        column = jnp.sum(jnp.where(lane == doc, slope, 0.0), 1, keepdims=True)
        grad = grad + column * sum_ref[doc]
        scaled_ref[doc] = (column * unit).T.astype(bf16)
    grad_ref[...] = grad

    def scatter_step(place, carry):
        kept = rank ^ scatter_order(place, order)
        sent = kept ^ (1 << order[0])
        kept_ref[place] = product(scaled_ref[kept // per_doc], counts_ref[kept]).astype(bf16)
        sent_ref[place] = product(scaled_ref[sent // per_doc], counts_ref[sent]).astype(bf16)
        return carry

    lax.fori_loop(0, half, scatter_step, 0, unroll=4)


def feed_back(
    part, waits, grad_unit, embed_ref, after_feed_ref, after_attend_ref, gate_slope_ref, up_slope_ref, feed_gain_ref,
    final_gain_ref, wo_ref, wg_ref, wu_ref, wd_ref, wp_ref, grads_out, after_out, mixed_out, more_ref,
):
    units, width = wd_ref.shape
    up_start, feed_start = units, 2 * units
    attend_start, embed_start = 2 * units + width, 2 * units + 2 * width
    embed = embed_ref[part, :]
    scale = lax.rsqrt(jnp.sum(embed * embed, -1, keepdims=True) + epsilon)
    inner = jnp.sum(grad_unit * embed, -1, keepdims=True)
    grad_embed = (scale * grad_unit - embed * (scale * scale * scale * inner)).astype(bf16)
    grads_out[:, embed_start : embed_start + embed.shape[1]] = grad_embed
    waits[0].wait()
    grad_after_feed = rms_back(
        after_feed_ref[part, :], final_gain_ref[...].reshape(1, -1), right_product(grad_embed, wp_ref[...])
    )
    after_out[...] = grad_after_feed
    grad_feed = grad_after_feed.astype(bf16)
    grads_out[:, feed_start:attend_start] = grad_feed
    for wait in waits[1:4]:
        wait.wait()

    def one_part(step, total):
        cols = tile(step, CHUNK)
        grad_hidden = right_product(grads_out[:, feed_start:attend_start], wd_ref[cols, :])
        grad_gate = (grad_hidden * gate_slope_ref[part, cols].astype(f32)).astype(bf16)
        grad_up = (grad_hidden * up_slope_ref[part, cols].astype(f32)).astype(bf16)
        grads_out[:, cols] = grad_gate
        grads_out[:, pl.ds(pl.multiple_of(up_start + step * CHUNK, CHUNK), CHUNK)] = grad_up
        more_ref[...] += right_product(grad_gate, wg_ref[:, cols]) + right_product(grad_up, wu_ref[:, cols])
        return total

    more_ref[...] = jnp.zeros_like(more_ref)
    lax.fori_loop(0, units // CHUNK, one_part, 0)
    total = more_ref[...]
    more = rms_back(after_attend_ref[part, :], feed_gain_ref[...].reshape(1, -1), total)
    grad_after_attend = after_out[...] + more
    after_out[...] = grad_after_attend
    grad_attend = grad_after_attend.astype(bf16)
    grads_out[:, attend_start:embed_start] = grad_attend
    waits[4].wait()
    mixed_out[...] = right_product(grad_attend, wo_ref[...]).astype(bf16)


def attend_back(
    far_parts, queries, keys, query_ref, key_ref, value_ref, probs_ref, mixed_ref, query_out, key_out, value_out,
    sums_out,
):
    rows = mixed_ref.shape[0]
    length = probs_ref.shape[2]
    half = LANES // 2
    first_lanes = lax.broadcasted_iota(jnp.int32, (rows, LANES), 1) < half
    row = lax.broadcasted_iota(jnp.int32, (rows, rows), 0)
    col = lax.broadcasted_iota(jnp.int32, (rows, rows), 1)
    flip = (row + col == rows - 1).astype(bf16)
    nothing = jnp.zeros((rows, LANES), f32)

    def one_pair(pair, carry):
        lanes = tile(pair)
        grad_mixed = halves(mixed_ref[:, lanes], first_lanes)
        query = halves(query_ref[queries, lanes], first_lanes)
        probs = probs_ref[pair]
        grad_probs = right_product(grad_mixed, value_ref[keys, lanes])
        exact = probs.astype(f32)
        inner = jnp.sum(exact * grad_probs, -1, keepdims=True)
        grad_scores = (exact * (grad_probs - inner)).astype(bf16)
        query_out(joined(product(grad_scores, key_ref[keys, lanes]), first_lanes).astype(bf16), pair)
        key_out(left_product(grad_scores, query).astype(bf16), pair)
        value_out(left_product(probs, grad_mixed).astype(bf16), pair)
        for side in range(2):
            head = 2 * pair + side
            own = grad_scores[side * rows : (side + 1) * rows, :]
            for part in range(length // LANES):
                piece = own[:, part * LANES : (part + 1) * LANES]
                if part in far_parts:
                    line = jnp.concatenate([piece.astype(f32), nothing], 1)
                else:
                    line = pltpu.roll(
                        jnp.concatenate([product(flip, piece), nothing], 1), 0, 1, stride=1, stride_axis=0
                    )
                sums_out[tile(head, 8), part * 2 * LANES : (part + 1) * 2 * LANES] = jnp.sum(
                    line.reshape(rows // 8, 8, 2 * LANES), 0
                )
        return carry

    lax.fori_loop(0, probs_ref.shape[0], one_pair, 0)


def input_back(tokens, gain_ref, after_ref, query, key, value, wq_ref, wk_ref, wv_ref):
    grad_normed = right_product(query, wq_ref[...])
    grad_normed = grad_normed + right_product(key, wk_ref[...])
    grad_normed = grad_normed + right_product(value, wv_ref[...])
    return after_ref[...] + rms_back(tokens, gain_ref[...].reshape(1, -1), grad_normed)


def table_sums(sums_ref, distances):
    heads = sums_ref.shape[0] // 8
    span = lax.broadcasted_iota(jnp.int32, (2 * LANES, LANES), 0) - (LANES - 1)
    bucket = lax.broadcasted_iota(jnp.int32, (2 * LANES, LANES), 1)
    total = jnp.zeros((heads, LANES), f32)
    for part, distance in enumerate(distances):
        lines = jnp.sum(sums_ref[:, part * 2 * LANES : (part + 1) * 2 * LANES].reshape(heads, 8, 2 * LANES), 1)
        hot = (bucket_index(span + distance * LANES) == bucket).astype(f32)
        total = total + lax.dot_general(
            lines, hot, (((1,), (0,)), ((), ())), precision=highest, preferred_element_type=f32
        )
    return total


def slot_back_kernel(
    slots, rank_ref, queries_ref, grad_unit_ref, embed_ref, after_feed_ref, after_attend_ref, gate_slope_ref,
    up_slope_ref, query_ref, key_ref, value_ref, probs_ref, attend_gain_ref, feed_gain_ref, final_gain_ref,
    wp_any, wd_any, wg_any, wu_any, wo_any, wq_any, wk_any, wv_any,
    grads_out, tokens_out, table_out,
    wp_ref, wd_ref, wg_ref, wu_ref, wo_ref, wq_ref, wk_ref, wv_ref, slot_ref, after_ref, mixed_ref, more_ref, sums_ref,
    load_sems, slot_sem,
):
    weights = loads(
        (wp_any, wd_any, wg_any, wu_any, wo_any, wq_any, wk_any, wv_any),
        (wp_ref, wd_ref, wg_ref, wu_ref, wo_ref, wq_ref, wk_ref, wv_ref),
        load_sems,
    )
    for weight in weights:
        weight.start()
    narrow_size = queries_ref.shape[0] // slots
    first = (rank_ref[0] & (narrow_size - 1)) * slots
    load_slots = pltpu.make_async_copy(queries_ref.at[pl.ds(first, slots)], slot_ref, slot_sem)
    load_slots.start()
    rows, width = after_ref.shape
    part = slice(0, rows)
    feed_back(
        part, weights[:5], grad_unit_ref[...], embed_ref, after_feed_ref, after_attend_ref, gate_slope_ref,
        up_slope_ref, feed_gain_ref, final_gain_ref, wo_ref, wg_ref, wu_ref, wd_ref, wp_ref, grads_out, after_ref,
        mixed_ref, more_ref,
    )
    start = grads_out.shape[1] - 3 * width

    def third(place):
        return grads_out.at[:, start + place * width : start + (place + 1) * width]

    def out(place):
        def store(values, pair):
            grads_out[:, pl.ds(pl.multiple_of(start + place * width + pair * LANES, LANES), LANES)] = values

        return store

    attend_back(
        (), part, part, query_ref, key_ref, value_ref, probs_ref, mixed_ref, out(0), out(1), out(2), sums_ref
    )
    table_out[...] = table_sums(sums_ref, [0])
    for weight in weights[5:]:
        weight.wait()
    load_slots.wait()
    tokens_out[...] = input_back(
        slot_ref[...].reshape(rows, width).astype(f32), attend_gain_ref, after_ref, third(0)[...], third(1)[...],
        third(2)[...], wq_ref, wk_ref, wv_ref,
    )


def doc_feed_kernel(came, *refs):
    parts, refs = refs[:came], refs[came:]
    (
        embed_ref, after_feed_ref, after_attend_ref, gate_slope_ref, up_slope_ref, feed_gain_ref, final_gain_ref,
        wp_any, wd_any, wg_any, wu_any, wo_any,
        grads_out, after_out, mixed_out,
        wp_ref, wd_ref, wg_ref, wu_ref, wo_ref, more_ref, load_sems,
    ) = refs
    weights = loads(
        (wp_any, wd_any, wg_any, wu_any, wo_any), (wp_ref, wd_ref, wg_ref, wu_ref, wo_ref), load_sems
    )
    for weight in weights:
        weight.start()
    rows = after_out.shape[0]
    grad_unit = add(*(part[0] for part in parts)).T
    feed_back(
        slice(embed_ref.shape[0] - rows, embed_ref.shape[0]), weights, grad_unit, embed_ref, after_feed_ref,
        after_attend_ref, gate_slope_ref, up_slope_ref, feed_gain_ref, final_gain_ref, wo_ref, wg_ref, wu_ref, wd_ref,
        wp_ref, grads_out, after_out, mixed_out, more_ref,
    )


def doc_attend_kernel(
    rank_ref, query_ref, key_ref, value_ref, probs_ref, mixed_ref, slot_table_ref, grads_out, table_out, query_room,
    sums_ref,
):
    rows, width = query_room.shape
    length = probs_ref.shape[2]
    first = key_ref.shape[0] - length

    def query_out(values, pair):
        query_room[:, tile(pair)] = values

    def key_out(values, pair):
        grads_out[:length, tile(pair)] = values

    def value_out(values, pair):
        grads_out[:length, pl.ds(pl.multiple_of(width + pair * LANES, LANES), LANES)] = values

    attend_back(
        (2,), slice(first, first + rows), slice(first, key_ref.shape[0]), query_ref, key_ref, value_ref, probs_ref,
        mixed_ref, query_out, key_out, value_out, sums_ref,
    )
    grads_out[length:, :width] = query_room[: rows // 2, :]
    grads_out[length:, width:] = query_room[rows // 2 :, :]
    parts = length // LANES
    narrow = rank_ref[0] & (parts - 1)
    table = table_sums(sums_ref, [(narrow ^ part) - narrow for part in range(parts)]) + slot_table_ref[...]
    heads = table.shape[0]
    table_out[...] = jnp.concatenate([table, jnp.zeros((16 - heads, LANES), f32)], 0).astype(bf16)


def pick_columns(values, total, order, flipped, rank):
    count = 1 << len(order) + 1
    size = total // count
    row = lax.broadcasted_iota(jnp.int32, (total, total // 2), 0)
    col = lax.broadcasted_iota(jnp.int32, (total, total // 2), 1)
    source = (scatter_order(col // size, order) ^ rank ^ flipped) * size + col % size
    return product(values, (row == source).astype(bf16)).astype(bf16)


def pick_tiles(values_ref, order, flipped, rank, store):
    rows = values_ref.shape[0]
    half = LANES // 2
    first_lanes = lax.broadcasted_iota(jnp.int32, (rows, LANES), 1) < half
    upper = ((rank ^ flipped) & 1) == 1

    def one_tile(step, carry):
        place = 2 * step
        sides = []
        for side in range(2):
            tile = (rank ^ scatter_order(place + side, order)) >> 1
            values = values_ref[:, pl.ds(pl.multiple_of(tile * LANES, LANES), LANES)].astype(f32)
            turned = pltpu.roll(values, half, 1)
            sides.append(jnp.where(upper, turned, values) if side == 0 else jnp.where(upper, values, turned))
        store(step, jnp.where(first_lanes, sides[0], sides[1]).astype(bf16))
        return carry

    lax.fori_loop(0, 1 << len(order) - 1, one_tile, 0)


def turn_kernel(
    orders, rank_ref, all_ref, normed_feed_ref, mixed_ref, normed_final_ref, hidden_ref, kept_out, sent_out, doc_out,
):
    first, second, third, fourth = orders
    rank = rank_ref[0]
    rows, width = normed_feed_ref.shape
    units = hidden_ref.shape[1]
    slots = all_ref.shape[0] - doc_out.shape[0]
    half = width // 2
    for out, flipped in ((kept_out, 0), (sent_out, 1)):
        out[:, :half] = pick_columns(normed_feed_ref[...], width, first, flipped, rank)
        out[:, half : 2 * half] = pick_columns(normed_feed_ref[...], width, second, flipped, rank)
        out[:, 2 * half : 3 * half] = pick_columns(mixed_ref[...], width, first, flipped, rank)
        out[:, 3 * half : 4 * half] = pick_columns(normed_final_ref[...], width, second, flipped, rank)
        start = 4 * half
        if units >> (len(third) + 1) == LANES // 2:

            def store(place, values):
                out[:, pl.ds(pl.multiple_of(start + place * LANES, LANES), LANES)] = values

            pick_tiles(hidden_ref, third, flipped, rank, store)
        else:
            out[:, start : start + units // 2] = pick_columns(hidden_ref[...], units, third, flipped, rank)
        start = start + units // 2
        out[slots:, start:] = jnp.zeros((rows - slots, half), bf16)
        if flipped:
            out[:slots, start:] = pick_columns(all_ref[:slots, :], width, fourth, flipped, rank)
        else:
            both = pick_columns(all_ref[...], width, fourth, flipped, rank)
            out[:slots, start:] = both[:slots]
            doc_out[...] = both[slots:]


def store_product(left, right_ref, columns, kept_ref, sent_ref, start):
    half = left.shape[1] // 2
    size = 2 * LANES

    def one_part(first, size):
        here = pl.ds(pl.multiple_of(start + first, LANES), size)
        result = left_product(left, right_ref[:, pl.ds(pl.multiple_of(first, LANES), size)]).astype(bf16)
        kept_ref[:half, here] = result[:half]
        sent_ref[:half, here] = result[half:]

    def step(place, carry):
        one_part(place * size, size)
        return carry

    lax.fori_loop(0, columns // size, step, 0)
    if columns % size:
        one_part(columns // size * size, columns % size)


def weight_kernel(
    terms, kept_any, came_any, slot_any, slot_came_any, doc_any, doc_came_any, kept_ref, sent_ref, left_ref, right_ref,
    sems,
):
    rows = kept_any.shape[0]
    part = slot_any.shape[0]
    copies = []
    left_place, right_place = 0, 0
    for left_start, left_width, right_start, right_width in terms:
        pieces = []
        for place, ref in enumerate((kept_any, came_any)):
            source = ref.at[:, left_start : left_start + left_width]
            target = left_ref.at[place * rows : (place + 1) * rows, left_place : left_place + left_width]
            pieces.append((source, target))
        for place, ref in enumerate((slot_any, doc_any, slot_came_any, doc_came_any)):
            source = ref.at[:, right_start : right_start + right_width]
            target = right_ref.at[place * part : (place + 1) * part, right_place : right_place + right_width]
            pieces.append((source, target))
        first = sum(len(group) for group in copies)
        copies.append(
            [pltpu.make_async_copy(one, two, sems.at[first + i]) for i, (one, two) in enumerate(pieces)]
        )
        left_place += left_width
        right_place += right_width
    for group in copies:
        for copy in group:
            copy.start()
    left_place, right_place = 0, 0
    for group, (_, left_width, _, right_width) in zip(copies, terms):
        for copy in group:
            copy.wait()
        left = left_ref[:, left_place : left_place + left_width]
        right = right_ref.at[:, right_place : right_place + right_width]
        store_product(left, right, right_width, kept_ref, sent_ref, right_place)
        left_place += left_width
        right_place += right_width


def attend_weight_kernel(
    doc_ref, kept_any, came_any, slot_any, slot_came_any, grads_ref, other_ref, table_ref, other_table_ref,
    kept_out, sent_out, pair_kept, pair_sent, slot_room, slot_came_room, left_ref, right_ref, query_ref, sems,
):
    rows = slot_any.shape[0]
    width = slot_room.shape[1] // 3
    half = doc_ref.shape[1]
    length = doc_ref.shape[0]
    start = slot_any.shape[1] - 3 * width
    lanes = slice(kept_any.shape[1] - half, kept_any.shape[1])
    copies = loads(
        (slot_any.at[:, start:], slot_came_any.at[:, start:], kept_any.at[:rows, lanes], came_any.at[:rows, lanes]),
        (slot_room, slot_came_room, left_ref.at[length : length + rows, :], left_ref.at[length + rows :, :]),
        sems,
    )
    for copy in copies:
        copy.start()
    left_ref[:length, :] = doc_ref[...]
    for part in range(length // LANES):
        here = slice(part * LANES, (part + 1) * LANES)
        there = slice((part ^ 1) * LANES, ((part ^ 1) + 1) * LANES)
        right_ref[here, :] = add(grads_ref[here, :], other_ref[there, :]).astype(bf16)
    pair_kept[...] = right_ref[:LANES, :]
    pair_sent[...] = right_ref[2 * LANES : 3 * LANES, :]
    small = LANES // 2
    for place, ref in enumerate((grads_ref, other_ref)):
        query_ref[2 * place * small : (2 * place + 1) * small, :] = ref[length:, :width]
        query_ref[(2 * place + 1) * small : (2 * place + 2) * small, :] = ref[length:, width:]
    for copy in copies:
        copy.wait()
    right_ref[length : length + rows, :] = slot_room[:, width:]
    right_ref[length + rows :, :] = slot_came_room[:, width:]
    query_ref[2 * LANES : 2 * LANES + rows, :] = slot_room[:, :width]
    query_ref[2 * LANES + rows :, :] = slot_came_room[:, :width]
    store_product(left_ref[...], right_ref, 2 * width, kept_out, sent_out, width)
    left = jnp.concatenate([left_ref[: 2 * LANES, :], left_ref[length:, :]], 0)
    store_product(left, query_ref, width, kept_out, sent_out, 0)
    tail = sent_out.shape[0] - 16
    sent_out[tail:, :] = jnp.zeros((16, sent_out.shape[1]), bf16)
    sent_out[tail:, :LANES] = add(table_ref[...], other_table_ref[...]).astype(bf16)


def doc_input_kernel(
    tokens_ref, gain_ref, after_ref, grads_ref, kept_ref, came_ref, wq_ref, wk_ref, wv_ref, tokens_out
):
    width = tokens_ref.shape[1]
    rest = grads_ref.shape[0] - tokens_ref.shape[0] // 2
    query = jnp.concatenate([grads_ref[rest:, :width], grads_ref[rest:, width:]], 0)
    pair = add(kept_ref[...], came_ref[...]).astype(bf16)
    tokens_out[...] = input_back(
        tokens_ref[...].astype(f32), gain_ref, after_ref, query, pair[:, :width], pair[:, width:], wq_ref, wk_ref, wv_ref
    )


def on_device(
    doc_tokens, query_tokens, query_lengths, positive_docs, retrieved, attend_gain, query_weight, key_weight,
    value_weight, output_weight, bias_table, feed_gain, gate_weight, up_weight, down_weight, final_gain, proj_weight,
):
    narrow_size = lax.axis_size("narrow")
    bits = rank_bits()
    rank = my_rank()
    rank_word = rank.astype(jnp.int32).reshape(1)
    doc_rows, width = doc_tokens.shape[1:]
    doc_length = doc_rows * narrow_size
    doc_total = doc_tokens.shape[0] * lax.axis_size("wide")
    slots = query_tokens.shape[0] // narrow_size
    slot_length = query_tokens.shape[1]
    heads = bias_table.shape[1]
    units = gate_weight.shape[1]
    columns = proj_weight.shape[1]
    slot_rows = slots * slot_length
    rows = slot_rows + doc_rows
    blocks = doc_total * doc_length // LANES
    assert doc_tokens.shape[0] == 1 and doc_rows == LANES and slot_rows == LANES and narrow_size == 4
    assert columns == LANES and doc_total <= LANES and blocks == 1 << bits
    gains = (attend_gain, feed_gain, final_gain)
    dma = pltpu.SemaphoreType.DMA
    over_y = [1, 2] + list(range(3, bits))
    over_x = [2, 1] + list(range(3, bits))
    over_z = [bits - 2, 2, 1] + list(range(3, bits - 2)) + [bits - 1]

    orders = (over_y, over_x, over_x, over_z)
    own_tokens = doc_tokens[0]
    y_tokens = swap(own_tokens, 2)
    core_tokens = swap(own_tokens, 1)
    pairs = heads // 2
    doc_bias, slot_bias = call(
        functools.partial(bias_kernel, doc_length),
        [shape((pairs, 2 * doc_rows, doc_length)), shape((pairs, 2 * slot_rows, slot_rows))],
        [rank_word, bias_table],
        "s",
        [pltpu.VMEM((heads, 2 * doc_length + LANES), f32)],
    )
    y_tokens = after(y_tokens, doc_bias)
    both_tokens = swap(y_tokens, 1)

    all_rows = slot_rows + doc_length
    forward_shapes = [
        shape((all_rows, width), bf16),
        shape((rows, width), bf16),
        shape((all_rows, width), bf16),
        shape((all_rows, width), bf16),
        shape((pairs, 2 * doc_rows, doc_length), bf16),
        shape((pairs, 2 * slot_rows, slot_rows), bf16),
        shape((rows, width), bf16),
        shape((rows, width)),
        shape((rows, width), bf16),
        shape((rows, units), bf16),
        shape((rows, units), bf16),
        shape((rows, units), bf16),
        shape((rows, width)),
        shape((rows, width), bf16),
        shape((rows, columns)),
        shape((slot_rows, columns), bf16),
        shape((doc_rows, columns), bf16),
    ]
    weights = [
        query_weight, key_weight, value_weight, output_weight, gate_weight, up_weight, down_weight, proj_weight,
    ]
    slot_room = pltpu.VMEM((slots, slot_length, width), bf16)
    (
        all_normed, query, key, value, doc_probs, slot_probs, mixed, after_attend, normed_feed, hidden, gate_slope,
        up_slope, after_feed, normed_final, embed, slot_unit, doc_unit,
    ) = call(
        functools.partial(forward_kernel, slots, slot_length),
        forward_shapes,
        [
            rank_word, query_lengths, query_tokens, own_tokens, core_tokens, y_tokens, both_tokens, doc_bias, slot_bias,
            *gains, *weights,
        ],
        "ssa" + "v" * 9 + "a" * 8 + "a" * len(forward_shapes),
        [room(value) for value in forward_shapes]
        + [room(weight) for weight in weights]
        + [slot_room, dma((8,)), dma((len(forward_shapes),)), dma],
    )

    phases = [list(range(high, max(high - 2, 0), -1)) for high in range(bits - 1, 0, -2)]
    gathered = []
    near_units = doc_unit[None]
    for phase, group in enumerate(phases):
        group = group[::-1]
        masks = [gather_order(place, group) for place in range(1, 1 << len(group))]
        came = [swap(near_units, mask) for mask in masks]
        if phase == 0:
            counts, tally = call(
                functools.partial(count_kernel, doc_length, doc_total),
                [shape((blocks, slot_rows, LANES), bf16), shape((slot_rows, LANES))],
                after([rank_word, retrieved], doc_unit),
                "sa",
                [
                    pltpu.VMEM((slots, slot_length, retrieved.shape[2]), jnp.int32),
                    pltpu.VMEM((slot_rows, retrieved.shape[2]), jnp.int32),
                    pltpu.VMEM((blocks * slot_rows, LANES), f32),
                    dma,
                ],
            )
            came = after(came, tally)
        if phase == 1:
            turned_cols = 5 * width // 2 + units // 2
            turned, turned_sent, turned_docs = call(
                functools.partial(turn_kernel, orders),
                [shape((rows, turned_cols), bf16)] * 2 + [shape((doc_length, width // 2), bf16)],
                after([rank_word, all_normed, normed_feed, mixed, normed_final, hidden], near_units),
                "s",
            )
            came = after(came, turned)
        near_units = jnp.concatenate([near_units] + came, 0)
        gathered = gathered + group
    gathered = gathered + [0]
    far_units = swap(near_units, 1)

    order = list(range(bits))
    half = blocks // 2
    losses, grad_slot_unit, kept, sent = call(
        functools.partial(loss_kernel, order, gathered, doc_total, slots),
        [
            shape((slots, LANES)),
            shape((slot_rows, columns)),
            shape((half, columns, LANES), bf16),
            shape((half, columns, LANES), bf16),
        ],
        [rank_word, query_lengths, positive_docs, counts, near_units, far_units, slot_unit, tally],
        "sss",
        [
            pltpu.VMEM((doc_total, slot_rows, columns), f32),
            pltpu.VMEM((doc_total, columns, slot_rows), bf16),
        ],
    )
    turned_came = swap(after(turned_sent, losses), 1)
    back_weights = [proj_weight, down_weight, gate_weight, up_weight, output_weight]
    all_weights = back_weights + [query_weight, key_weight, value_weight]
    doc_cols = 2 * units + 2 * width + columns

    came = [swap(sent, 1)]
    rest = order[1:]
    parts = [kept]
    first_phase = True
    while rest:
        group, rest = rest[:2], rest[2:]
        count = 1 << len(group)
        size = parts[0].shape[0] // count
        pieces = []
        for place in range(count):
            here = slice(place * size, (place + 1) * size)
            pieces.append(add(*(part[here] for part in parts), *(one[here] for one in came)).astype(bf16))
        masks = [scatter_order(place, group) for place in range(count)]
        came = [swap(piece, mask) for piece, mask in zip(pieces[1:], masks[1:])]
        parts = [pieces[0]]
        if first_phase:
            slot_grads, query_grad, slot_table = call(
                functools.partial(slot_back_kernel, slots),
                [shape((slot_rows, doc_cols + 3 * width), bf16), shape((slot_rows, width)), shape((heads, LANES))],
                [rank_word, query_tokens, after(grad_slot_unit, pieces[1], turned_came)]
                + [embed, after_feed, after_attend, gate_slope, up_slope, query, key, value, slot_probs, *gains]
                + all_weights,
                "sa" + "v" * 13 + "a" * 8,
                [room(weight) for weight in all_weights]
                + [slot_room, pltpu.VMEM((slot_rows, width), f32), pltpu.VMEM((slot_rows, width), bf16)]
                + [pltpu.VMEM((slot_rows, width), f32)]
                + [pltpu.VMEM((heads * 8, 2 * LANES), f32), dma((8,)), dma],
            )
            came = after(came, slot_table)
            first_phase = False
    slot_came = swap(after(slot_grads, *pieces[1:]), 1)

    doc_grads, doc_after, doc_mixed = call(
        functools.partial(doc_feed_kernel, 1 + len(came)),
        [shape((doc_rows, doc_cols), bf16), shape((doc_rows, width)), shape((doc_rows, width), bf16)],
        parts + after(came, slot_came)
        + [embed, after_feed, after_attend, gate_slope, up_slope, gains[1], gains[2]]
        + back_weights,
        "v" * (8 + len(came)) + "a" * 5,
        [room(weight) for weight in back_weights] + [pltpu.VMEM((doc_rows, width), f32), dma((5,))],
    )
    doc_came = swap(doc_grads, 1)

    class Stream:
        def __init__(self, kept, sent, order):
            self.kept, self.order, self.step = kept, order, 0
            self.loaded = sent.shape[0] > kept.shape[0]
            if self.loaded:
                self.small = sent[-16:]
            self.send(sent)

        def send(self, sent):
            self.came = swap(sent, 1 << self.order[self.step])
            self.step += 1

        def advance(self, *wait):
            came = after(self.came, *wait)
            if self.loaded:
                self.small = add(self.small, came[-16:]).astype(bf16)
                came = came[:-16]
            if self.step == len(self.order):
                self.result = add(self.kept, came)
                return self.result
            self.kept, sent = cut(self.kept, came)
            if self.loaded:
                sent = jnp.concatenate([sent, self.small], 0)
            self.send(sent)
            return self.kept

    def weight_product(terms, order, *wait):
        left = sum(term[1] for term in terms)
        right = sum(term[3] for term in terms)
        tall = terms[0][1] // 2
        args = after([turned, turned_came, slot_grads, slot_came, doc_grads, doc_came], *wait)
        kept, sent = call(
            functools.partial(weight_kernel, terms),
            [shape((tall, right), bf16)] * 2,
            args,
            "a" * 6,
            [pltpu.VMEM((2 * rows, left), bf16), pltpu.VMEM((2 * rows, right), bf16), dma((6 * len(terms),))],
        )
        return Stream(kept, sent, order)

    small_half = width // 2
    att_grads, table = call(
        doc_attend_kernel,
        [shape((doc_length + doc_rows // 2, 2 * width), bf16), shape((16, LANES), bf16)],
        [rank_word, query, key, value, doc_probs, doc_mixed, slot_table],
        "s",
        [pltpu.VMEM((doc_rows, width), bf16), pltpu.VMEM((heads * 8, 2 * doc_length), f32)],
    )
    att_came, table_came = swap(att_grads, 1), swap(table, 1)
    first = weight_product(
        [(0, small_half, 0, units), (2 * small_half, small_half, 2 * units + width, width)], orders[0], table
    )
    fourth_kept, fourth_sent, pair_kept, pair_sent = call(
        attend_weight_kernel,
        [
            shape((width // 4, 3 * width), bf16),
            shape((width // 4 + 16, 3 * width), bf16),
            shape((doc_rows, 2 * width), bf16),
            shape((doc_rows, 2 * width), bf16),
        ],
        [turned_docs, turned, turned_came, slot_grads, slot_came, att_grads, att_came, after(table, first.kept), table_came],
        "vaaaa",
        [
            pltpu.VMEM((slot_rows, 3 * width), bf16),
            pltpu.VMEM((slot_rows, 3 * width), bf16),
            pltpu.VMEM((doc_length + 2 * slot_rows, width // 2), bf16),
            pltpu.VMEM((doc_length + 2 * slot_rows, 2 * width), bf16),
            pltpu.VMEM((2 * doc_rows + 2 * slot_rows, width), bf16),
            dma((4,)),
        ],
    )
    fourth = Stream(fourth_kept, fourth_sent, orders[3])
    second = weight_product(
        [(small_half, small_half, units, units), (3 * small_half, small_half, 2 * units + 2 * width, columns)],
        orders[1],
        fourth_kept,
    )
    third = weight_product([(4 * small_half, units // 2, 2 * units, width)], orders[2], second.kept)
    pair_came = swap(pair_sent, 2)
    done = third.kept
    for step in range(bits - 1):
        for stream in (first, fourth, second, third):
            done = stream.advance(done)
        if step == 1:
            (doc_grad,) = call(
                doc_input_kernel,
                [shape((doc_rows, width))],
                [own_tokens, gains[0], doc_after, att_grads, pair_kept, after(pair_came, done)]
                + [query_weight, key_weight, value_weight],
            )
            done = doc_grad

    def own_rows(values):
        return lax.dynamic_slice_in_dim(values, rank * (width >> bits), width >> bits, 0).astype(f32)

    def gain_grad(gain, *pairs):
        return sum(jnp.sum(own_rows(weight) * grad, 1) for weight, grad in pairs) / own_rows(gain)

    gate_grad, output_grad = first.result[:, :units], first.result[:, units:]
    up_grad, proj_grad = second.result[:, :units], second.result[:, units:]
    query_g, key_g, value_g = (fourth.result[:, place * width : (place + 1) * width] for place in range(3))
    return (
        losses[:, 0],
        doc_grad[None],
        query_grad.reshape(slots, slot_length, width),
        gain_grad(attend_gain, (query_weight, query_g), (key_weight, key_g), (value_weight, value_g)),
        query_g,
        key_g,
        value_g,
        output_grad,
        fourth.small[:heads, :BUCKETS].astype(f32).T,
        gain_grad(feed_gain, (gate_weight, gate_grad), (up_weight, up_grad)),
        gate_grad,
        up_grad,
        third.result,
        gain_grad(final_gain, (proj_weight, proj_grad)),
        proj_grad,
    )


def solution(mesh):
    return jax.shard_map(
        on_device,
        mesh=mesh,
        in_specs=(
            P("wide", "narrow", None),
            P("wide", None, None),
            P("wide"),
            P("wide"),
            P("wide", None, None),
            P(),
            P(),
            P(),
            P(),
            P(),
            P(),
            P(),
            P(),
            P(),
            P(),
            P(),
            P(),
        ),
        out_specs=(
            P(("wide", "narrow")),
            P("wide", "narrow", None),
            P(("wide", "narrow"), None, None),
            P(("wide", "narrow")),
            P(("wide", "narrow"), None),
            P(("wide", "narrow"), None),
            P(("wide", "narrow"), None),
            P(("wide", "narrow"), None),
            P(),
            P(("wide", "narrow")),
            P(("wide", "narrow"), None),
            P(("wide", "narrow"), None),
            P(("wide", "narrow"), None),
            P(("wide", "narrow")),
            P(("wide", "narrow"), None),
        ),
        check_vma=False,
    )
```

```python
import functools

import jax
import jax.numpy as jnp
from jax import lax
from jax.experimental import pallas as pl
from jax.experimental.pallas import tpu as pltpu
from jax.sharding import PartitionSpec as P

BUCKETS = 32
LANES = 128
CHUNK = 512
VM = (60, 34, 24, 16, 8)
COST = 1.1e9

epsilon = 1e-06
contrastive_sharpness_factor = 0.01
masked_value = -1000000000.0
bucket_edges = (12, 16, 23, 32, 46, 64, 91)
highest = lax.Precision.HIGHEST
f32 = jnp.float32
bf16 = jnp.bfloat16


def bucket_index(offset):
    distance = jnp.abs(offset)
    beyond = 8 + sum(((distance >= boundary).astype(jnp.int32) for boundary in bucket_edges))
    inside = jnp.where(distance < 8, distance, beyond)
    return inside + BUCKETS // 2 * (offset > 0).astype(jnp.int32)


def product(left, right):
    return jnp.dot(left, right, preferred_element_type=f32)


def left_product(left, right):
    return lax.dot_general(left, right, (((0,), (0,)), ((), ())), preferred_element_type=f32)


def right_product(left, right):
    return lax.dot_general(left, right, (((1,), (1,)), ((), ())), preferred_element_type=f32)


def rank_bits():
    return (lax.axis_size("wide") * lax.axis_size("narrow")).bit_length() - 1


def my_rank():
    return lax.axis_index("wide") * lax.axis_size("narrow") + lax.axis_index("narrow")


def swap(values, mask):
    ranks = 1 << rank_bits()
    pairs = [(rank, rank ^ mask) for rank in range(ranks)]
    return lax.ppermute(values, ("wide", "narrow"), pairs)


def scatter_order(position, order):
    count = len(order)
    return sum(((position >> (count - 1 - step)) & 1) << bit for step, bit in enumerate(order))


def gather_order(position, order):
    return sum(((position >> step) & 1) << bit for step, bit in enumerate(order))


def after(values, *others):
    flat, tree = jax.tree.flatten(values)
    done = lax.optimization_barrier(tuple(flat) + tuple(others))
    return jax.tree.unflatten(tree, done[: len(flat)])


def add(*values):
    total = values[0].astype(f32)
    for value in values[1:]:
        total = total + value.astype(f32)
    return total


def cut_kernel(kept_ref, came_ref, kept_out, sent_out):
    half = kept_out.shape[0]
    kept_out[...] = add(kept_ref[:half, :], came_ref[:half, :]).astype(bf16)
    sent_out[...] = add(kept_ref[half:, :], came_ref[half:, :]).astype(bf16)


def cut_loaded_kernel(kept_ref, came_ref, small_ref, kept_out, sent_out, small_out):
    half = kept_out.shape[0]
    kept_out[...] = add(kept_ref[:half, :], came_ref[:half, :]).astype(bf16)
    sent_out[:half, :] = add(kept_ref[half:, :], came_ref[half : 2 * half, :]).astype(bf16)
    small = add(small_ref[...], came_ref[2 * half :, :]).astype(bf16)
    sent_out[half:, :] = small
    small_out[...] = small


def cut(kept, came, small=None):
    half, cols = kept.shape[0] // 2, kept.shape[1]
    if half % 16 == 0 and small is None:
        return *call(cut_kernel, [shape((half, cols), bf16)] * 2, [kept, came], vmem=VM[4], us=0), None
    if half % 16 == 0:
        outs = [shape((half, cols), bf16), shape((half + 16, cols), bf16), shape((16, cols), bf16)]
        return call(cut_loaded_kernel, outs, [kept, came, small], vmem=VM[4], us=0)
    if small is not None:
        small = add(small, came[-16:]).astype(bf16)
        came = came[:-16]
    next_sent = add(kept[half:], came[half:]).astype(bf16)
    if small is not None:
        next_sent = jnp.concatenate([next_sent, small], 0)
    return add(kept[:half], came[:half]).astype(bf16), next_sent, small


def call(kernel, outs, args, spaces="", scratch=(), vmem=None, us=3, wide=False):
    kinds = {"s": pltpu.SMEM, "v": pltpu.VMEM, "a": pl.ANY, "h": pltpu.HBM}
    spaces = spaces.ljust(len(args) + len(outs), "v")
    specs = [pl.BlockSpec(memory_space=kinds[kind]) for kind in spaces]
    return pl.pallas_call(
        kernel,
        out_shape=tuple(outs),
        in_specs=specs[: len(args)],
        out_specs=tuple(specs[len(args) :]),
        scratch_shapes=list(scratch),
        compiler_params=pltpu.CompilerParams(vmem_limit_bytes=(60 if wide else vmem or VM[3]) * 1024 * 1024),
        cost_estimate=pl.CostEstimate(flops=int(us * COST), bytes_accessed=0, transcendentals=0),
    )(*args)


def shape(dims, kind=f32):
    return jax.ShapeDtypeStruct(tuple(dims), kind)


def room(values):
    return pltpu.VMEM(values.shape, values.dtype)


def loads(refs, rooms, sems):
    return [pltpu.make_async_copy(ref, place, sems.at[i]) for i, (ref, place) in enumerate(zip(refs, rooms))]


def bias_kernel(doc_length, rank_ref, table_ref, doc_bias_ref, slot_bias_ref, line_ref):
    pairs = doc_bias_ref.shape[0]
    parts = doc_length // LANES
    length = line_ref.shape[1]
    offset = lax.broadcasted_iota(jnp.int32, (BUCKETS, length), 1) - doc_length
    hot = (bucket_index(offset) == lax.broadcasted_iota(jnp.int32, (BUCKETS, length), 0)).astype(f32)
    line_ref[...] = lax.dot_general(
        table_ref[...], hot, (((0,), (0,)), ((), ())), precision=highest, preferred_element_type=f32
    )
    narrow = rank_ref[0] & (parts - 1)

    def spread(head, start):
        line = line_ref[pl.ds(head, 1), pl.ds(pl.multiple_of(start, LANES), 2 * LANES)]
        rolled = pltpu.roll(jnp.broadcast_to(line, (LANES, 2 * LANES)), 0, 1, stride=1, stride_axis=0)
        return rolled[:, LANES:]

    def one_pair(pair, carry):
        for side in range(2):
            rows = slice(side * LANES, (side + 1) * LANES)
            head = 2 * pair + side
            for part in range(parts):
                distance = (narrow ^ part) - narrow
                doc_bias_ref[pair, rows, part * LANES : (part + 1) * LANES] = spread(
                    head, doc_length - LANES + distance * LANES
                )
            slot_bias_ref[pair, rows, :] = spread(head, doc_length - LANES)
        return carry

    lax.fori_loop(0, pairs, one_pair, 0)


def count_kernel(doc_length, doc_total, rank_ref, picked_ref, counts_ref, tally_ref, load_ref, places_ref, scratch_ref, sem):
    slots, slot_length, picks = load_ref.shape
    rows = slots * slot_length
    blocks = counts_ref.shape[0]
    narrow_size = picked_ref.shape[0] // slots
    first = (rank_ref[0] & (narrow_size - 1)) * slots
    load = pltpu.make_async_copy(picked_ref.at[pl.ds(first, slots)], load_ref, sem)
    load.start()
    load.wait()

    places_ref[...] = load_ref[...].reshape(rows, picks)

    def one_row(row, carry):
        places = places_ref[pl.ds(row, 1), :]
        high = places >> 7
        low = places & 127
        high_hot = (lax.broadcasted_iota(jnp.int32, (blocks, picks), 0) == high).astype(bf16)
        low_hot = (lax.broadcasted_iota(jnp.int32, (LANES, picks), 0) == low).astype(bf16)
        scratch_ref[pl.ds(row, blocks, stride=rows), :] = right_product(high_hot, low_hot)
        return carry

    lax.fori_loop(0, rows, one_row, 0, unroll=8)

    def one_block(block, carry):
        start = pl.multiple_of(block * rows, rows)
        counts_ref[block] = scratch_ref[pl.ds(start, rows), :].astype(bf16)
        return carry

    lax.fori_loop(0, blocks, one_block, 0, unroll=4)

    owner = places_ref[...] // doc_length
    lane = lax.broadcasted_iota(jnp.int32, (rows, LANES), 1)
    tally = jnp.zeros((rows, LANES), f32)
    for doc in range(doc_total):
        number = jnp.sum((owner == doc).astype(f32), 1, keepdims=True)
        tally = jnp.where(lane == doc, number, tally)
    tally_ref[...] = tally


def rms_scale(values):
    return lax.rsqrt(jnp.mean(values * values, -1, keepdims=True) + epsilon)


def rms_back(values, gain, grad):
    scale = rms_scale(values)
    weighted = grad * gain
    inner = jnp.mean(weighted * values, -1, keepdims=True)
    return scale * weighted - values * (scale * scale * scale * inner)


def tile(index, size=LANES):
    return pl.ds(pl.multiple_of(index * size, size), size)


def halves(values, zero_row):
    return jnp.concatenate([jnp.where(zero_row, values, jnp.zeros((), values.dtype)),
                            jnp.where(zero_row, jnp.zeros((), values.dtype), values)], 0)


def joined(values, first_lanes):
    rows = values.shape[0] // 2
    return jnp.where(first_lanes, values[:rows], values[rows:])


def forward_kernel(
    slots, slot_length, rank_ref, lengths_ref, queries_ref, own_ref, near_ref, far_ref, last_ref, doc_bias_ref,
    slot_bias_ref, attend_gain_ref, feed_gain_ref, final_gain_ref,
    wq_any, wk_any, wv_any, wo_any, wg_any, wu_any, wd_any, wp_any,
    all_any, query_any, key_any, value_any, doc_probs_any, slot_probs_any, mixed_any, after_attend_any,
    normed_feed_any, hidden_any, gate_slope_any, up_slope_any, after_feed_any, normed_final_any, embed_any,
    slot_unit_any, doc_unit_any,
    all_ref, query_ref, key_ref, value_ref, doc_probs_ref, slot_probs_ref, mixed_ref, after_attend_ref,
    normed_feed_ref, hidden_ref, gate_slope_ref, up_slope_ref, after_feed_ref, normed_final_ref, embed_ref,
    slot_unit_ref, doc_unit_ref,
    wq_ref, wk_ref, wv_ref, wo_ref, wg_ref, wu_ref, wd_ref, wp_ref, slot_ref, load_sems, store_sems, slot_sem,
):
    slot_rows = slots * slot_length
    rows, width = query_ref.shape
    pairs = doc_probs_ref.shape[0]
    half = LANES // 2
    narrow_size = queries_ref.shape[0] // slots
    first = (rank_ref[0] & (narrow_size - 1)) * slots
    load_slots = pltpu.make_async_copy(queries_ref.at[pl.ds(first, slots)], slot_ref, slot_sem)
    load_slots.start()
    weights = loads(
        (wq_any, wk_any, wv_any, wo_any, wg_any, wu_any, wd_any, wp_any),
        (wq_ref, wk_ref, wv_ref, wo_ref, wg_ref, wu_ref, wd_ref, wp_ref),
        load_sems,
    )
    stores = loads(
        (all_ref, query_ref, key_ref, value_ref, doc_probs_ref, slot_probs_ref, mixed_ref, after_attend_ref,
         normed_feed_ref, hidden_ref, gate_slope_ref, up_slope_ref, after_feed_ref, normed_final_ref, embed_ref,
         slot_unit_ref, doc_unit_ref),
        (all_any, query_any, key_any, value_any, doc_probs_any, slot_probs_any, mixed_any, after_attend_any,
         normed_feed_any, hidden_any, gate_slope_any, up_slope_any, after_feed_any, normed_final_any, embed_any,
         slot_unit_any, doc_unit_any),
        store_sems,
    )
    for weight in weights[:3]:
        weight.start()
    gain = attend_gain_ref[...].reshape(1, width)
    place = slot_rows
    for ref in (own_ref, near_ref, far_ref, last_ref):
        tokens = ref[...].astype(f32)
        all_ref[place : place + ref.shape[0], :] = (tokens * rms_scale(tokens) * gain).astype(bf16)
        place += ref.shape[0]
    load_slots.wait()
    slot_tokens = slot_ref[...].reshape(slot_rows, width).astype(f32)
    all_ref[:slot_rows, :] = (slot_tokens * rms_scale(slot_tokens) * gain).astype(bf16)
    normed = all_ref[:rows, :]
    stores[0].start()
    weights[0].wait()
    for weight in weights[3:]:
        weight.start()
    query_ref[...] = product(normed, wq_ref[...]).astype(bf16)
    stores[1].start()
    weights[1].wait()
    key_ref[...] = product(all_ref[...], wk_ref[...]).astype(bf16)
    stores[2].start()
    weights[2].wait()
    value_ref[...] = product(all_ref[...], wv_ref[...]).astype(bf16)
    stores[3].start()

    lane = lax.broadcasted_iota(jnp.int32, (slot_rows, LANES), 1)
    row = lax.broadcasted_iota(jnp.int32, (slot_rows, slot_rows), 0)
    col = lax.broadcasted_iota(jnp.int32, (slot_rows, slot_rows), 1)
    slot_keep = row < 0
    for slot in range(slots):
        start = slot * slot_length
        inside = (row >= start) & (row < start + slot_length) & (col >= start)
        slot_keep = slot_keep | (inside & (col < start + lengths_ref[first + slot]))

    def softmax(scores):
        weights = jnp.exp(scores - jnp.max(scores, -1, keepdims=True))
        return (weights * (1.0 / jnp.sum(weights, -1, keepdims=True))).astype(bf16)

    first_lanes = lane < half
    pair_keep = jnp.concatenate([slot_keep, slot_keep], 0)

    def one_pair(pair, carry):
        lanes = tile(pair)
        slot_query = halves(query_ref[:slot_rows, lanes], first_lanes)
        scores = right_product(slot_query, key_ref[:slot_rows, lanes]) + slot_bias_ref[pair]
        probs = softmax(jnp.where(pair_keep, scores, masked_value))
        slot_probs_ref[pair] = probs
        slot_mixed = product(probs, value_ref[:slot_rows, lanes])
        mixed_ref[:slot_rows, lanes] = joined(slot_mixed, first_lanes).astype(bf16)
        doc_query = halves(query_ref[slot_rows:, lanes], first_lanes)
        scores = right_product(doc_query, key_ref[slot_rows:, lanes]) + doc_bias_ref[pair]
        probs = softmax(scores)
        doc_probs_ref[pair] = probs
        doc_mixed = product(probs, value_ref[slot_rows:, lanes])
        mixed_ref[slot_rows:, lanes] = joined(doc_mixed, first_lanes).astype(bf16)
        return carry

    lax.fori_loop(0, pairs, one_pair, 0)
    for store in stores[4:7]:
        store.start()

    weights[3].wait()
    attended = product(mixed_ref[...], wo_ref[...])
    after_attend_ref[:slot_rows, :] = slot_ref[...].reshape(slot_rows, width).astype(f32) + attended[:slot_rows]
    after_attend_ref[slot_rows:, :] = own_ref[...].astype(f32) + attended[slot_rows:]
    stores[7].start()
    after_attend = after_attend_ref[...]
    feed_gain = feed_gain_ref[...].reshape(1, width)
    normed_feed_ref[...] = (after_attend * rms_scale(after_attend) * feed_gain).astype(bf16)
    stores[8].start()
    weights[4].wait()
    weights[5].wait()

    def one_part(step, carry):
        part = tile(step, CHUNK)
        gate = product(normed_feed_ref[...], wg_ref[:, part])
        upward = product(normed_feed_ref[...], wu_ref[:, part])
        factor = 0.7978845608028654
        square = gate * gate
        bent = jnp.tanh(factor * gate * (1.0 + 0.044715 * square))
        curve = 0.5 * gate * (1.0 + bent)
        slope = 0.5 * (1.0 + bent) + 0.5 * factor * gate * (1.0 - bent * bent) * (1.0 + 3 * 0.044715 * square)
        hidden_ref[:, part] = (curve * upward).astype(bf16)
        gate_slope_ref[:, part] = (upward * slope).astype(bf16)
        up_slope_ref[:, part] = curve.astype(bf16)
        return carry

    lax.fori_loop(0, hidden_ref.shape[1] // CHUNK, one_part, 0)
    for store in stores[9:12]:
        store.start()
    weights[6].wait()
    after_feed = after_attend_ref[...] + product(hidden_ref[...], wd_ref[...])
    after_feed_ref[...] = after_feed
    stores[12].start()
    final_gain = final_gain_ref[...].reshape(1, width)
    normed_final = (after_feed * rms_scale(after_feed) * final_gain).astype(bf16)
    normed_final_ref[...] = normed_final
    stores[13].start()
    weights[7].wait()
    embed = product(normed_final, wp_ref[...])
    embed_ref[...] = embed
    unit = (embed * lax.rsqrt(jnp.sum(embed * embed, -1, keepdims=True) + epsilon)).astype(bf16)
    slot_unit_ref[...] = unit[:slot_rows]
    doc_unit_ref[...] = unit[slot_rows:]
    for store in stores[14:]:
        store.start()
    for store in stores:
        store.wait()


def loss_kernel(
    order, gathered, doc_total, slots, rank_ref, lengths_ref, positives_ref, counts_ref, near_ref, far_ref, unit_ref,
    tally_ref, losses_ref, grad_ref, kept_ref, sent_ref, sum_ref, scaled_ref,
):
    rows = unit_ref.shape[0]
    blocks = counts_ref.shape[0]
    per_doc = blocks // doc_total
    rank = rank_ref[0]
    half = blocks // 2
    sum_ref[...] = jnp.zeros_like(sum_ref)

    def gather_step(place, carry):
        near = rank ^ gather_order(place, gathered)
        far = near ^ (1 << gathered[-1])
        sum_ref[near // per_doc] += product(counts_ref[near], near_ref[place])
        sum_ref[far // per_doc] += product(counts_ref[far], far_ref[place])
        return carry

    lax.fori_loop(0, half, gather_step, 0, unroll=4)

    unit = unit_ref[...].astype(f32)
    lane = lax.broadcasted_iota(jnp.int32, (rows, LANES), 1)
    summed = jnp.zeros((rows, LANES), f32)
    for doc in range(doc_total):
        number = jnp.sum(sum_ref[doc] * unit, 1, keepdims=True)
        summed = jnp.where(lane == doc, number, summed)
    tally = tally_ref[...]
    most = jnp.maximum(tally, 1.0)
    slot_length = rows // slots
    narrow_size = lengths_ref.shape[0] // slots
    first = (rank & (narrow_size - 1)) * slots
    row = lax.broadcasted_iota(jnp.int32, (rows, LANES), 0)
    slot_row = lax.broadcasted_iota(jnp.int32, (slots, LANES), 0)
    valid = row < 0
    positive = jnp.zeros((slots, LANES), jnp.int32)
    for slot in range(slots):
        start = slot * slot_length
        valid = valid | ((row >= start) & (row < start + lengths_ref[first + slot]))
        positive = jnp.where(slot_row == slot, positives_ref[first + slot], positive)
    weight = jnp.where(valid, jnp.minimum(tally, 1.0), 0.0)
    pooled = (weight * (summed / most)).reshape(slots, slot_length, LANES)
    weight_sum = jnp.maximum(jnp.sum(weight.reshape(slots, slot_length, LANES), 1), 1.0)
    scores = jnp.sum(pooled, 1) / weight_sum / contrastive_sharpness_factor
    slot_lane = lax.broadcasted_iota(jnp.int32, (slots, LANES), 1)
    inside = slot_lane < doc_total
    scores = jnp.where(inside, scores, -jnp.inf)
    top = jnp.max(scores, -1, keepdims=True)
    powers = jnp.exp(scores - top)
    total = jnp.sum(powers, -1, keepdims=True)
    chosen = (slot_lane == positive).astype(f32)
    picked = jnp.sum(jnp.where(slot_lane == positive, scores, 0.0), -1, keepdims=True)
    losses_ref[...] = jnp.broadcast_to(top + jnp.log(total) - picked, (slots, LANES))
    slope = (powers / total - chosen) / contrastive_sharpness_factor / weight_sum
    slope = jnp.where(inside, slope, 0.0)
    slope = jnp.broadcast_to(slope[:, None, :], (slots, slot_length, LANES)).reshape(rows, LANES)
    slope = slope * weight / most

    grad = jnp.zeros((rows, unit.shape[1]), f32)
    for doc in range(doc_total):
        column = jnp.sum(jnp.where(lane == doc, slope, 0.0), 1, keepdims=True)
        grad = grad + column * sum_ref[doc]
        scaled_ref[doc] = (column * unit).T.astype(bf16)
    grad_ref[...] = grad

    def scatter_step(place, carry):
        kept = rank ^ scatter_order(place, order)
        sent = kept ^ (1 << order[0])
        kept_ref[place] = product(scaled_ref[kept // per_doc], counts_ref[kept]).astype(bf16)
        sent_ref[place] = product(scaled_ref[sent // per_doc], counts_ref[sent]).astype(bf16)
        return carry

    lax.fori_loop(0, half, scatter_step, 0, unroll=4)


def feed_back(
    part, waits, grad_unit, embed_ref, after_feed_ref, after_attend_ref, gate_slope_ref, up_slope_ref, feed_gain_ref,
    final_gain_ref, wo_ref, wg_ref, wu_ref, wd_ref, wp_ref, grads_out, after_out, mixed_out, more_ref,
):
    units, width = wd_ref.shape
    up_start, feed_start = units, 2 * units
    attend_start, embed_start = 2 * units + width, 2 * units + 2 * width
    embed = embed_ref[part, :]
    scale = lax.rsqrt(jnp.sum(embed * embed, -1, keepdims=True) + epsilon)
    inner = jnp.sum(grad_unit * embed, -1, keepdims=True)
    grad_embed = (scale * grad_unit - embed * (scale * scale * scale * inner)).astype(bf16)
    grads_out[:, embed_start : embed_start + embed.shape[1]] = grad_embed
    waits[0].wait()
    grad_after_feed = rms_back(
        after_feed_ref[part, :], final_gain_ref[...].reshape(1, -1), right_product(grad_embed, wp_ref[...])
    )
    after_out[...] = grad_after_feed
    grad_feed = grad_after_feed.astype(bf16)
    grads_out[:, feed_start:attend_start] = grad_feed
    for wait in waits[1:4]:
        wait.wait()

    def one_part(step, total):
        cols = tile(step, CHUNK)
        grad_hidden = right_product(grads_out[:, feed_start:attend_start], wd_ref[cols, :])
        grad_gate = (grad_hidden * gate_slope_ref[part, cols].astype(f32)).astype(bf16)
        grad_up = (grad_hidden * up_slope_ref[part, cols].astype(f32)).astype(bf16)
        grads_out[:, cols] = grad_gate
        grads_out[:, pl.ds(pl.multiple_of(up_start + step * CHUNK, CHUNK), CHUNK)] = grad_up
        more_ref[...] += right_product(grad_gate, wg_ref[:, cols]) + right_product(grad_up, wu_ref[:, cols])
        return total

    more_ref[...] = jnp.zeros_like(more_ref)
    lax.fori_loop(0, units // CHUNK, one_part, 0)
    total = more_ref[...]
    more = rms_back(after_attend_ref[part, :], feed_gain_ref[...].reshape(1, -1), total)
    grad_after_attend = after_out[...] + more
    after_out[...] = grad_after_attend
    grad_attend = grad_after_attend.astype(bf16)
    grads_out[:, attend_start:embed_start] = grad_attend
    waits[4].wait()
    mixed_out[...] = right_product(grad_attend, wo_ref[...]).astype(bf16)


def attend_back(
    far_parts, queries, keys, query_ref, key_ref, value_ref, probs_ref, mixed_ref, query_out, key_out, value_out,
    sums_out,
):
    rows = mixed_ref.shape[0]
    length = probs_ref.shape[2]
    half = LANES // 2
    first_lanes = lax.broadcasted_iota(jnp.int32, (rows, LANES), 1) < half
    row = lax.broadcasted_iota(jnp.int32, (rows, rows), 0)
    col = lax.broadcasted_iota(jnp.int32, (rows, rows), 1)
    flip = (row + col == rows - 1).astype(bf16)
    nothing = jnp.zeros((rows, LANES), f32)

    def one_pair(pair, carry):
        lanes = tile(pair)
        grad_mixed = halves(mixed_ref[:, lanes], first_lanes)
        query = halves(query_ref[queries, lanes], first_lanes)
        probs = probs_ref[pair]
        grad_probs = right_product(grad_mixed, value_ref[keys, lanes])
        exact = probs.astype(f32)
        inner = jnp.sum(exact * grad_probs, -1, keepdims=True)
        grad_scores = (exact * (grad_probs - inner)).astype(bf16)
        query_out(joined(product(grad_scores, key_ref[keys, lanes]), first_lanes).astype(bf16), pair)
        key_out(left_product(grad_scores, query).astype(bf16), pair)
        value_out(left_product(probs, grad_mixed).astype(bf16), pair)
        for side in range(2):
            head = 2 * pair + side
            own = grad_scores[side * rows : (side + 1) * rows, :]
            for part in range(length // LANES):
                piece = own[:, part * LANES : (part + 1) * LANES]
                if part in far_parts:
                    line = jnp.concatenate([piece.astype(f32), nothing], 1)
                else:
                    line = pltpu.roll(
                        jnp.concatenate([product(flip, piece), nothing], 1), 0, 1, stride=1, stride_axis=0
                    )
                sums_out[tile(head, 8), part * 2 * LANES : (part + 1) * 2 * LANES] = jnp.sum(
                    line.reshape(rows // 8, 8, 2 * LANES), 0
                )
        return carry

    lax.fori_loop(0, probs_ref.shape[0], one_pair, 0)


def input_back(tokens, gain_ref, after_ref, query, key, value, wq_ref, wk_ref, wv_ref):
    grad_normed = right_product(query, wq_ref[...])
    grad_normed = grad_normed + right_product(key, wk_ref[...])
    grad_normed = grad_normed + right_product(value, wv_ref[...])
    return after_ref[...] + rms_back(tokens, gain_ref[...].reshape(1, -1), grad_normed)


def table_sums(sums_ref, distances):
    heads = sums_ref.shape[0] // 8
    span = lax.broadcasted_iota(jnp.int32, (2 * LANES, LANES), 0) - (LANES - 1)
    bucket = lax.broadcasted_iota(jnp.int32, (2 * LANES, LANES), 1)
    total = jnp.zeros((heads, LANES), f32)
    for part, distance in enumerate(distances):
        lines = jnp.sum(sums_ref[:, part * 2 * LANES : (part + 1) * 2 * LANES].reshape(heads, 8, 2 * LANES), 1)
        hot = (bucket_index(span + distance * LANES) == bucket).astype(f32)
        total = total + lax.dot_general(
            lines, hot, (((1,), (0,)), ((), ())), precision=highest, preferred_element_type=f32
        )
    return total


def slot_feed_kernel(
    grad_unit_ref, embed_ref, after_feed_ref, after_attend_ref, gate_slope_ref, up_slope_ref, feed_gain_ref,
    final_gain_ref, wp_any, wd_any, wg_any, wu_any, wo_any,
    grads_out, after_out, mixed_out,
    wp_ref, wd_ref, wg_ref, wu_ref, wo_ref, more_ref, load_sems,
):
    weights = loads(
        (wp_any, wd_any, wg_any, wu_any, wo_any), (wp_ref, wd_ref, wg_ref, wu_ref, wo_ref), load_sems
    )
    for weight in weights:
        weight.start()
    feed_back(
        slice(0, after_out.shape[0]), weights, grad_unit_ref[...], embed_ref, after_feed_ref, after_attend_ref,
        gate_slope_ref, up_slope_ref, feed_gain_ref, final_gain_ref, wo_ref, wg_ref, wu_ref, wd_ref, wp_ref, grads_out,
        after_out, mixed_out, more_ref,
    )


def slot_attend_kernel(
    query_ref, key_ref, value_ref, probs_ref, mixed_ref, grads_out, table_out, sums_ref
):
    rows, width = mixed_ref.shape

    def out(place):
        def store(values, pair):
            grads_out[:, pl.ds(pl.multiple_of(place * width + pair * LANES, LANES), LANES)] = values

        return store

    part = slice(0, rows)
    attend_back(
        (), part, part, query_ref, key_ref, value_ref, probs_ref, mixed_ref, out(0), out(1), out(2), sums_ref
    )
    table_out[...] = table_sums(sums_ref, [0])


def doc_feed_kernel(came, *refs):
    parts, refs = refs[:came], refs[came:]
    (
        embed_ref, after_feed_ref, after_attend_ref, gate_slope_ref, up_slope_ref, feed_gain_ref, final_gain_ref,
        wp_any, wd_any, wg_any, wu_any, wo_any,
        grads_out, after_out, mixed_out,
        wp_ref, wd_ref, wg_ref, wu_ref, wo_ref, more_ref, load_sems,
    ) = refs
    weights = loads(
        (wp_any, wd_any, wg_any, wu_any, wo_any), (wp_ref, wd_ref, wg_ref, wu_ref, wo_ref), load_sems
    )
    for weight in weights:
        weight.start()
    rows = after_out.shape[0]
    grad_unit = add(*(part[0] for part in parts)).T
    feed_back(
        slice(embed_ref.shape[0] - rows, embed_ref.shape[0]), weights, grad_unit, embed_ref, after_feed_ref,
        after_attend_ref, gate_slope_ref, up_slope_ref, feed_gain_ref, final_gain_ref, wo_ref, wg_ref, wu_ref, wd_ref,
        wp_ref, grads_out, after_out, mixed_out, more_ref,
    )


def doc_attend_kernel(
    rank_ref, query_ref, key_ref, value_ref, probs_ref, mixed_ref, slot_table_ref, grads_out, table_out, query_room,
    sums_ref,
):
    rows, width = query_room.shape
    length = probs_ref.shape[2]
    first = key_ref.shape[0] - length

    def query_out(values, pair):
        query_room[:, tile(pair)] = values

    def key_out(values, pair):
        grads_out[:length, tile(pair)] = values

    def value_out(values, pair):
        grads_out[:length, pl.ds(pl.multiple_of(width + pair * LANES, LANES), LANES)] = values

    attend_back(
        (2,), slice(first, first + rows), slice(first, key_ref.shape[0]), query_ref, key_ref, value_ref, probs_ref,
        mixed_ref, query_out, key_out, value_out, sums_ref,
    )
    grads_out[length:, :width] = query_room[: rows // 2, :]
    grads_out[length:, width:] = query_room[rows // 2 :, :]
    parts = length // LANES
    narrow = rank_ref[0] & (parts - 1)
    table = table_sums(sums_ref, [(narrow ^ part) - narrow for part in range(parts)]) + slot_table_ref[...]
    heads = table.shape[0]
    table_out[...] = jnp.concatenate([table, jnp.zeros((16 - heads, LANES), f32)], 0).astype(bf16)


def pick_columns(values, total, order, flipped, rank):
    count = 1 << len(order) + 1
    size = total // count
    row = lax.broadcasted_iota(jnp.int32, (total, total // 2), 0)
    col = lax.broadcasted_iota(jnp.int32, (total, total // 2), 1)
    source = (scatter_order(col // size, order) ^ rank ^ flipped) * size + col % size
    return product(values, (row == source).astype(bf16)).astype(bf16)


def pick_tiles(values_ref, order, flipped, rank, store):
    rows = values_ref.shape[0]
    half = LANES // 2
    first_lanes = lax.broadcasted_iota(jnp.int32, (rows, LANES), 1) < half
    upper = ((rank ^ flipped) & 1) == 1

    def one_tile(step, carry):
        place = 2 * step
        sides = []
        for side in range(2):
            tile = (rank ^ scatter_order(place + side, order)) >> 1
            values = values_ref[:, pl.ds(pl.multiple_of(tile * LANES, LANES), LANES)].astype(f32)
            turned = pltpu.roll(values, half, 1)
            sides.append(jnp.where(upper, turned, values) if side == 0 else jnp.where(upper, values, turned))
        store(step, jnp.where(first_lanes, sides[0], sides[1]).astype(bf16))
        return carry

    lax.fori_loop(0, 1 << len(order) - 1, one_tile, 0)


def turn_kernel(
    orders, rank_ref, all_ref, normed_feed_ref, mixed_ref, normed_final_ref, hidden_ref, kept_out, sent_out, doc_out,
):
    first, second, third, fourth = orders
    rank = rank_ref[0]
    rows, width = normed_feed_ref.shape
    units = hidden_ref.shape[1]
    slots = all_ref.shape[0] - doc_out.shape[0]
    half = width // 2
    for out, flipped in ((kept_out, 0), (sent_out, 1)):
        out[:, :half] = pick_columns(normed_feed_ref[...], width, first, flipped, rank)
        out[:, half : 2 * half] = pick_columns(normed_feed_ref[...], width, second, flipped, rank)
        out[:, 2 * half : 3 * half] = pick_columns(mixed_ref[...], width, first, flipped, rank)
        out[:, 3 * half : 4 * half] = pick_columns(normed_final_ref[...], width, second, flipped, rank)
        start = 4 * half
        if units >> (len(third) + 1) == LANES // 2:

            def store(place, values):
                out[:, pl.ds(pl.multiple_of(start + place * LANES, LANES), LANES)] = values

            pick_tiles(hidden_ref, third, flipped, rank, store)
        else:
            out[:, start : start + units // 2] = pick_columns(hidden_ref[...], units, third, flipped, rank)
        start = start + units // 2
        out[slots:, start:] = jnp.zeros((rows - slots, half), bf16)
        if flipped:
            out[:slots, start:] = pick_columns(all_ref[:slots, :], width, fourth, flipped, rank)
        else:
            both = pick_columns(all_ref[...], width, fourth, flipped, rank)
            out[:slots, start:] = both[:slots]
            doc_out[...] = both[slots:]


def store_product(left, right_ref, columns, kept_ref, sent_ref, start):
    half = left.shape[1] // 2
    size = 2 * LANES

    def one_part(first, size):
        here = pl.ds(pl.multiple_of(start + first, LANES), size)
        result = left_product(left, right_ref[:, pl.ds(pl.multiple_of(first, LANES), size)]).astype(bf16)
        kept_ref[:half, here] = result[:half]
        sent_ref[:half, here] = result[half:]

    def step(place, carry):
        one_part(place * size, size)
        return carry

    lax.fori_loop(0, columns // size, step, 0)
    if columns % size:
        one_part(columns // size * size, columns % size)


def weight_kernel(
    terms, kept_any, came_any, slot_any, slot_came_any, doc_any, doc_came_any, kept_ref, sent_ref, left_ref, right_ref,
    sems,
):
    rows = kept_any.shape[0]
    part = slot_any.shape[0]
    copies = []
    left_place, right_place = 0, 0
    for left_start, left_width, right_start, right_width in terms:
        pieces = []
        for place, ref in enumerate((kept_any, came_any)):
            source = ref.at[:, left_start : left_start + left_width]
            target = left_ref.at[place * rows : (place + 1) * rows, left_place : left_place + left_width]
            pieces.append((source, target))
        for place, ref in enumerate((slot_any, doc_any, slot_came_any, doc_came_any)):
            source = ref.at[:, right_start : right_start + right_width]
            target = right_ref.at[place * part : (place + 1) * part, right_place : right_place + right_width]
            pieces.append((source, target))
        first = sum(len(group) for group in copies)
        copies.append(
            [pltpu.make_async_copy(one, two, sems.at[first + i]) for i, (one, two) in enumerate(pieces)]
        )
        left_place += left_width
        right_place += right_width
    for group in copies:
        for copy in group:
            copy.start()
    left_place, right_place = 0, 0
    for group, (_, left_width, _, right_width) in zip(copies, terms):
        for copy in group:
            copy.wait()
        left = left_ref[:, left_place : left_place + left_width]
        right = right_ref.at[:, right_place : right_place + right_width]
        store_product(left, right, right_width, kept_ref, sent_ref, right_place)
        left_place += left_width
        right_place += right_width


def attend_weight_kernel(
    doc_ref, kept_any, came_any, slot_any, slot_came_any, grads_ref, other_ref, table_ref, other_table_ref,
    kept_out, sent_out, pair_kept, pair_sent, slot_room, slot_came_room, left_ref, right_ref, query_ref, sems,
):
    rows = slot_any.shape[0]
    width = slot_room.shape[1] // 3
    half = doc_ref.shape[1]
    length = doc_ref.shape[0]
    lanes = slice(kept_any.shape[1] - half, kept_any.shape[1])
    copies = loads(
        (slot_any, slot_came_any, kept_any.at[:rows, lanes], came_any.at[:rows, lanes]),
        (slot_room, slot_came_room, left_ref.at[length : length + rows, :], left_ref.at[length + rows :, :]),
        sems,
    )
    for copy in copies:
        copy.start()
    left_ref[:length, :] = doc_ref[...]
    for part in range(length // LANES):
        here = slice(part * LANES, (part + 1) * LANES)
        there = slice((part ^ 1) * LANES, ((part ^ 1) + 1) * LANES)
        right_ref[here, :] = add(grads_ref[here, :], other_ref[there, :]).astype(bf16)
    pair_kept[...] = right_ref[:LANES, :]
    pair_sent[...] = right_ref[2 * LANES : 3 * LANES, :]
    small = LANES // 2
    for place, ref in enumerate((grads_ref, other_ref)):
        query_ref[2 * place * small : (2 * place + 1) * small, :] = ref[length:, :width]
        query_ref[(2 * place + 1) * small : (2 * place + 2) * small, :] = ref[length:, width:]
    for copy in copies:
        copy.wait()
    right_ref[length : length + rows, :] = slot_room[:, width:]
    right_ref[length + rows :, :] = slot_came_room[:, width:]
    query_ref[2 * LANES : 2 * LANES + rows, :] = slot_room[:, :width]
    query_ref[2 * LANES + rows :, :] = slot_came_room[:, :width]
    store_product(left_ref[...], right_ref, 2 * width, kept_out, sent_out, width)
    left = jnp.concatenate([left_ref[: 2 * LANES, :], left_ref[length:, :]], 0)
    store_product(left, query_ref, width, kept_out, sent_out, 0)
    tail = sent_out.shape[0] - 16
    sent_out[tail:, :] = jnp.zeros((16, sent_out.shape[1]), bf16)
    sent_out[tail:, :LANES] = add(table_ref[...], other_table_ref[...]).astype(bf16)


def input_kernel(
    slots, rank_ref, tokens_ref, gain_ref, after_ref, grads_ref, kept_ref, came_ref, queries_any, slot_after_ref,
    slot_grads_ref, wq_ref, wk_ref, wv_ref, tokens_out, queries_out, slot_room, sem,
):
    narrow_size = queries_any.shape[0] // slots
    first = (rank_ref[0] & (narrow_size - 1)) * slots
    load = pltpu.make_async_copy(queries_any.at[pl.ds(first, slots)], slot_room, sem)
    load.start()
    rows, width = tokens_ref.shape
    rest = grads_ref.shape[0] - rows // 2
    query = jnp.concatenate([grads_ref[rest:, :width], grads_ref[rest:, width:]], 0)
    pair = add(kept_ref[...], came_ref[...]).astype(bf16)
    tokens_out[...] = input_back(
        tokens_ref[...].astype(f32), gain_ref, after_ref, query, pair[:, :width], pair[:, width:], wq_ref, wk_ref, wv_ref
    )
    load.wait()
    query, key, value = (slot_grads_ref[:, place * width : (place + 1) * width] for place in range(3))
    queries_out[...] = input_back(
        slot_room[...].reshape(queries_out.shape).astype(f32), gain_ref, slot_after_ref, query, key, value, wq_ref,
        wk_ref, wv_ref,
    )


def on_device(
    doc_tokens, query_tokens, query_lengths, positive_docs, retrieved, attend_gain, query_weight, key_weight,
    value_weight, output_weight, bias_table, feed_gain, gate_weight, up_weight, down_weight, final_gain, proj_weight,
):
    narrow_size = lax.axis_size("narrow")
    bits = rank_bits()
    rank = my_rank()
    rank_word = rank.astype(jnp.int32).reshape(1)
    doc_rows, width = doc_tokens.shape[1:]
    doc_length = doc_rows * narrow_size
    doc_total = doc_tokens.shape[0] * lax.axis_size("wide")
    slots = query_tokens.shape[0] // narrow_size
    slot_length = query_tokens.shape[1]
    heads = bias_table.shape[1]
    units = gate_weight.shape[1]
    columns = proj_weight.shape[1]
    slot_rows = slots * slot_length
    rows = slot_rows + doc_rows
    blocks = doc_total * doc_length // LANES
    assert doc_tokens.shape[0] == 1 and doc_rows == LANES and slot_rows == LANES and narrow_size == 4
    assert columns == LANES and doc_total <= LANES and blocks == 1 << bits
    gains = (attend_gain, feed_gain, final_gain)
    dma = pltpu.SemaphoreType.DMA
    waxes = list(range(3, bits))

    orders = ([1, 2] + waxes, waxes[:1] + [1, 2] + waxes[1:], [1] + waxes[:1] + [2] + waxes[1:], [2] + waxes[:1] + [1] + waxes[1:])
    own_tokens = doc_tokens[0]
    y_tokens = swap(own_tokens, 2)
    core_tokens = swap(own_tokens, 1)
    pairs = heads // 2
    doc_bias, slot_bias = call(
        functools.partial(bias_kernel, doc_length),
        [shape((pairs, 2 * doc_rows, doc_length)), shape((pairs, 2 * slot_rows, slot_rows))],
        [rank_word, bias_table],
        "s",
        [pltpu.VMEM((heads, 2 * doc_length + LANES), f32)],
    )
    y_tokens = after(y_tokens, doc_bias)
    both_tokens = swap(y_tokens, 1)

    all_rows = slot_rows + doc_length
    forward_shapes = [
        shape((all_rows, width), bf16),
        shape((rows, width), bf16),
        shape((all_rows, width), bf16),
        shape((all_rows, width), bf16),
        shape((pairs, 2 * doc_rows, doc_length), bf16),
        shape((pairs, 2 * slot_rows, slot_rows), bf16),
        shape((rows, width), bf16),
        shape((rows, width)),
        shape((rows, width), bf16),
        shape((rows, units), bf16),
        shape((rows, units), bf16),
        shape((rows, units), bf16),
        shape((rows, width)),
        shape((rows, width), bf16),
        shape((rows, columns)),
        shape((slot_rows, columns), bf16),
        shape((doc_rows, columns), bf16),
    ]
    weights = [
        query_weight, key_weight, value_weight, output_weight, gate_weight, up_weight, down_weight, proj_weight,
    ]
    slot_room = pltpu.VMEM((slots, slot_length, width), bf16)
    (
        all_normed, query, key, value, doc_probs, slot_probs, mixed, after_attend, normed_feed, hidden, gate_slope,
        up_slope, after_feed, normed_final, embed, slot_unit, doc_unit,
    ) = call(
        functools.partial(forward_kernel, slots, slot_length),
        forward_shapes,
        [
            rank_word, query_lengths, query_tokens, own_tokens, core_tokens, y_tokens, both_tokens, doc_bias, slot_bias,
            *gains, *weights,
        ],
        "ssa" + "v" * 9 + "h" * 8 + "a" * len(forward_shapes),
        [room(value) for value in forward_shapes]
        + [room(weight) for weight in weights]
        + [slot_room, dma((8,)), dma((len(forward_shapes),)), dma],
        vmem=VM[0],
        us=18,
    )

    phases = [list(range(high, max(high - 2, 0), -1)) for high in range(bits - 1, 0, -2)]
    gathered = []
    near_units = doc_unit[None]
    for phase, group in enumerate(phases):
        group = group[::-1]
        masks = [gather_order(place, group) for place in range(1, 1 << len(group))]
        came = [swap(near_units, mask) for mask in masks]
        if phase == 0:
            counts, tally = call(
                functools.partial(count_kernel, doc_length, doc_total),
                [shape((blocks, slot_rows, LANES), bf16), shape((slot_rows, LANES))],
                after([rank_word, retrieved], doc_unit),
                "sa",
                [
                    pltpu.VMEM((slots, slot_length, retrieved.shape[2]), jnp.int32),
                    pltpu.VMEM((slot_rows, retrieved.shape[2]), jnp.int32),
                    pltpu.VMEM((blocks * slot_rows, LANES), f32),
                    dma,
                ],
                us=5,
                wide=bits > 5,
            )
            came = after(came, tally)
        if phase == 1:
            turned_cols = 5 * width // 2 + units // 2
            turned, turned_sent, turned_docs = call(
                functools.partial(turn_kernel, orders),
                [shape((rows, turned_cols), bf16)] * 2 + [shape((doc_length, width // 2), bf16)],
                after([rank_word, all_normed, normed_feed, mixed, normed_final, hidden], near_units),
                "s",
                us=5,
                wide=bits > 5,
            )
            came = after(came, turned)
        near_units = jnp.concatenate([near_units] + came, 0)
        gathered = gathered + group
    gathered = gathered + [0]
    far_units = swap(near_units, 1)

    order = list(range(bits))
    half = blocks // 2
    losses, grad_slot_unit, kept, sent = call(
        functools.partial(loss_kernel, order, gathered, doc_total, slots),
        [
            shape((slots, LANES)),
            shape((slot_rows, columns)),
            shape((half, columns, LANES), bf16),
            shape((half, columns, LANES), bf16),
        ],
        [rank_word, query_lengths, positive_docs, counts, near_units, far_units, slot_unit, tally],
        "sss",
        [
            pltpu.VMEM((doc_total, slot_rows, columns), f32),
            pltpu.VMEM((doc_total, columns, slot_rows), bf16),
        ],
        wide=bits > 5,
    )
    turned_came = swap(after(turned_sent, losses), 1)
    back_weights = [proj_weight, down_weight, gate_weight, up_weight, output_weight]
    doc_cols = 2 * units + 2 * width + columns

    came = [swap(sent, 1)]
    rest = order[1:]
    parts = [kept]
    phase = 0
    feed_shapes = [shape((LANES, doc_cols), bf16), shape((LANES, width)), shape((LANES, width), bf16)]
    while rest:
        group, rest = rest[:2], rest[2:]
        count = 1 << len(group)
        size = parts[0].shape[0] // count
        pieces = []
        for place in range(count):
            here = slice(place * size, (place + 1) * size)
            pieces.append(add(*(part[here] for part in parts), *(one[here] for one in came)).astype(bf16))
        masks = [scatter_order(place, group) for place in range(count)]
        came = [swap(piece, mask) for piece, mask in zip(pieces[1:], masks[1:])]
        parts = [pieces[0]]
        if phase == 0:
            slot_grads, slot_after, slot_mixed = call(
                slot_feed_kernel,
                feed_shapes,
                [after(grad_slot_unit, pieces[1], turned_came)]
                + [embed, after_feed, after_attend, gate_slope, up_slope, gains[1], gains[2]]
                + back_weights,
                "v" * 8 + "a" * 5,
                [room(weight) for weight in back_weights] + [pltpu.VMEM((slot_rows, width), f32), dma((5,))],
                vmem=VM[1],
                us=7,
            )
            came = after(came, slot_after)
        if phase == 1:
            slot_came = swap(after(slot_grads, *pieces[1:]), 1)
            slot_thirds, slot_table = call(
                slot_attend_kernel,
                [shape((slot_rows, 3 * width), bf16), shape((heads, LANES))],
                [query, key, value, slot_probs, after(slot_mixed, *pieces[1:])],
                scratch=[pltpu.VMEM((heads * 8, 2 * LANES), f32)],
                us=4,
            )
            came = after(came, slot_table)
        phase += 1

    doc_grads, doc_after, doc_mixed = call(
        functools.partial(doc_feed_kernel, 1 + len(came)),
        feed_shapes,
        parts + after(came, slot_came)
        + [embed, after_feed, after_attend, gate_slope, up_slope, gains[1], gains[2]]
        + back_weights,
        "v" * (8 + len(came)) + "a" * 5,
        [room(weight) for weight in back_weights] + [pltpu.VMEM((doc_rows, width), f32), dma((5,))],
        vmem=VM[2],
        us=7,
    )
    thirds_came = swap(after(slot_thirds, doc_after), 1)
    doc_came = swap(doc_grads, 1)

    class Stream:
        def __init__(self, kept, sent, order):
            self.kept, self.order, self.step = kept, order, 0
            self.loaded = sent.shape[0] > kept.shape[0]
            self.small = sent[-16:] if self.loaded else None
            self.send(sent)

        def send(self, sent):
            self.came = swap(sent, 1 << self.order[self.step])
            self.step += 1

        def advance(self, *wait):
            came = after(self.came, *wait)
            if self.step == len(self.order):
                if self.loaded:
                    self.small = add(self.small, came[-16:]).astype(bf16)
                    came = came[:-16]
                self.result = add(self.kept, came)
                return self.result
            self.kept, sent, self.small = cut(self.kept, came, self.small)
            self.send(sent)
            return self.kept

    def weight_product(terms, order, *wait):
        left = sum(term[1] for term in terms)
        right = sum(term[3] for term in terms)
        tall = terms[0][1] // 2
        args = after([turned, turned_came, slot_grads, slot_came, doc_grads, doc_came], *wait)
        kept, sent = call(
            functools.partial(weight_kernel, terms),
            [shape((tall, right), bf16)] * 2,
            args,
            "a" * 6,
            [pltpu.VMEM((2 * rows, left), bf16), pltpu.VMEM((2 * rows, right), bf16), dma((6 * len(terms),))],
        )
        return Stream(kept, sent, order)

    small_half = width // 2
    att_grads, table = call(
        doc_attend_kernel,
        [shape((doc_length + doc_rows // 2, 2 * width), bf16), shape((16, LANES), bf16)],
        [rank_word, query, key, value, doc_probs, doc_mixed, slot_table],
        "s",
        [pltpu.VMEM((doc_rows, width), bf16), pltpu.VMEM((heads * 8, 2 * doc_length), f32)],
    )
    att_came, table_came = swap(att_grads, 1), swap(table, 1)
    first = weight_product(
        [(0, small_half, 0, units), (2 * small_half, small_half, 2 * units + width, width)], orders[0], table
    )
    fourth_kept, fourth_sent, pair_kept, pair_sent = call(
        attend_weight_kernel,
        [
            shape((width // 4, 3 * width), bf16),
            shape((width // 4 + 16, 3 * width), bf16),
            shape((doc_rows, 2 * width), bf16),
            shape((doc_rows, 2 * width), bf16),
        ],
        [turned_docs, turned, turned_came, slot_thirds, thirds_came, att_grads, att_came, after(table, first.kept), table_came],
        "vaaaa",
        [
            pltpu.VMEM((slot_rows, 3 * width), bf16),
            pltpu.VMEM((slot_rows, 3 * width), bf16),
            pltpu.VMEM((doc_length + 2 * slot_rows, width // 2), bf16),
            pltpu.VMEM((doc_length + 2 * slot_rows, 2 * width), bf16),
            pltpu.VMEM((2 * doc_rows + 2 * slot_rows, width), bf16),
            dma((4,)),
        ],
    )
    fourth = Stream(fourth_kept, fourth_sent, orders[3])
    second = weight_product(
        [(small_half, small_half, units, units), (3 * small_half, small_half, 2 * units + 2 * width, columns)],
        orders[1],
        fourth_kept,
    )
    third = weight_product([(4 * small_half, units // 2, 2 * units, width)], orders[2], second.kept)
    done = third.kept
    for step in range(bits - 1):
        for stream in (first, fourth, second, third):
            done = stream.advance(done)
        if step == 0:
            pair_came = swap(after(pair_sent, done), 2)
        if step == 2:
            doc_grad, query_grad = call(
                functools.partial(input_kernel, slots),
                [shape((doc_rows, width)), shape((slot_rows, width))],
                [rank_word, own_tokens, gains[0], doc_after, att_grads, pair_kept, after(pair_came, done)]
                + [query_tokens, slot_after, slot_thirds, query_weight, key_weight, value_weight],
                "s" + "v" * 6 + "a",
                [slot_room, dma],
                us=4,
            )
            done = doc_grad

    def own_rows(values):
        return lax.dynamic_slice_in_dim(values, rank * (width >> bits), width >> bits, 0).astype(f32)

    def gain_grad(gain, *pairs):
        return sum(jnp.sum(own_rows(weight) * grad, 1) for weight, grad in pairs) / own_rows(gain)

    gate_grad, output_grad = first.result[:, :units], first.result[:, units:]
    up_grad, proj_grad = second.result[:, :units], second.result[:, units:]
    query_g, key_g, value_g = (fourth.result[:, place * width : (place + 1) * width] for place in range(3))
    return (
        losses[:, 0],
        doc_grad[None],
        query_grad.reshape(slots, slot_length, width),
        gain_grad(attend_gain, (query_weight, query_g), (key_weight, key_g), (value_weight, value_g)),
        query_g,
        key_g,
        value_g,
        output_grad,
        fourth.small[:heads, :BUCKETS].astype(f32).T,
        gain_grad(feed_gain, (gate_weight, gate_grad), (up_weight, up_grad)),
        gate_grad,
        up_grad,
        third.result,
        gain_grad(final_gain, (proj_weight, proj_grad)),
        proj_grad,
    )


def solution(mesh):
    return jax.shard_map(
        on_device,
        mesh=mesh,
        in_specs=(
            P("wide", "narrow", None),
            P("wide", None, None),
            P("wide"),
            P("wide"),
            P("wide", None, None),
            P(),
            P(),
            P(),
            P(),
            P(),
            P(),
            P(),
            P(),
            P(),
            P(),
            P(),
            P(),
        ),
        out_specs=(
            P(("wide", "narrow")),
            P("wide", "narrow", None),
            P(("wide", "narrow"), None, None),
            P(("wide", "narrow")),
            P(("wide", "narrow"), None),
            P(("wide", "narrow"), None),
            P(("wide", "narrow"), None),
            P(("wide", "narrow"), None),
            P(),
            P(("wide", "narrow")),
            P(("wide", "narrow"), None),
            P(("wide", "narrow"), None),
            P(("wide", "narrow"), None),
            P(("wide", "narrow")),
            P(("wide", "narrow"), None),
        ),
        check_vma=False,
    )
```

```python
import functools

import jax
import jax.numpy as jnp
from jax import lax
from jax.experimental import pallas as pl
from jax.experimental.pallas import tpu as pltpu
from jax.sharding import PartitionSpec as P

BUCKETS = 32
LANES = 128
CHUNK = 512
VM = (12, 12, 12, 16, 8)
COST = 1.1e9

epsilon = 1e-06
contrastive_sharpness_factor = 0.01
masked_value = -1000000000.0
bucket_edges = (12, 16, 23, 32, 46, 64, 91)
highest = lax.Precision.HIGHEST
f32 = jnp.float32
bf16 = jnp.bfloat16


def bucket_index(offset):
    distance = jnp.abs(offset)
    beyond = 8 + sum(((distance >= boundary).astype(jnp.int32) for boundary in bucket_edges))
    inside = jnp.where(distance < 8, distance, beyond)
    return inside + BUCKETS // 2 * (offset > 0).astype(jnp.int32)


def product(left, right):
    return jnp.dot(left, right, preferred_element_type=f32)


def left_product(left, right):
    return lax.dot_general(left, right, (((0,), (0,)), ((), ())), preferred_element_type=f32)


def right_product(left, right):
    return lax.dot_general(left, right, (((1,), (1,)), ((), ())), preferred_element_type=f32)


def rank_bits():
    return (lax.axis_size("wide") * lax.axis_size("narrow")).bit_length() - 1


def my_rank():
    return lax.axis_index("wide") * lax.axis_size("narrow") + lax.axis_index("narrow")


def swap(values, mask):
    ranks = 1 << rank_bits()
    pairs = [(rank, rank ^ mask) for rank in range(ranks)]
    return lax.ppermute(values, ("wide", "narrow"), pairs)


def scatter_order(position, order):
    count = len(order)
    return sum(((position >> (count - 1 - step)) & 1) << bit for step, bit in enumerate(order))


def gather_order(position, order):
    return sum(((position >> step) & 1) << bit for step, bit in enumerate(order))


def after(values, *others):
    flat, tree = jax.tree.flatten(values)
    done = lax.optimization_barrier(tuple(flat) + tuple(others))
    return jax.tree.unflatten(tree, done[: len(flat)])


def add(*values):
    total = values[0].astype(f32)
    for value in values[1:]:
        total = total + value.astype(f32)
    return total


def cut_kernel(kept_ref, came_ref, kept_out, sent_out):
    half = kept_out.shape[0]
    kept_out[...] = add(kept_ref[:half, :], came_ref[:half, :]).astype(bf16)
    sent_out[...] = add(kept_ref[half:, :], came_ref[half:, :]).astype(bf16)


def cut_loaded_kernel(kept_ref, came_ref, small_ref, kept_out, sent_out, small_out):
    half = kept_out.shape[0]
    kept_out[...] = add(kept_ref[:half, :], came_ref[:half, :]).astype(bf16)
    sent_out[:half, :] = add(kept_ref[half:, :], came_ref[half : 2 * half, :]).astype(bf16)
    small = add(small_ref[...], came_ref[2 * half :, :]).astype(bf16)
    sent_out[half:, :] = small
    small_out[...] = small


def cut(kept, came, small=None):
    half, cols = kept.shape[0] // 2, kept.shape[1]
    if half % 16 == 0 and small is None:
        return *call(cut_kernel, [shape((half, cols), bf16)] * 2, [kept, came], vmem=VM[4], us=0), None
    if half % 16 == 0:
        outs = [shape((half, cols), bf16), shape((half + 16, cols), bf16), shape((16, cols), bf16)]
        return call(cut_loaded_kernel, outs, [kept, came, small], vmem=VM[4], us=0)
    if small is not None:
        small = add(small, came[-16:]).astype(bf16)
        came = came[:-16]
    next_sent = add(kept[half:], came[half:]).astype(bf16)
    if small is not None:
        next_sent = jnp.concatenate([next_sent, small], 0)
    return add(kept[:half], came[:half]).astype(bf16), next_sent, small


def call(kernel, outs, args, spaces="", scratch=(), vmem=None, us=3, wide=False):
    kinds = {"s": pltpu.SMEM, "v": pltpu.VMEM, "a": pl.ANY, "h": pltpu.HBM}
    spaces = spaces.ljust(len(args) + len(outs), "v")
    specs = [pl.BlockSpec(memory_space=kinds[kind]) for kind in spaces]
    return pl.pallas_call(
        kernel,
        out_shape=tuple(outs),
        in_specs=specs[: len(args)],
        out_specs=tuple(specs[len(args) :]),
        scratch_shapes=list(scratch),
        compiler_params=pltpu.CompilerParams(vmem_limit_bytes=(60 if wide else vmem or VM[3]) * 1024 * 1024),
        cost_estimate=pl.CostEstimate(flops=int(us * COST), bytes_accessed=0, transcendentals=0),
    )(*args)


def shape(dims, kind=f32):
    return jax.ShapeDtypeStruct(tuple(dims), kind)


def room(values):
    return pltpu.VMEM(values.shape, values.dtype)


def loads(refs, rooms, sems):
    return [pltpu.make_async_copy(ref, place, sems.at[i]) for i, (ref, place) in enumerate(zip(refs, rooms))]


def bias_kernel(doc_length, rank_ref, table_ref, doc_bias_ref, slot_bias_ref, line_ref):
    pairs = doc_bias_ref.shape[0]
    parts = doc_length // LANES
    length = line_ref.shape[1]
    offset = lax.broadcasted_iota(jnp.int32, (BUCKETS, length), 1) - doc_length
    hot = (bucket_index(offset) == lax.broadcasted_iota(jnp.int32, (BUCKETS, length), 0)).astype(f32)
    line_ref[...] = lax.dot_general(
        table_ref[...], hot, (((0,), (0,)), ((), ())), precision=highest, preferred_element_type=f32
    )
    narrow = rank_ref[0] & (parts - 1)

    def spread(head, start):
        line = line_ref[pl.ds(head, 1), pl.ds(pl.multiple_of(start, LANES), 2 * LANES)]
        rolled = pltpu.roll(jnp.broadcast_to(line, (LANES, 2 * LANES)), 0, 1, stride=1, stride_axis=0)
        return rolled[:, LANES:]

    def one_pair(pair, carry):
        for side in range(2):
            rows = slice(side * LANES, (side + 1) * LANES)
            head = 2 * pair + side
            for part in range(parts):
                distance = (narrow ^ part) - narrow
                doc_bias_ref[pair, rows, part * LANES : (part + 1) * LANES] = spread(
                    head, doc_length - LANES + distance * LANES
                )
            slot_bias_ref[pair, rows, :] = spread(head, doc_length - LANES)
        return carry

    lax.fori_loop(0, pairs, one_pair, 0)


def count_kernel(doc_length, doc_total, rank_ref, picked_ref, counts_ref, tally_ref, load_ref, places_ref, scratch_ref, sem):
    slots, slot_length, picks = load_ref.shape
    rows = slots * slot_length
    blocks = counts_ref.shape[0]
    narrow_size = picked_ref.shape[0] // slots
    first = (rank_ref[0] & (narrow_size - 1)) * slots
    load = pltpu.make_async_copy(picked_ref.at[pl.ds(first, slots)], load_ref, sem)
    load.start()
    load.wait()

    places_ref[...] = load_ref[...].reshape(rows, picks)

    def one_row(row, carry):
        places = places_ref[pl.ds(row, 1), :]
        high = places >> 7
        low = places & 127
        high_hot = (lax.broadcasted_iota(jnp.int32, (blocks, picks), 0) == high).astype(bf16)
        low_hot = (lax.broadcasted_iota(jnp.int32, (LANES, picks), 0) == low).astype(bf16)
        scratch_ref[pl.ds(row, blocks, stride=rows), :] = right_product(high_hot, low_hot)
        return carry

    lax.fori_loop(0, rows, one_row, 0, unroll=8)

    def one_block(block, carry):
        start = pl.multiple_of(block * rows, rows)
        counts_ref[block] = scratch_ref[pl.ds(start, rows), :].astype(bf16)
        return carry

    lax.fori_loop(0, blocks, one_block, 0, unroll=4)

    owner = places_ref[...] // doc_length
    lane = lax.broadcasted_iota(jnp.int32, (rows, LANES), 1)
    tally = jnp.zeros((rows, LANES), f32)
    for doc in range(doc_total):
        number = jnp.sum((owner == doc).astype(f32), 1, keepdims=True)
        tally = jnp.where(lane == doc, number, tally)
    tally_ref[...] = tally


def rms_scale(values):
    return lax.rsqrt(jnp.mean(values * values, -1, keepdims=True) + epsilon)


def rms_back(values, gain, grad):
    scale = rms_scale(values)
    weighted = grad * gain
    inner = jnp.mean(weighted * values, -1, keepdims=True)
    return scale * weighted - values * (scale * scale * scale * inner)


def tile(index, size=LANES):
    return pl.ds(pl.multiple_of(index * size, size), size)


def halves(values, zero_row):
    return jnp.concatenate([jnp.where(zero_row, values, jnp.zeros((), values.dtype)),
                            jnp.where(zero_row, jnp.zeros((), values.dtype), values)], 0)


def joined(values, first_lanes):
    rows = values.shape[0] // 2
    return jnp.where(first_lanes, values[:rows], values[rows:])


def forward_kernel(
    slots, slot_length, rank_ref, lengths_ref, queries_ref, own_ref, near_ref, far_ref, last_ref, doc_bias_ref,
    slot_bias_ref, attend_gain_ref, feed_gain_ref, final_gain_ref,
    wq_ref, wk_ref, wv_ref, wo_ref, wg_ref, wu_ref, wd_ref, wp_ref,
    all_ref, query_ref, key_ref, value_ref, doc_probs_ref, slot_probs_ref, mixed_ref, after_attend_ref,
    normed_feed_ref, hidden_ref, gate_slope_ref, up_slope_ref, after_feed_ref, normed_final_ref, embed_ref,
    slot_unit_ref, doc_unit_ref,
    slot_ref, slot_sem,
):
    slot_rows = slots * slot_length
    rows, width = query_ref.shape
    pairs = doc_probs_ref.shape[0]
    half = LANES // 2
    narrow_size = queries_ref.shape[0] // slots
    first = (rank_ref[0] & (narrow_size - 1)) * slots
    load_slots = pltpu.make_async_copy(queries_ref.at[pl.ds(first, slots)], slot_ref, slot_sem)
    load_slots.start()
    gain = attend_gain_ref[...].reshape(1, width)
    place = slot_rows
    for ref in (own_ref, near_ref, far_ref, last_ref):
        tokens = ref[...].astype(f32)
        all_ref[place : place + ref.shape[0], :] = (tokens * rms_scale(tokens) * gain).astype(bf16)
        place += ref.shape[0]
    load_slots.wait()
    slot_tokens = slot_ref[...].reshape(slot_rows, width).astype(f32)
    all_ref[:slot_rows, :] = (slot_tokens * rms_scale(slot_tokens) * gain).astype(bf16)
    normed = all_ref[:rows, :]
    query_ref[...] = product(normed, wq_ref[...]).astype(bf16)
    key_ref[...] = product(all_ref[...], wk_ref[...]).astype(bf16)
    value_ref[...] = product(all_ref[...], wv_ref[...]).astype(bf16)

    lane = lax.broadcasted_iota(jnp.int32, (slot_rows, LANES), 1)
    row = lax.broadcasted_iota(jnp.int32, (slot_rows, slot_rows), 0)
    col = lax.broadcasted_iota(jnp.int32, (slot_rows, slot_rows), 1)
    slot_keep = row < 0
    for slot in range(slots):
        start = slot * slot_length
        inside = (row >= start) & (row < start + slot_length) & (col >= start)
        slot_keep = slot_keep | (inside & (col < start + lengths_ref[first + slot]))

    def softmax(scores):
        weights = jnp.exp(scores - jnp.max(scores, -1, keepdims=True))
        return (weights * (1.0 / jnp.sum(weights, -1, keepdims=True))).astype(bf16)

    first_lanes = lane < half
    pair_keep = jnp.concatenate([slot_keep, slot_keep], 0)

    def one_pair(pair, carry):
        lanes = tile(pair)
        slot_query = halves(query_ref[:slot_rows, lanes], first_lanes)
        scores = right_product(slot_query, key_ref[:slot_rows, lanes]) + slot_bias_ref[pair]
        probs = softmax(jnp.where(pair_keep, scores, masked_value))
        slot_probs_ref[pair] = probs
        slot_mixed = product(probs, value_ref[:slot_rows, lanes])
        mixed_ref[:slot_rows, lanes] = joined(slot_mixed, first_lanes).astype(bf16)
        doc_query = halves(query_ref[slot_rows:, lanes], first_lanes)
        scores = right_product(doc_query, key_ref[slot_rows:, lanes]) + doc_bias_ref[pair]
        probs = softmax(scores)
        doc_probs_ref[pair] = probs
        doc_mixed = product(probs, value_ref[slot_rows:, lanes])
        mixed_ref[slot_rows:, lanes] = joined(doc_mixed, first_lanes).astype(bf16)
        return carry

    lax.fori_loop(0, pairs, one_pair, 0, unroll=2)

    attended = product(mixed_ref[...], wo_ref[...])
    after_attend_ref[:slot_rows, :] = slot_ref[...].reshape(slot_rows, width).astype(f32) + attended[:slot_rows]
    after_attend_ref[slot_rows:, :] = own_ref[...].astype(f32) + attended[slot_rows:]
    after_attend = after_attend_ref[...]
    feed_gain = feed_gain_ref[...].reshape(1, width)
    normed_feed_ref[...] = (after_attend * rms_scale(after_attend) * feed_gain).astype(bf16)

    def one_part(step, carry):
        part = tile(step, CHUNK)
        gate = product(normed_feed_ref[...], wg_ref[:, part])
        upward = product(normed_feed_ref[...], wu_ref[:, part])
        factor = 0.7978845608028654
        square = gate * gate
        bent = jnp.tanh(factor * gate * (1.0 + 0.044715 * square))
        curve = 0.5 * gate * (1.0 + bent)
        slope = 0.5 * (1.0 + bent) + 0.5 * factor * gate * (1.0 - bent * bent) * (1.0 + 3 * 0.044715 * square)
        hidden_ref[:, part] = (curve * upward).astype(bf16)
        gate_slope_ref[:, part] = (upward * slope).astype(bf16)
        up_slope_ref[:, part] = curve.astype(bf16)
        return carry

    lax.fori_loop(0, hidden_ref.shape[1] // CHUNK, one_part, 0, unroll=2)
    after_feed = after_attend_ref[...] + product(hidden_ref[...], wd_ref[...])
    after_feed_ref[...] = after_feed
    final_gain = final_gain_ref[...].reshape(1, width)
    normed_final = (after_feed * rms_scale(after_feed) * final_gain).astype(bf16)
    normed_final_ref[...] = normed_final
    embed = product(normed_final, wp_ref[...])
    embed_ref[...] = embed
    unit = (embed * lax.rsqrt(jnp.sum(embed * embed, -1, keepdims=True) + epsilon)).astype(bf16)
    slot_unit_ref[...] = unit[:slot_rows]
    doc_unit_ref[...] = unit[slot_rows:]


def loss_kernel(
    order, gathered, doc_total, slots, rank_ref, lengths_ref, positives_ref, counts_ref, near_ref, far_ref, unit_ref,
    tally_ref, losses_ref, grad_ref, kept_ref, sent_ref, sum_ref, scaled_ref,
):
    rows = unit_ref.shape[0]
    blocks = counts_ref.shape[0]
    per_doc = blocks // doc_total
    rank = rank_ref[0]
    half = blocks // 2
    sum_ref[...] = jnp.zeros_like(sum_ref)

    def gather_step(place, carry):
        near = rank ^ gather_order(place, gathered)
        far = near ^ (1 << gathered[-1])
        sum_ref[near // per_doc] += product(counts_ref[near], near_ref[place])
        sum_ref[far // per_doc] += product(counts_ref[far], far_ref[place])
        return carry

    lax.fori_loop(0, half, gather_step, 0, unroll=4)

    unit = unit_ref[...].astype(f32)
    lane = lax.broadcasted_iota(jnp.int32, (rows, LANES), 1)
    summed = jnp.zeros((rows, LANES), f32)
    for doc in range(doc_total):
        number = jnp.sum(sum_ref[doc] * unit, 1, keepdims=True)
        summed = jnp.where(lane == doc, number, summed)
    tally = tally_ref[...]
    most = jnp.maximum(tally, 1.0)
    slot_length = rows // slots
    narrow_size = lengths_ref.shape[0] // slots
    first = (rank & (narrow_size - 1)) * slots
    row = lax.broadcasted_iota(jnp.int32, (rows, LANES), 0)
    slot_row = lax.broadcasted_iota(jnp.int32, (slots, LANES), 0)
    valid = row < 0
    positive = jnp.zeros((slots, LANES), jnp.int32)
    for slot in range(slots):
        start = slot * slot_length
        valid = valid | ((row >= start) & (row < start + lengths_ref[first + slot]))
        positive = jnp.where(slot_row == slot, positives_ref[first + slot], positive)
    weight = jnp.where(valid, jnp.minimum(tally, 1.0), 0.0)
    pooled = (weight * (summed / most)).reshape(slots, slot_length, LANES)
    weight_sum = jnp.maximum(jnp.sum(weight.reshape(slots, slot_length, LANES), 1), 1.0)
    scores = jnp.sum(pooled, 1) / weight_sum / contrastive_sharpness_factor
    slot_lane = lax.broadcasted_iota(jnp.int32, (slots, LANES), 1)
    inside = slot_lane < doc_total
    scores = jnp.where(inside, scores, -jnp.inf)
    top = jnp.max(scores, -1, keepdims=True)
    powers = jnp.exp(scores - top)
    total = jnp.sum(powers, -1, keepdims=True)
    chosen = (slot_lane == positive).astype(f32)
    picked = jnp.sum(jnp.where(slot_lane == positive, scores, 0.0), -1, keepdims=True)
    losses_ref[...] = jnp.broadcast_to(top + jnp.log(total) - picked, (slots, LANES))
    slope = (powers / total - chosen) / contrastive_sharpness_factor / weight_sum
    slope = jnp.where(inside, slope, 0.0)
    slope = jnp.broadcast_to(slope[:, None, :], (slots, slot_length, LANES)).reshape(rows, LANES)
    slope = slope * weight / most

    grad = jnp.zeros((rows, unit.shape[1]), f32)
    for doc in range(doc_total):
        column = jnp.sum(jnp.where(lane == doc, slope, 0.0), 1, keepdims=True)
        grad = grad + column * sum_ref[doc]
        scaled_ref[doc] = (column * unit).T.astype(bf16)
    grad_ref[...] = grad

    def scatter_step(place, carry):
        kept = rank ^ scatter_order(place, order)
        sent = kept ^ (1 << order[0])
        kept_ref[place] = product(scaled_ref[kept // per_doc], counts_ref[kept]).astype(bf16)
        sent_ref[place] = product(scaled_ref[sent // per_doc], counts_ref[sent]).astype(bf16)
        return carry

    lax.fori_loop(0, half, scatter_step, 0, unroll=4)


def feed_back(
    part, grad_unit, embed_ref, after_feed_ref, after_attend_ref, gate_slope_ref, up_slope_ref, feed_gain_ref,
    final_gain_ref, wo_ref, wg_ref, wu_ref, wd_ref, wp_ref, grads_out, after_out, mixed_out, more_ref,
):
    units, width = wd_ref.shape
    up_start, feed_start = units, 2 * units
    attend_start, embed_start = 2 * units + width, 2 * units + 2 * width
    embed = embed_ref[part, :]
    scale = lax.rsqrt(jnp.sum(embed * embed, -1, keepdims=True) + epsilon)
    inner = jnp.sum(grad_unit * embed, -1, keepdims=True)
    grad_embed = (scale * grad_unit - embed * (scale * scale * scale * inner)).astype(bf16)
    grads_out[:, embed_start : embed_start + embed.shape[1]] = grad_embed
    grad_after_feed = rms_back(
        after_feed_ref[part, :], final_gain_ref[...].reshape(1, -1), right_product(grad_embed, wp_ref[...])
    )
    after_out[...] = grad_after_feed
    grad_feed = grad_after_feed.astype(bf16)
    grads_out[:, feed_start:attend_start] = grad_feed
    def one_part(step, total):
        cols = tile(step, CHUNK)
        grad_hidden = right_product(grads_out[:, feed_start:attend_start], wd_ref[cols, :])
        grad_gate = (grad_hidden * gate_slope_ref[part, cols].astype(f32)).astype(bf16)
        grad_up = (grad_hidden * up_slope_ref[part, cols].astype(f32)).astype(bf16)
        grads_out[:, cols] = grad_gate
        grads_out[:, pl.ds(pl.multiple_of(up_start + step * CHUNK, CHUNK), CHUNK)] = grad_up
        more_ref[...] += right_product(grad_gate, wg_ref[:, cols]) + right_product(grad_up, wu_ref[:, cols])
        return total

    more_ref[...] = jnp.zeros_like(more_ref)
    lax.fori_loop(0, units // CHUNK, one_part, 0, unroll=2)
    total = more_ref[...]
    more = rms_back(after_attend_ref[part, :], feed_gain_ref[...].reshape(1, -1), total)
    grad_after_attend = after_out[...] + more
    after_out[...] = grad_after_attend
    grad_attend = grad_after_attend.astype(bf16)
    grads_out[:, attend_start:embed_start] = grad_attend
    mixed_out[...] = right_product(grad_attend, wo_ref[...]).astype(bf16)


def attend_back(
    far_parts, queries, keys, query_ref, key_ref, value_ref, probs_ref, mixed_ref, query_out, key_out, value_out,
    sums_out,
):
    rows = mixed_ref.shape[0]
    length = probs_ref.shape[2]
    half = LANES // 2
    first_lanes = lax.broadcasted_iota(jnp.int32, (rows, LANES), 1) < half
    row = lax.broadcasted_iota(jnp.int32, (rows, rows), 0)
    col = lax.broadcasted_iota(jnp.int32, (rows, rows), 1)
    flip = (row + col == rows - 1).astype(bf16)
    nothing = jnp.zeros((rows, LANES), f32)

    def one_pair(pair, carry):
        lanes = tile(pair)
        grad_mixed = halves(mixed_ref[:, lanes], first_lanes)
        query = halves(query_ref[queries, lanes], first_lanes)
        probs = probs_ref[pair]
        grad_probs = right_product(grad_mixed, value_ref[keys, lanes])
        exact = probs.astype(f32)
        inner = jnp.sum(exact * grad_probs, -1, keepdims=True)
        grad_scores = (exact * (grad_probs - inner)).astype(bf16)
        query_out(joined(product(grad_scores, key_ref[keys, lanes]), first_lanes).astype(bf16), pair)
        key_out(left_product(grad_scores, query).astype(bf16), pair)
        value_out(left_product(probs, grad_mixed).astype(bf16), pair)
        for side in range(2):
            head = 2 * pair + side
            own = grad_scores[side * rows : (side + 1) * rows, :]
            for part in range(length // LANES):
                piece = own[:, part * LANES : (part + 1) * LANES]
                if part in far_parts:
                    line = jnp.concatenate([piece.astype(f32), nothing], 1)
                else:
                    line = pltpu.roll(
                        jnp.concatenate([product(flip, piece), nothing], 1), 0, 1, stride=1, stride_axis=0
                    )
                sums_out[tile(head, 8), part * 2 * LANES : (part + 1) * 2 * LANES] = jnp.sum(
                    line.reshape(rows // 8, 8, 2 * LANES), 0
                )
        return carry

    lax.fori_loop(0, probs_ref.shape[0], one_pair, 0, unroll=2)


def input_back(tokens, gain_ref, after_ref, query, key, value, wq_ref, wk_ref, wv_ref):
    grad_normed = right_product(query, wq_ref[...])
    grad_normed = grad_normed + right_product(key, wk_ref[...])
    grad_normed = grad_normed + right_product(value, wv_ref[...])
    return after_ref[...] + rms_back(tokens, gain_ref[...].reshape(1, -1), grad_normed)


def table_sums(sums_ref, distances):
    heads = sums_ref.shape[0] // 8
    span = lax.broadcasted_iota(jnp.int32, (2 * LANES, LANES), 0) - (LANES - 1)
    bucket = lax.broadcasted_iota(jnp.int32, (2 * LANES, LANES), 1)
    total = jnp.zeros((heads, LANES), f32)
    for part, distance in enumerate(distances):
        lines = jnp.sum(sums_ref[:, part * 2 * LANES : (part + 1) * 2 * LANES].reshape(heads, 8, 2 * LANES), 1)
        hot = (bucket_index(span + distance * LANES) == bucket).astype(f32)
        total = total + lax.dot_general(
            lines, hot, (((1,), (0,)), ((), ())), precision=highest, preferred_element_type=f32
        )
    return total


def slot_feed_kernel(
    grad_unit_ref, embed_ref, after_feed_ref, after_attend_ref, gate_slope_ref, up_slope_ref, feed_gain_ref,
    final_gain_ref, wp_ref, wd_ref, wg_ref, wu_ref, wo_ref,
    grads_out, after_out, mixed_out, more_ref,
):
    feed_back(
        slice(0, after_out.shape[0]), grad_unit_ref[...], embed_ref, after_feed_ref, after_attend_ref,
        gate_slope_ref, up_slope_ref, feed_gain_ref, final_gain_ref, wo_ref, wg_ref, wu_ref, wd_ref, wp_ref, grads_out,
        after_out, mixed_out, more_ref,
    )


def slot_attend_kernel(
    query_ref, key_ref, value_ref, probs_ref, mixed_ref, grads_out, table_out, sums_ref
):
    rows, width = mixed_ref.shape

    def out(place):
        def store(values, pair):
            grads_out[:, pl.ds(pl.multiple_of(place * width + pair * LANES, LANES), LANES)] = values

        return store

    part = slice(0, rows)
    attend_back(
        (), part, part, query_ref, key_ref, value_ref, probs_ref, mixed_ref, out(0), out(1), out(2), sums_ref
    )
    table_out[...] = table_sums(sums_ref, [0])


def doc_feed_kernel(came, *refs):
    parts, refs = refs[:came], refs[came:]
    (
        embed_ref, after_feed_ref, after_attend_ref, gate_slope_ref, up_slope_ref, feed_gain_ref, final_gain_ref,
        wp_ref, wd_ref, wg_ref, wu_ref, wo_ref,
        grads_out, after_out, mixed_out, more_ref,
    ) = refs
    rows = after_out.shape[0]
    grad_unit = add(*(part[0] for part in parts)).T
    feed_back(
        slice(embed_ref.shape[0] - rows, embed_ref.shape[0]), grad_unit, embed_ref, after_feed_ref,
        after_attend_ref, gate_slope_ref, up_slope_ref, feed_gain_ref, final_gain_ref, wo_ref, wg_ref, wu_ref, wd_ref,
        wp_ref, grads_out, after_out, mixed_out, more_ref,
    )


def doc_attend_kernel(
    rank_ref, query_ref, key_ref, value_ref, probs_ref, mixed_ref, slot_table_ref, grads_out, table_out, query_room,
    sums_ref,
):
    rows, width = query_room.shape
    length = probs_ref.shape[2]
    first = key_ref.shape[0] - length

    def query_out(values, pair):
        query_room[:, tile(pair)] = values

    def key_out(values, pair):
        grads_out[:length, tile(pair)] = values

    def value_out(values, pair):
        grads_out[:length, pl.ds(pl.multiple_of(width + pair * LANES, LANES), LANES)] = values

    attend_back(
        (2,), slice(first, first + rows), slice(first, key_ref.shape[0]), query_ref, key_ref, value_ref, probs_ref,
        mixed_ref, query_out, key_out, value_out, sums_ref,
    )
    grads_out[length:, :width] = query_room[: rows // 2, :]
    grads_out[length:, width:] = query_room[rows // 2 :, :]
    parts = length // LANES
    narrow = rank_ref[0] & (parts - 1)
    table = table_sums(sums_ref, [(narrow ^ part) - narrow for part in range(parts)]) + slot_table_ref[...]
    heads = table.shape[0]
    table_out[...] = jnp.concatenate([table, jnp.zeros((16 - heads, LANES), f32)], 0).astype(bf16)


def pick_columns(values, total, order, flipped, rank):
    count = 1 << len(order) + 1
    size = total // count
    row = lax.broadcasted_iota(jnp.int32, (total, total // 2), 0)
    col = lax.broadcasted_iota(jnp.int32, (total, total // 2), 1)
    source = (scatter_order(col // size, order) ^ rank ^ flipped) * size + col % size
    return product(values, (row == source).astype(bf16)).astype(bf16)


def pick_tiles(values_ref, order, flipped, rank, store):
    rows = values_ref.shape[0]
    half = LANES // 2
    first_lanes = lax.broadcasted_iota(jnp.int32, (rows, LANES), 1) < half
    upper = ((rank ^ flipped) & 1) == 1

    def one_tile(step, carry):
        place = 2 * step
        sides = []
        for side in range(2):
            tile = (rank ^ scatter_order(place + side, order)) >> 1
            values = values_ref[:, pl.ds(pl.multiple_of(tile * LANES, LANES), LANES)].astype(f32)
            turned = pltpu.roll(values, half, 1)
            sides.append(jnp.where(upper, turned, values) if side == 0 else jnp.where(upper, values, turned))
        store(step, jnp.where(first_lanes, sides[0], sides[1]).astype(bf16))
        return carry

    lax.fori_loop(0, 1 << len(order) - 1, one_tile, 0)


def turn_kernel(
    orders, rank_ref, all_ref, normed_feed_ref, mixed_ref, normed_final_ref, hidden_ref, kept_out, sent_out, doc_out,
):
    first, second, third, fourth = orders
    rank = rank_ref[0]
    rows, width = normed_feed_ref.shape
    units = hidden_ref.shape[1]
    slots = all_ref.shape[0] - doc_out.shape[0]
    half = width // 2
    for out, flipped in ((kept_out, 0), (sent_out, 1)):
        out[:, :half] = pick_columns(normed_feed_ref[...], width, first, flipped, rank)
        out[:, half : 2 * half] = pick_columns(normed_feed_ref[...], width, second, flipped, rank)
        out[:, 2 * half : 3 * half] = pick_columns(mixed_ref[...], width, first, flipped, rank)
        out[:, 3 * half : 4 * half] = pick_columns(normed_final_ref[...], width, second, flipped, rank)
        start = 4 * half
        if units >> (len(third) + 1) == LANES // 2:

            def store(place, values):
                out[:, pl.ds(pl.multiple_of(start + place * LANES, LANES), LANES)] = values

            pick_tiles(hidden_ref, third, flipped, rank, store)
        else:
            out[:, start : start + units // 2] = pick_columns(hidden_ref[...], units, third, flipped, rank)
        start = start + units // 2
        out[slots:, start:] = jnp.zeros((rows - slots, half), bf16)
        if flipped:
            out[:slots, start:] = pick_columns(all_ref[:slots, :], width, fourth, flipped, rank)
        else:
            both = pick_columns(all_ref[...], width, fourth, flipped, rank)
            out[:slots, start:] = both[:slots]
            doc_out[...] = both[slots:]


def store_product(left, right_ref, columns, kept_ref, sent_ref, start):
    half = left.shape[1] // 2
    size = 2 * LANES

    def one_part(first, size):
        here = pl.ds(pl.multiple_of(start + first, LANES), size)
        result = left_product(left, right_ref[:, pl.ds(pl.multiple_of(first, LANES), size)]).astype(bf16)
        kept_ref[:half, here] = result[:half]
        sent_ref[:half, here] = result[half:]

    def step(place, carry):
        one_part(place * size, size)
        return carry

    lax.fori_loop(0, columns // size, step, 0, unroll=2)
    if columns % size:
        one_part(columns // size * size, columns % size)


def weight_kernel(
    terms, kept_any, came_any, slot_any, slot_came_any, doc_any, doc_came_any, kept_ref, sent_ref, left_ref, right_ref,
    sems,
):
    rows = kept_any.shape[0]
    part = slot_any.shape[0]
    copies = []
    left_place, right_place = 0, 0
    for left_start, left_width, right_start, right_width in terms:
        pieces = []
        for place, ref in enumerate((kept_any, came_any)):
            source = ref.at[:, left_start : left_start + left_width]
            target = left_ref.at[place * rows : (place + 1) * rows, left_place : left_place + left_width]
            pieces.append((source, target))
        for place, ref in enumerate((slot_any, doc_any, slot_came_any, doc_came_any)):
            source = ref.at[:, right_start : right_start + right_width]
            target = right_ref.at[place * part : (place + 1) * part, right_place : right_place + right_width]
            pieces.append((source, target))
        first = sum(len(group) for group in copies)
        copies.append(
            [pltpu.make_async_copy(one, two, sems.at[first + i]) for i, (one, two) in enumerate(pieces)]
        )
        left_place += left_width
        right_place += right_width
    for group in copies:
        for copy in group:
            copy.start()
    left_place, right_place = 0, 0
    for group, (_, left_width, _, right_width) in zip(copies, terms):
        for copy in group:
            copy.wait()
        left = left_ref[:, left_place : left_place + left_width]
        right = right_ref.at[:, right_place : right_place + right_width]
        store_product(left, right, right_width, kept_ref, sent_ref, right_place)
        left_place += left_width
        right_place += right_width


def attend_weight_kernel(
    doc_ref, kept_any, came_any, slot_any, slot_came_any, grads_ref, other_ref, table_ref, other_table_ref,
    kept_out, sent_out, pair_kept, pair_sent, slot_room, slot_came_room, left_ref, right_ref, query_ref, sems,
):
    rows = slot_any.shape[0]
    width = slot_room.shape[1] // 3
    half = doc_ref.shape[1]
    length = doc_ref.shape[0]
    lanes = slice(kept_any.shape[1] - half, kept_any.shape[1])
    copies = loads(
        (slot_any, slot_came_any, kept_any.at[:rows, lanes], came_any.at[:rows, lanes]),
        (slot_room, slot_came_room, left_ref.at[length : length + rows, :], left_ref.at[length + rows :, :]),
        sems,
    )
    for copy in copies:
        copy.start()
    left_ref[:length, :] = doc_ref[...]
    for part in range(length // LANES):
        here = slice(part * LANES, (part + 1) * LANES)
        there = slice((part ^ 1) * LANES, ((part ^ 1) + 1) * LANES)
        right_ref[here, :] = add(grads_ref[here, :], other_ref[there, :]).astype(bf16)
    pair_kept[...] = right_ref[:LANES, :]
    pair_sent[...] = right_ref[2 * LANES : 3 * LANES, :]
    small = LANES // 2
    for place, ref in enumerate((grads_ref, other_ref)):
        query_ref[2 * place * small : (2 * place + 1) * small, :] = ref[length:, :width]
        query_ref[(2 * place + 1) * small : (2 * place + 2) * small, :] = ref[length:, width:]
    for copy in copies:
        copy.wait()
    right_ref[length : length + rows, :] = slot_room[:, width:]
    right_ref[length + rows :, :] = slot_came_room[:, width:]
    query_ref[2 * LANES : 2 * LANES + rows, :] = slot_room[:, :width]
    query_ref[2 * LANES + rows :, :] = slot_came_room[:, :width]
    store_product(left_ref[...], right_ref, 2 * width, kept_out, sent_out, width)
    left = jnp.concatenate([left_ref[: 2 * LANES, :], left_ref[length:, :]], 0)
    store_product(left, query_ref, width, kept_out, sent_out, 0)
    tail = sent_out.shape[0] - 16
    sent_out[tail:, :] = jnp.zeros((16, sent_out.shape[1]), bf16)
    sent_out[tail:, :LANES] = add(table_ref[...], other_table_ref[...]).astype(bf16)


def doc_input_kernel(
    tokens_ref, gain_ref, after_ref, grads_ref, kept_ref, came_ref, wq_ref, wk_ref, wv_ref, tokens_out
):
    rows, width = tokens_ref.shape
    rest = grads_ref.shape[0] - rows // 2
    query = jnp.concatenate([grads_ref[rest:, :width], grads_ref[rest:, width:]], 0)
    pair = add(kept_ref[...], came_ref[...]).astype(bf16)
    tokens_out[...] = input_back(
        tokens_ref[...].astype(f32), gain_ref, after_ref, query, pair[:, :width], pair[:, width:], wq_ref, wk_ref, wv_ref
    )


def slot_input_kernel(
    slots, rank_ref, tokens_any, gain_ref, after_ref, grads_ref, wq_ref, wk_ref, wv_ref, tokens_out, slot_room, sem
):
    narrow_size = tokens_any.shape[0] // slots
    first = (rank_ref[0] & (narrow_size - 1)) * slots
    load = pltpu.make_async_copy(tokens_any.at[pl.ds(first, slots)], slot_room, sem)
    load.start()
    load.wait()
    width = tokens_out.shape[1]
    query, key, value = (grads_ref[:, place * width : (place + 1) * width] for place in range(3))
    tokens_out[...] = input_back(
        slot_room[...].reshape(tokens_out.shape).astype(f32), gain_ref, after_ref, query, key, value, wq_ref, wk_ref,
        wv_ref,
    )


def on_device(
    doc_tokens, query_tokens, query_lengths, positive_docs, retrieved, attend_gain, query_weight, key_weight,
    value_weight, output_weight, bias_table, feed_gain, gate_weight, up_weight, down_weight, final_gain, proj_weight,
):
    narrow_size = lax.axis_size("narrow")
    bits = rank_bits()
    rank = my_rank()
    rank_word = rank.astype(jnp.int32).reshape(1)
    doc_rows, width = doc_tokens.shape[1:]
    doc_length = doc_rows * narrow_size
    doc_total = doc_tokens.shape[0] * lax.axis_size("wide")
    slots = query_tokens.shape[0] // narrow_size
    slot_length = query_tokens.shape[1]
    heads = bias_table.shape[1]
    units = gate_weight.shape[1]
    columns = proj_weight.shape[1]
    slot_rows = slots * slot_length
    rows = slot_rows + doc_rows
    blocks = doc_total * doc_length // LANES
    assert doc_tokens.shape[0] == 1 and doc_rows == LANES and slot_rows == LANES and narrow_size == 4
    assert columns == LANES and doc_total <= LANES and blocks == 1 << bits
    gains = (attend_gain, feed_gain, final_gain)
    dma = pltpu.SemaphoreType.DMA
    waxes = list(range(3, bits))

    orders = (
        waxes[:1] + [2] + [1] + waxes[1:],
        [1] + [2] + waxes[:1] + waxes[1:],
        waxes[:1] + [2] + [1] + waxes[1:],
        [2] + [1] + waxes[:1] + waxes[1:],
    )
    own_tokens = doc_tokens[0]
    y_tokens = swap(own_tokens, 2)
    core_tokens = swap(own_tokens, 1)
    pairs = heads // 2
    doc_bias, slot_bias = call(
        functools.partial(bias_kernel, doc_length),
        [shape((pairs, 2 * doc_rows, doc_length)), shape((pairs, 2 * slot_rows, slot_rows))],
        [rank_word, bias_table],
        "s",
        [pltpu.VMEM((heads, 2 * doc_length + LANES), f32)],
    )
    y_tokens = after(y_tokens, doc_bias)
    both_tokens = swap(y_tokens, 1)

    all_rows = slot_rows + doc_length
    forward_shapes = [
        shape((all_rows, width), bf16),
        shape((rows, width), bf16),
        shape((all_rows, width), bf16),
        shape((all_rows, width), bf16),
        shape((pairs, 2 * doc_rows, doc_length), bf16),
        shape((pairs, 2 * slot_rows, slot_rows), bf16),
        shape((rows, width), bf16),
        shape((rows, width)),
        shape((rows, width), bf16),
        shape((rows, units), bf16),
        shape((rows, units), bf16),
        shape((rows, units), bf16),
        shape((rows, width)),
        shape((rows, width), bf16),
        shape((rows, columns)),
        shape((slot_rows, columns), bf16),
        shape((doc_rows, columns), bf16),
    ]
    weights = [
        query_weight, key_weight, value_weight, output_weight, gate_weight, up_weight, down_weight, proj_weight,
    ]
    slot_room = pltpu.VMEM((slots, slot_length, width), bf16)
    (
        all_normed, query, key, value, doc_probs, slot_probs, mixed, after_attend, normed_feed, hidden, gate_slope,
        up_slope, after_feed, normed_final, embed, slot_unit, doc_unit,
    ) = call(
        functools.partial(forward_kernel, slots, slot_length),
        forward_shapes,
        [
            rank_word, query_lengths, query_tokens, own_tokens, core_tokens, y_tokens, both_tokens, doc_bias, slot_bias,
            *gains, *weights,
        ],
        "ssa" + "v" * 9 + "v" * 8 + "v" * len(forward_shapes),
        [slot_room, dma],
        vmem=VM[0],
        us=18,
    )

    phases = [list(range(high, max(high - 2, 0), -1)) for high in range(bits - 1, 0, -2)]
    gathered = []
    near_units = doc_unit[None]
    for phase, group in enumerate(phases):
        group = group[::-1]
        masks = [gather_order(place, group) for place in range(1, 1 << len(group))]
        came = [swap(near_units, mask) for mask in masks]
        if phase == 0:
            counts, tally = call(
                functools.partial(count_kernel, doc_length, doc_total),
                [shape((blocks, slot_rows, LANES), bf16), shape((slot_rows, LANES))],
                after([rank_word, retrieved], doc_unit),
                "sa",
                [
                    pltpu.VMEM((slots, slot_length, retrieved.shape[2]), jnp.int32),
                    pltpu.VMEM((slot_rows, retrieved.shape[2]), jnp.int32),
                    pltpu.VMEM((blocks * slot_rows, LANES), f32),
                    dma,
                ],
                us=5,
                wide=bits > 5,
            )
            came = after(came, tally)
        if phase == 1:
            turned_cols = 5 * width // 2 + units // 2
            turned, turned_sent, turned_docs = call(
                functools.partial(turn_kernel, orders),
                [shape((rows, turned_cols), bf16)] * 2 + [shape((doc_length, width // 2), bf16)],
                after([rank_word, all_normed, normed_feed, mixed, normed_final, hidden], near_units),
                "s",
                us=5,
                wide=bits > 5,
            )
            came = after(came, turned)
        near_units = jnp.concatenate([near_units] + came, 0)
        gathered = gathered + group
    gathered = gathered + [0]
    far_units = swap(near_units, 1)

    order = list(range(bits))
    half = blocks // 2
    losses, grad_slot_unit, kept, sent = call(
        functools.partial(loss_kernel, order, gathered, doc_total, slots),
        [
            shape((slots, LANES)),
            shape((slot_rows, columns)),
            shape((half, columns, LANES), bf16),
            shape((half, columns, LANES), bf16),
        ],
        [rank_word, query_lengths, positive_docs, counts, near_units, far_units, slot_unit, tally],
        "sss",
        [
            pltpu.VMEM((doc_total, slot_rows, columns), f32),
            pltpu.VMEM((doc_total, columns, slot_rows), bf16),
        ],
        wide=bits > 5,
    )
    turned_came = swap(after(turned_sent, losses), 1)
    back_weights = [proj_weight, down_weight, gate_weight, up_weight, output_weight]
    doc_cols = 2 * units + 2 * width + columns

    came = [swap(sent, 1)]
    rest = order[1:]
    parts = [kept]
    phase = 0
    feed_shapes = [shape((LANES, doc_cols), bf16), shape((LANES, width)), shape((LANES, width), bf16)]
    while rest:
        group, rest = rest[:2], rest[2:]
        count = 1 << len(group)
        size = parts[0].shape[0] // count
        pieces = []
        for place in range(count):
            here = slice(place * size, (place + 1) * size)
            pieces.append(add(*(part[here] for part in parts), *(one[here] for one in came)).astype(bf16))
        masks = [scatter_order(place, group) for place in range(count)]
        came = [swap(piece, mask) for piece, mask in zip(pieces[1:], masks[1:])]
        parts = [pieces[0]]
        if phase == 0:
            slot_grads, slot_after, slot_mixed = call(
                slot_feed_kernel,
                feed_shapes,
                [after(grad_slot_unit, pieces[1], turned_came)]
                + [embed, after_feed, after_attend, gate_slope, up_slope, gains[1], gains[2]]
                + back_weights,
                "",
                [pltpu.VMEM((slot_rows, width), f32)],
                vmem=VM[1],
                us=7,
            )
            came = after(came, slot_after)
        if phase == 1:
            slot_came = swap(after(slot_grads, *pieces[1:]), 1)
            slot_thirds, slot_table = call(
                slot_attend_kernel,
                [shape((slot_rows, 3 * width), bf16), shape((heads, LANES))],
                [query, key, value, slot_probs, after(slot_mixed, *pieces[1:])],
                scratch=[pltpu.VMEM((heads * 8, 2 * LANES), f32)],
                us=4,
            )
            came = after(came, slot_table)
        phase += 1

    doc_grads, doc_after, doc_mixed = call(
        functools.partial(doc_feed_kernel, 1 + len(came)),
        feed_shapes,
        parts + after(came, slot_came)
        + [embed, after_feed, after_attend, gate_slope, up_slope, gains[1], gains[2]]
        + back_weights,
        "",
        [pltpu.VMEM((doc_rows, width), f32)],
        vmem=VM[2],
        us=7,
    )
    thirds_came = swap(after(slot_thirds, doc_after), 1)
    doc_came = swap(doc_grads, 1)

    class Stream:
        def __init__(self, kept, sent, order):
            self.kept, self.order, self.step = kept, order, 0
            self.loaded = sent.shape[0] > kept.shape[0]
            self.small = sent[-16:] if self.loaded else None
            self.send(sent)

        def send(self, sent):
            self.came = swap(sent, 1 << self.order[self.step])
            self.step += 1

        def advance(self, *wait):
            came = after(self.came, *wait)
            if self.step == len(self.order):
                if self.loaded:
                    self.small = add(self.small, came[-16:]).astype(bf16)
                    came = came[:-16]
                self.result = add(self.kept, came)
                return self.result
            self.kept, sent, self.small = cut(self.kept, came, self.small)
            self.send(sent)
            return self.kept

    def weight_product(terms, order, *wait):
        left = sum(term[1] for term in terms)
        right = sum(term[3] for term in terms)
        tall = terms[0][1] // 2
        args = after([turned, turned_came, slot_grads, slot_came, doc_grads, doc_came], *wait)
        kept, sent = call(
            functools.partial(weight_kernel, terms),
            [shape((tall, right), bf16)] * 2,
            args,
            "a" * 6,
            [pltpu.VMEM((2 * rows, left), bf16), pltpu.VMEM((2 * rows, right), bf16), dma((6 * len(terms),))],
        )
        return Stream(kept, sent, order)

    small_half = width // 2
    att_grads, table = call(
        doc_attend_kernel,
        [shape((doc_length + doc_rows // 2, 2 * width), bf16), shape((16, LANES), bf16)],
        [rank_word, query, key, value, doc_probs, doc_mixed, slot_table],
        "s",
        [pltpu.VMEM((doc_rows, width), bf16), pltpu.VMEM((heads * 8, 2 * doc_length), f32)],
    )
    att_came, table_came = swap(att_grads, 1), swap(table, 1)
    first = weight_product(
        [(0, small_half, 0, units), (2 * small_half, small_half, 2 * units + width, width)], orders[0], table
    )
    fourth_kept, fourth_sent, pair_kept, pair_sent = call(
        attend_weight_kernel,
        [
            shape((width // 4, 3 * width), bf16),
            shape((width // 4 + 16, 3 * width), bf16),
            shape((doc_rows, 2 * width), bf16),
            shape((doc_rows, 2 * width), bf16),
        ],
        [turned_docs, turned, turned_came, slot_thirds, thirds_came, att_grads, att_came, after(table, first.kept), table_came],
        "vaaaa",
        [
            pltpu.VMEM((slot_rows, 3 * width), bf16),
            pltpu.VMEM((slot_rows, 3 * width), bf16),
            pltpu.VMEM((doc_length + 2 * slot_rows, width // 2), bf16),
            pltpu.VMEM((doc_length + 2 * slot_rows, 2 * width), bf16),
            pltpu.VMEM((2 * doc_rows + 2 * slot_rows, width), bf16),
            dma((4,)),
        ],
    )
    fourth = Stream(fourth_kept, fourth_sent, orders[3])
    second = weight_product(
        [(small_half, small_half, units, units), (3 * small_half, small_half, 2 * units + 2 * width, columns)],
        orders[1],
        fourth_kept,
    )
    third = weight_product([(4 * small_half, units // 2, 2 * units, width)], orders[2], second.kept)
    def own_rows(values):
        return lax.dynamic_slice_in_dim(values, rank * (width >> bits), width >> bits, 0).astype(f32)

    def gain_grad(gain, *pairs):
        return sum(jnp.sum(own_rows(weight) * grad, 1) for weight, grad in pairs) / own_rows(gain)

    streams = {"A": first, "B": second, "C": third, "D": fourth}
    plan = "JADBACDpBADCBCIABDC"
    if bits != 5:
        plan = "J" + "ADBC" + "p" + "ADBC" * (bits - 3) + "I" + "ABDC"
    done = third.kept
    for event in plan[:-1]:
        if event in streams:
            done = streams[event].advance(done)
        elif event == "p":
            pair_came = swap(after(pair_sent, done), 2)
        elif event == "I":
            (done,) = call(
                doc_input_kernel,
                [shape((doc_rows, width))],
                [own_tokens, gains[0], doc_after, att_grads, pair_kept, after(pair_came, done)]
                + [query_weight, key_weight, value_weight],
                us=3,
            )
            doc_grad = done
        else:
            (done,) = call(
                functools.partial(slot_input_kernel, slots),
                [shape((slot_rows, width))],
                [rank_word, query_tokens, gains[0], slot_after, after(slot_thirds, done)]
                + [query_weight, key_weight, value_weight],
                "sa",
                [slot_room, dma],
                us=3,
            )
            query_grad = done
    gate_grad, output_grad = first.result[:, :units], first.result[:, units:]
    up_grad, proj_grad = second.result[:, :units], second.result[:, units:]
    query_g, key_g, value_g = (fourth.result[:, place * width : (place + 1) * width] for place in range(3))
    attend_gain_grad = gain_grad(attend_gain, (query_weight, query_g), (key_weight, key_g), (value_weight, value_g))
    feed_gain_grad = gain_grad(feed_gain, (gate_weight, gate_grad), (up_weight, up_grad))
    final_gain_grad = gain_grad(final_gain, (proj_weight, proj_grad))
    third.advance(done, attend_gain_grad, feed_gain_grad, final_gain_grad)
    return (
        losses[:, 0],
        doc_grad[None],
        query_grad.reshape(slots, slot_length, width),
        attend_gain_grad,
        query_g,
        key_g,
        value_g,
        output_grad,
        fourth.small[:heads, :BUCKETS].astype(f32).T,
        feed_gain_grad,
        gate_grad,
        up_grad,
        third.result,
        final_gain_grad,
        proj_grad,
    )


def solution(mesh):
    return jax.shard_map(
        on_device,
        mesh=mesh,
        in_specs=(
            P("wide", "narrow", None),
            P("wide", None, None),
            P("wide"),
            P("wide"),
            P("wide", None, None),
            P(),
            P(),
            P(),
            P(),
            P(),
            P(),
            P(),
            P(),
            P(),
            P(),
            P(),
            P(),
        ),
        out_specs=(
            P(("wide", "narrow")),
            P("wide", "narrow", None),
            P(("wide", "narrow"), None, None),
            P(("wide", "narrow")),
            P(("wide", "narrow"), None),
            P(("wide", "narrow"), None),
            P(("wide", "narrow"), None),
            P(("wide", "narrow"), None),
            P(),
            P(("wide", "narrow")),
            P(("wide", "narrow"), None),
            P(("wide", "narrow"), None),
            P(("wide", "narrow"), None),
            P(("wide", "narrow")),
            P(("wide", "narrow"), None),
        ),
        check_vma=False,
    )
```

```python
import functools

import jax
import jax.numpy as jnp
from jax import lax
from jax.experimental import pallas as pl
from jax.experimental.pallas import tpu as pltpu
from jax.sharding import PartitionSpec as P

BUCKETS = 32
LANES = 128
CHUNK = 512
VM = (12, 12, 12, 16, 8)
COST = 1.1e9

epsilon = 1e-06
contrastive_sharpness_factor = 0.01
masked_value = -1000000000.0
bucket_edges = (12, 16, 23, 32, 46, 64, 91)
highest = lax.Precision.HIGHEST
f32 = jnp.float32
bf16 = jnp.bfloat16


def bucket_index(offset):
    distance = jnp.abs(offset)
    beyond = 8 + sum(((distance >= boundary).astype(jnp.int32) for boundary in bucket_edges))
    inside = jnp.where(distance < 8, distance, beyond)
    return inside + BUCKETS // 2 * (offset > 0).astype(jnp.int32)


def product(left, right):
    return jnp.dot(left, right, preferred_element_type=f32)


def left_product(left, right):
    return lax.dot_general(left, right, (((0,), (0,)), ((), ())), preferred_element_type=f32)


def right_product(left, right):
    return lax.dot_general(left, right, (((1,), (1,)), ((), ())), preferred_element_type=f32)


def rank_bits():
    return (lax.axis_size("wide") * lax.axis_size("narrow")).bit_length() - 1


def my_rank():
    return lax.axis_index("wide") * lax.axis_size("narrow") + lax.axis_index("narrow")


def swap(values, mask):
    ranks = 1 << rank_bits()
    pairs = [(rank, rank ^ mask) for rank in range(ranks)]
    return lax.ppermute(values, ("wide", "narrow"), pairs)


def scatter_order(position, order):
    count = len(order)
    return sum(((position >> (count - 1 - step)) & 1) << bit for step, bit in enumerate(order))


def gather_order(position, order):
    return sum(((position >> step) & 1) << bit for step, bit in enumerate(order))


def after(values, *others):
    flat, tree = jax.tree.flatten(values)
    done = lax.optimization_barrier(tuple(flat) + tuple(others))
    return jax.tree.unflatten(tree, done[: len(flat)])


def add(*values):
    total = values[0].astype(f32)
    for value in values[1:]:
        total = total + value.astype(f32)
    return total


def cut_kernel(kept_ref, came_ref, kept_out, sent_out):
    half = kept_out.shape[0]
    kept_out[...] = add(kept_ref[:half, :], came_ref[:half, :]).astype(bf16)
    sent_out[...] = add(kept_ref[half:, :], came_ref[half:, :]).astype(bf16)


def cut_loaded_kernel(kept_ref, came_ref, small_ref, kept_out, sent_out, small_out):
    half = kept_out.shape[0]
    kept_out[...] = add(kept_ref[:half, :], came_ref[:half, :]).astype(bf16)
    sent_out[:half, :] = add(kept_ref[half:, :], came_ref[half : 2 * half, :]).astype(bf16)
    small = add(small_ref[...], came_ref[2 * half :, :]).astype(bf16)
    sent_out[half:, :] = small
    small_out[...] = small


def cut(kept, came, small=None):
    half, cols = kept.shape[0] // 2, kept.shape[1]
    if half % 16 == 0 and small is None:
        return *call(cut_kernel, [shape((half, cols), bf16)] * 2, [kept, came], vmem=VM[4], us=0), None
    if half % 16 == 0:
        outs = [shape((half, cols), bf16), shape((half + 16, cols), bf16), shape((16, cols), bf16)]
        return call(cut_loaded_kernel, outs, [kept, came, small], vmem=VM[4], us=0)
    if small is not None:
        small = add(small, came[-16:]).astype(bf16)
        came = came[:-16]
    next_sent = add(kept[half:], came[half:]).astype(bf16)
    if small is not None:
        next_sent = jnp.concatenate([next_sent, small], 0)
    return add(kept[:half], came[:half]).astype(bf16), next_sent, small


def call(kernel, outs, args, spaces="", scratch=(), vmem=None, us=3, wide=False):
    kinds = {"s": pltpu.SMEM, "v": pltpu.VMEM, "a": pl.ANY, "h": pltpu.HBM}
    spaces = spaces.ljust(len(args) + len(outs), "v")
    specs = [pl.BlockSpec(memory_space=kinds[kind]) for kind in spaces]
    return pl.pallas_call(
        kernel,
        out_shape=tuple(outs),
        in_specs=specs[: len(args)],
        out_specs=tuple(specs[len(args) :]),
        scratch_shapes=list(scratch),
        compiler_params=pltpu.CompilerParams(vmem_limit_bytes=(60 if wide else vmem or VM[3]) * 1024 * 1024),
        cost_estimate=pl.CostEstimate(flops=int(us * COST), bytes_accessed=0, transcendentals=0),
    )(*args)


def shape(dims, kind=f32):
    return jax.ShapeDtypeStruct(tuple(dims), kind)


def room(values):
    return pltpu.VMEM(values.shape, values.dtype)


def loads(refs, rooms, sems):
    return [pltpu.make_async_copy(ref, place, sems.at[i]) for i, (ref, place) in enumerate(zip(refs, rooms))]


def bias_kernel(doc_length, rank_ref, table_ref, doc_bias_ref, slot_bias_ref, line_ref):
    pairs = doc_bias_ref.shape[0]
    parts = doc_length // LANES
    length = line_ref.shape[1]
    offset = lax.broadcasted_iota(jnp.int32, (BUCKETS, length), 1) - doc_length
    hot = (bucket_index(offset) == lax.broadcasted_iota(jnp.int32, (BUCKETS, length), 0)).astype(f32)
    line_ref[...] = lax.dot_general(
        table_ref[...], hot, (((0,), (0,)), ((), ())), precision=highest, preferred_element_type=f32
    )
    narrow = rank_ref[0] & (parts - 1)

    def spread(head, start):
        line = line_ref[pl.ds(head, 1), pl.ds(pl.multiple_of(start, LANES), 2 * LANES)]
        rolled = pltpu.roll(jnp.broadcast_to(line, (LANES, 2 * LANES)), 0, 1, stride=1, stride_axis=0)
        return rolled[:, LANES:]

    def one_pair(pair, carry):
        for side in range(2):
            rows = slice(side * LANES, (side + 1) * LANES)
            head = 2 * pair + side
            for part in range(parts):
                distance = (narrow ^ part) - narrow
                doc_bias_ref[pair, rows, part * LANES : (part + 1) * LANES] = spread(
                    head, doc_length - LANES + distance * LANES
                )
            slot_bias_ref[pair, rows, :] = spread(head, doc_length - LANES)
        return carry

    lax.fori_loop(0, pairs, one_pair, 0)


def count_kernel(doc_length, doc_total, rank_ref, picked_ref, counts_ref, tally_ref, load_ref, places_ref, scratch_ref, sem):
    slots, slot_length, picks = load_ref.shape
    rows = slots * slot_length
    blocks = counts_ref.shape[0]
    narrow_size = picked_ref.shape[0] // slots
    first = (rank_ref[0] & (narrow_size - 1)) * slots
    load = pltpu.make_async_copy(picked_ref.at[pl.ds(first, slots)], load_ref, sem)
    load.start()
    load.wait()

    places_ref[...] = load_ref[...].reshape(rows, picks)

    def one_row(row, carry):
        places = places_ref[pl.ds(row, 1), :]
        high = places >> 7
        low = places & 127
        high_hot = (lax.broadcasted_iota(jnp.int32, (blocks, picks), 0) == high).astype(bf16)
        low_hot = (lax.broadcasted_iota(jnp.int32, (LANES, picks), 0) == low).astype(bf16)
        scratch_ref[pl.ds(row, blocks, stride=rows), :] = right_product(high_hot, low_hot)
        return carry

    lax.fori_loop(0, rows, one_row, 0, unroll=8)

    def one_block(block, carry):
        start = pl.multiple_of(block * rows, rows)
        counts_ref[block] = scratch_ref[pl.ds(start, rows), :].astype(bf16)
        return carry

    lax.fori_loop(0, blocks, one_block, 0, unroll=4)

    owner = places_ref[...] // doc_length
    lane = lax.broadcasted_iota(jnp.int32, (rows, LANES), 1)
    tally = jnp.zeros((rows, LANES), f32)
    for doc in range(doc_total):
        number = jnp.sum((owner == doc).astype(f32), 1, keepdims=True)
        tally = jnp.where(lane == doc, number, tally)
    tally_ref[...] = tally


def rms_scale(values):
    return lax.rsqrt(jnp.mean(values * values, -1, keepdims=True) + epsilon)


def rms_back(values, gain, grad):
    scale = rms_scale(values)
    weighted = grad * gain
    inner = jnp.mean(weighted * values, -1, keepdims=True)
    return scale * weighted - values * (scale * scale * scale * inner)


def tile(index, size=LANES):
    return pl.ds(pl.multiple_of(index * size, size), size)


def halves(values, zero_row):
    return jnp.concatenate([jnp.where(zero_row, values, jnp.zeros((), values.dtype)),
                            jnp.where(zero_row, jnp.zeros((), values.dtype), values)], 0)


def joined(values, first_lanes):
    rows = values.shape[0] // 2
    return jnp.where(first_lanes, values[:rows], values[rows:])


def forward_kernel(
    slots, slot_length, rank_ref, lengths_ref, queries_ref, own_ref, near_ref, far_ref, last_ref, doc_bias_ref,
    slot_bias_ref, attend_gain_ref, feed_gain_ref, final_gain_ref,
    wq_ref, wk_ref, wv_ref, wo_ref, wg_ref, wu_ref, wd_ref, wp_ref,
    all_ref, query_ref, key_ref, value_ref, doc_probs_ref, slot_probs_ref, mixed_ref, after_attend_ref,
    normed_feed_ref, hidden_ref, gate_slope_ref, up_slope_ref, after_feed_ref, normed_final_ref, embed_ref,
    slot_unit_ref, doc_unit_ref,
    slot_ref, slot_sem,
):
    slot_rows = slots * slot_length
    rows, width = query_ref.shape
    pairs = doc_probs_ref.shape[0]
    half = LANES // 2
    narrow_size = queries_ref.shape[0] // slots
    first = (rank_ref[0] & (narrow_size - 1)) * slots
    load_slots = pltpu.make_async_copy(queries_ref.at[pl.ds(first, slots)], slot_ref, slot_sem)
    load_slots.start()
    gain = attend_gain_ref[...].reshape(1, width)
    place = slot_rows
    for ref in (own_ref, near_ref, far_ref, last_ref):
        tokens = ref[...].astype(f32)
        all_ref[place : place + ref.shape[0], :] = (tokens * rms_scale(tokens) * gain).astype(bf16)
        place += ref.shape[0]
    load_slots.wait()
    slot_tokens = slot_ref[...].reshape(slot_rows, width).astype(f32)
    all_ref[:slot_rows, :] = (slot_tokens * rms_scale(slot_tokens) * gain).astype(bf16)
    normed = all_ref[:rows, :]
    query_ref[...] = product(normed, wq_ref[...]).astype(bf16)
    key_ref[...] = product(all_ref[...], wk_ref[...]).astype(bf16)
    value_ref[...] = product(all_ref[...], wv_ref[...]).astype(bf16)

    lane = lax.broadcasted_iota(jnp.int32, (slot_rows, LANES), 1)
    row = lax.broadcasted_iota(jnp.int32, (slot_rows, slot_rows), 0)
    col = lax.broadcasted_iota(jnp.int32, (slot_rows, slot_rows), 1)
    slot_keep = row < 0
    for slot in range(slots):
        start = slot * slot_length
        inside = (row >= start) & (row < start + slot_length) & (col >= start)
        slot_keep = slot_keep | (inside & (col < start + lengths_ref[first + slot]))

    def softmax(scores):
        weights = jnp.exp(scores - jnp.max(scores, -1, keepdims=True))
        return (weights * (1.0 / jnp.sum(weights, -1, keepdims=True))).astype(bf16)

    first_lanes = lane < half
    pair_keep = jnp.concatenate([slot_keep, slot_keep], 0)

    def one_pair(pair, carry):
        lanes = tile(pair)
        slot_query = halves(query_ref[:slot_rows, lanes], first_lanes)
        scores = right_product(slot_query, key_ref[:slot_rows, lanes]) + slot_bias_ref[pair]
        probs = softmax(jnp.where(pair_keep, scores, masked_value))
        slot_probs_ref[pair] = probs
        slot_mixed = product(probs, value_ref[:slot_rows, lanes])
        mixed_ref[:slot_rows, lanes] = joined(slot_mixed, first_lanes).astype(bf16)
        doc_query = halves(query_ref[slot_rows:, lanes], first_lanes)
        scores = right_product(doc_query, key_ref[slot_rows:, lanes]) + doc_bias_ref[pair]
        probs = softmax(scores)
        doc_probs_ref[pair] = probs
        doc_mixed = product(probs, value_ref[slot_rows:, lanes])
        mixed_ref[slot_rows:, lanes] = joined(doc_mixed, first_lanes).astype(bf16)
        return carry

    lax.fori_loop(0, pairs, one_pair, 0, unroll=2)

    attended = product(mixed_ref[...], wo_ref[...])
    after_attend_ref[:slot_rows, :] = slot_ref[...].reshape(slot_rows, width).astype(f32) + attended[:slot_rows]
    after_attend_ref[slot_rows:, :] = own_ref[...].astype(f32) + attended[slot_rows:]
    after_attend = after_attend_ref[...]
    feed_gain = feed_gain_ref[...].reshape(1, width)
    normed_feed_ref[...] = (after_attend * rms_scale(after_attend) * feed_gain).astype(bf16)

    def one_part(step, carry):
        part = tile(step, CHUNK)
        gate = product(normed_feed_ref[...], wg_ref[:, part])
        upward = product(normed_feed_ref[...], wu_ref[:, part])
        factor = 0.7978845608028654
        square = gate * gate
        bent = jnp.tanh(factor * gate * (1.0 + 0.044715 * square))
        curve = 0.5 * gate * (1.0 + bent)
        slope = 0.5 * (1.0 + bent) + 0.5 * factor * gate * (1.0 - bent * bent) * (1.0 + 3 * 0.044715 * square)
        hidden_ref[:, part] = (curve * upward).astype(bf16)
        gate_slope_ref[:, part] = (upward * slope).astype(bf16)
        up_slope_ref[:, part] = curve.astype(bf16)
        return carry

    lax.fori_loop(0, hidden_ref.shape[1] // CHUNK, one_part, 0, unroll=2)
    after_feed = after_attend_ref[...] + product(hidden_ref[...], wd_ref[...])
    after_feed_ref[...] = after_feed
    final_gain = final_gain_ref[...].reshape(1, width)
    normed_final = (after_feed * rms_scale(after_feed) * final_gain).astype(bf16)
    normed_final_ref[...] = normed_final
    embed = product(normed_final, wp_ref[...])
    embed_ref[...] = embed
    unit = (embed * lax.rsqrt(jnp.sum(embed * embed, -1, keepdims=True) + epsilon)).astype(bf16)
    slot_unit_ref[...] = unit[:slot_rows]
    doc_unit_ref[...] = unit[slot_rows:]


def loss_kernel(
    order, gathered, doc_total, slots, rank_ref, lengths_ref, positives_ref, counts_ref, near_ref, far_ref, unit_ref,
    tally_ref, losses_ref, grad_ref, kept_ref, sent_ref, sum_ref, scaled_ref,
):
    rows = unit_ref.shape[0]
    blocks = counts_ref.shape[0]
    per_doc = blocks // doc_total
    rank = rank_ref[0]
    half = blocks // 2
    sum_ref[...] = jnp.zeros_like(sum_ref)

    def gather_step(place, carry):
        near = rank ^ gather_order(place, gathered)
        far = near ^ (1 << gathered[-1])
        sum_ref[near // per_doc] += product(counts_ref[near], near_ref[place])
        sum_ref[far // per_doc] += product(counts_ref[far], far_ref[place])
        return carry

    lax.fori_loop(0, half, gather_step, 0, unroll=4)

    unit = unit_ref[...].astype(f32)
    lane = lax.broadcasted_iota(jnp.int32, (rows, LANES), 1)
    summed = jnp.zeros((rows, LANES), f32)
    for doc in range(doc_total):
        number = jnp.sum(sum_ref[doc] * unit, 1, keepdims=True)
        summed = jnp.where(lane == doc, number, summed)
    tally = tally_ref[...]
    most = jnp.maximum(tally, 1.0)
    slot_length = rows // slots
    narrow_size = lengths_ref.shape[0] // slots
    first = (rank & (narrow_size - 1)) * slots
    row = lax.broadcasted_iota(jnp.int32, (rows, LANES), 0)
    slot_row = lax.broadcasted_iota(jnp.int32, (slots, LANES), 0)
    valid = row < 0
    positive = jnp.zeros((slots, LANES), jnp.int32)
    for slot in range(slots):
        start = slot * slot_length
        valid = valid | ((row >= start) & (row < start + lengths_ref[first + slot]))
        positive = jnp.where(slot_row == slot, positives_ref[first + slot], positive)
    weight = jnp.where(valid, jnp.minimum(tally, 1.0), 0.0)
    pooled = (weight * (summed / most)).reshape(slots, slot_length, LANES)
    weight_sum = jnp.maximum(jnp.sum(weight.reshape(slots, slot_length, LANES), 1), 1.0)
    scores = jnp.sum(pooled, 1) / weight_sum / contrastive_sharpness_factor
    slot_lane = lax.broadcasted_iota(jnp.int32, (slots, LANES), 1)
    inside = slot_lane < doc_total
    scores = jnp.where(inside, scores, -jnp.inf)
    top = jnp.max(scores, -1, keepdims=True)
    powers = jnp.exp(scores - top)
    total = jnp.sum(powers, -1, keepdims=True)
    chosen = (slot_lane == positive).astype(f32)
    picked = jnp.sum(jnp.where(slot_lane == positive, scores, 0.0), -1, keepdims=True)
    losses_ref[...] = jnp.broadcast_to(top + jnp.log(total) - picked, (slots, LANES))
    slope = (powers / total - chosen) / contrastive_sharpness_factor / weight_sum
    slope = jnp.where(inside, slope, 0.0)
    slope = jnp.broadcast_to(slope[:, None, :], (slots, slot_length, LANES)).reshape(rows, LANES)
    slope = slope * weight / most

    grad = jnp.zeros((rows, unit.shape[1]), f32)
    for doc in range(doc_total):
        column = jnp.sum(jnp.where(lane == doc, slope, 0.0), 1, keepdims=True)
        grad = grad + column * sum_ref[doc]
        scaled_ref[doc] = (column * unit).T.astype(bf16)
    grad_ref[...] = grad

    def scatter_step(place, carry):
        kept = rank ^ scatter_order(place, order)
        sent = kept ^ (1 << order[0])
        kept_ref[place] = product(scaled_ref[kept // per_doc], counts_ref[kept]).astype(bf16)
        sent_ref[place] = product(scaled_ref[sent // per_doc], counts_ref[sent]).astype(bf16)
        return carry

    lax.fori_loop(0, half, scatter_step, 0, unroll=4)


def feed_back(
    part, grad_unit, embed_ref, after_feed_ref, after_attend_ref, gate_slope_ref, up_slope_ref, feed_gain_ref,
    final_gain_ref, wo_ref, wg_ref, wu_ref, wd_ref, wp_ref, grads_out, after_out, mixed_out, more_ref,
):
    units, width = wd_ref.shape
    up_start, feed_start = units, 2 * units
    attend_start, embed_start = 2 * units + width, 2 * units + 2 * width
    embed = embed_ref[part, :]
    scale = lax.rsqrt(jnp.sum(embed * embed, -1, keepdims=True) + epsilon)
    inner = jnp.sum(grad_unit * embed, -1, keepdims=True)
    grad_embed = (scale * grad_unit - embed * (scale * scale * scale * inner)).astype(bf16)
    grads_out[:, embed_start : embed_start + embed.shape[1]] = grad_embed
    grad_after_feed = rms_back(
        after_feed_ref[part, :], final_gain_ref[...].reshape(1, -1), right_product(grad_embed, wp_ref[...])
    )
    after_out[...] = grad_after_feed
    grad_feed = grad_after_feed.astype(bf16)
    grads_out[:, feed_start:attend_start] = grad_feed
    def one_part(step, total):
        cols = tile(step, CHUNK)
        grad_hidden = right_product(grads_out[:, feed_start:attend_start], wd_ref[cols, :])
        grad_gate = (grad_hidden * gate_slope_ref[part, cols].astype(f32)).astype(bf16)
        grad_up = (grad_hidden * up_slope_ref[part, cols].astype(f32)).astype(bf16)
        grads_out[:, cols] = grad_gate
        grads_out[:, pl.ds(pl.multiple_of(up_start + step * CHUNK, CHUNK), CHUNK)] = grad_up
        more_ref[...] += right_product(grad_gate, wg_ref[:, cols]) + right_product(grad_up, wu_ref[:, cols])
        return total

    more_ref[...] = jnp.zeros_like(more_ref)
    lax.fori_loop(0, units // CHUNK, one_part, 0, unroll=2)
    total = more_ref[...]
    more = rms_back(after_attend_ref[part, :], feed_gain_ref[...].reshape(1, -1), total)
    grad_after_attend = after_out[...] + more
    after_out[...] = grad_after_attend
    grad_attend = grad_after_attend.astype(bf16)
    grads_out[:, attend_start:embed_start] = grad_attend
    mixed_out[...] = right_product(grad_attend, wo_ref[...]).astype(bf16)


def attend_back(
    far_parts, queries, keys, query_ref, key_ref, value_ref, probs_ref, mixed_ref, query_out, key_out, value_out,
    sums_out,
):
    rows = mixed_ref.shape[0]
    length = probs_ref.shape[2]
    half = LANES // 2
    first_lanes = lax.broadcasted_iota(jnp.int32, (rows, LANES), 1) < half
    row = lax.broadcasted_iota(jnp.int32, (rows, rows), 0)
    col = lax.broadcasted_iota(jnp.int32, (rows, rows), 1)
    flip = (row + col == rows - 1).astype(bf16)
    nothing = jnp.zeros((rows, LANES), f32)

    def one_pair(pair, carry):
        lanes = tile(pair)
        grad_mixed = halves(mixed_ref[:, lanes], first_lanes)
        query = halves(query_ref[queries, lanes], first_lanes)
        probs = probs_ref[pair]
        grad_probs = right_product(grad_mixed, value_ref[keys, lanes])
        exact = probs.astype(f32)
        inner = jnp.sum(exact * grad_probs, -1, keepdims=True)
        grad_scores = (exact * (grad_probs - inner)).astype(bf16)
        query_out(joined(product(grad_scores, key_ref[keys, lanes]), first_lanes).astype(bf16), pair)
        key_out(left_product(grad_scores, query).astype(bf16), pair)
        value_out(left_product(probs, grad_mixed).astype(bf16), pair)
        for side in range(2):
            head = 2 * pair + side
            own = grad_scores[side * rows : (side + 1) * rows, :]
            for part in range(length // LANES):
                piece = own[:, part * LANES : (part + 1) * LANES]
                if part in far_parts:
                    line = jnp.concatenate([piece.astype(f32), nothing], 1)
                else:
                    line = pltpu.roll(
                        jnp.concatenate([product(flip, piece), nothing], 1), 0, 1, stride=1, stride_axis=0
                    )
                sums_out[tile(head, 8), part * 2 * LANES : (part + 1) * 2 * LANES] = jnp.sum(
                    line.reshape(rows // 8, 8, 2 * LANES), 0
                )
        return carry

    lax.fori_loop(0, probs_ref.shape[0], one_pair, 0, unroll=2)


def input_back(tokens, gain_ref, after_ref, query, key, value, wq_ref, wk_ref, wv_ref):
    grad_normed = right_product(query, wq_ref[...])
    grad_normed = grad_normed + right_product(key, wk_ref[...])
    grad_normed = grad_normed + right_product(value, wv_ref[...])
    return after_ref[...] + rms_back(tokens, gain_ref[...].reshape(1, -1), grad_normed)


def table_sums(sums_ref, distances):
    heads = sums_ref.shape[0] // 8
    span = lax.broadcasted_iota(jnp.int32, (2 * LANES, LANES), 0) - (LANES - 1)
    bucket = lax.broadcasted_iota(jnp.int32, (2 * LANES, LANES), 1)
    total = jnp.zeros((heads, LANES), f32)
    for part, distance in enumerate(distances):
        lines = jnp.sum(sums_ref[:, part * 2 * LANES : (part + 1) * 2 * LANES].reshape(heads, 8, 2 * LANES), 1)
        hot = (bucket_index(span + distance * LANES) == bucket).astype(f32)
        total = total + lax.dot_general(
            lines, hot, (((1,), (0,)), ((), ())), precision=highest, preferred_element_type=f32
        )
    return total


def slot_feed_kernel(
    grad_unit_ref, embed_ref, after_feed_ref, after_attend_ref, gate_slope_ref, up_slope_ref, feed_gain_ref,
    final_gain_ref, wp_ref, wd_ref, wg_ref, wu_ref, wo_ref,
    grads_out, after_out, mixed_out, more_ref,
):
    feed_back(
        slice(0, after_out.shape[0]), grad_unit_ref[...], embed_ref, after_feed_ref, after_attend_ref,
        gate_slope_ref, up_slope_ref, feed_gain_ref, final_gain_ref, wo_ref, wg_ref, wu_ref, wd_ref, wp_ref, grads_out,
        after_out, mixed_out, more_ref,
    )


def slot_attend_kernel(
    query_ref, key_ref, value_ref, probs_ref, mixed_ref, grads_out, table_out, sums_ref
):
    rows, width = mixed_ref.shape

    def out(place):
        def store(values, pair):
            grads_out[:, pl.ds(pl.multiple_of(place * width + pair * LANES, LANES), LANES)] = values

        return store

    part = slice(0, rows)
    attend_back(
        (), part, part, query_ref, key_ref, value_ref, probs_ref, mixed_ref, out(0), out(1), out(2), sums_ref
    )
    table_out[...] = table_sums(sums_ref, [0])


def doc_feed_kernel(came, *refs):
    parts, refs = refs[:came], refs[came:]
    (
        embed_ref, after_feed_ref, after_attend_ref, gate_slope_ref, up_slope_ref, feed_gain_ref, final_gain_ref,
        wp_ref, wd_ref, wg_ref, wu_ref, wo_ref,
        grads_out, after_out, mixed_out, more_ref,
    ) = refs
    rows = after_out.shape[0]
    grad_unit = add(*(part[0] for part in parts)).T
    feed_back(
        slice(embed_ref.shape[0] - rows, embed_ref.shape[0]), grad_unit, embed_ref, after_feed_ref,
        after_attend_ref, gate_slope_ref, up_slope_ref, feed_gain_ref, final_gain_ref, wo_ref, wg_ref, wu_ref, wd_ref,
        wp_ref, grads_out, after_out, mixed_out, more_ref,
    )


def doc_attend_kernel(
    rank_ref, query_ref, key_ref, value_ref, probs_ref, mixed_ref, slot_table_ref, grads_out, table_out, query_room,
    sums_ref,
):
    rows, width = query_room.shape
    length = probs_ref.shape[2]
    first = key_ref.shape[0] - length

    def query_out(values, pair):
        query_room[:, tile(pair)] = values

    def key_out(values, pair):
        grads_out[:length, tile(pair)] = values

    def value_out(values, pair):
        grads_out[:length, pl.ds(pl.multiple_of(width + pair * LANES, LANES), LANES)] = values

    attend_back(
        (2,), slice(first, first + rows), slice(first, key_ref.shape[0]), query_ref, key_ref, value_ref, probs_ref,
        mixed_ref, query_out, key_out, value_out, sums_ref,
    )
    grads_out[length:, :width] = query_room[: rows // 2, :]
    grads_out[length:, width:] = query_room[rows // 2 :, :]
    parts = length // LANES
    narrow = rank_ref[0] & (parts - 1)
    table = table_sums(sums_ref, [(narrow ^ part) - narrow for part in range(parts)]) + slot_table_ref[...]
    heads = table.shape[0]
    table_out[...] = jnp.concatenate([table, jnp.zeros((16 - heads, LANES), f32)], 0).astype(bf16)


def pick_columns(values, total, order, flipped, rank):
    count = 1 << len(order) + 1
    size = total // count
    row = lax.broadcasted_iota(jnp.int32, (total, total // 2), 0)
    col = lax.broadcasted_iota(jnp.int32, (total, total // 2), 1)
    source = (scatter_order(col // size, order) ^ rank ^ flipped) * size + col % size
    return product(values, (row == source).astype(bf16)).astype(bf16)


def pick_tiles(values_ref, order, flipped, rank, store):
    rows = values_ref.shape[0]
    half = LANES // 2
    first_lanes = lax.broadcasted_iota(jnp.int32, (rows, LANES), 1) < half
    upper = ((rank ^ flipped) & 1) == 1

    def one_tile(step, carry):
        place = 2 * step
        sides = []
        for side in range(2):
            tile = (rank ^ scatter_order(place + side, order)) >> 1
            values = values_ref[:, pl.ds(pl.multiple_of(tile * LANES, LANES), LANES)].astype(f32)
            turned = pltpu.roll(values, half, 1)
            sides.append(jnp.where(upper, turned, values) if side == 0 else jnp.where(upper, values, turned))
        store(step, jnp.where(first_lanes, sides[0], sides[1]).astype(bf16))
        return carry

    lax.fori_loop(0, 1 << len(order) - 1, one_tile, 0)


def turn_kernel(
    orders, rank_ref, all_ref, normed_feed_ref, mixed_ref, normed_final_ref, hidden_ref, kept_out, sent_out, doc_out,
):
    first, second, third, fourth = orders
    rank = rank_ref[0]
    rows, width = normed_feed_ref.shape
    units = hidden_ref.shape[1]
    slots = all_ref.shape[0] - doc_out.shape[0]
    half = width // 2
    for out, flipped in ((kept_out, 0), (sent_out, 1)):
        out[:, :half] = pick_columns(normed_feed_ref[...], width, first, flipped, rank)
        out[:, half : 2 * half] = pick_columns(normed_feed_ref[...], width, second, flipped, rank)
        out[:, 2 * half : 3 * half] = pick_columns(mixed_ref[...], width, first, flipped, rank)
        out[:, 3 * half : 4 * half] = pick_columns(normed_final_ref[...], width, second, flipped, rank)
        start = 4 * half
        if units >> (len(third) + 1) == LANES // 2:

            def store(place, values):
                out[:, pl.ds(pl.multiple_of(start + place * LANES, LANES), LANES)] = values

            pick_tiles(hidden_ref, third, flipped, rank, store)
        else:
            out[:, start : start + units // 2] = pick_columns(hidden_ref[...], units, third, flipped, rank)
        start = start + units // 2
        out[slots:, start:] = jnp.zeros((rows - slots, half), bf16)
        if flipped:
            out[:slots, start:] = pick_columns(all_ref[:slots, :], width, fourth, flipped, rank)
        else:
            both = pick_columns(all_ref[...], width, fourth, flipped, rank)
            out[:slots, start:] = both[:slots]
            doc_out[...] = both[slots:]


def store_product(left, right_ref, columns, kept_ref, sent_ref, start):
    half = left.shape[1] // 2
    size = 2 * LANES

    def one_part(first, size):
        here = pl.ds(pl.multiple_of(start + first, LANES), size)
        result = left_product(left, right_ref[:, pl.ds(pl.multiple_of(first, LANES), size)]).astype(bf16)
        kept_ref[:half, here] = result[:half]
        sent_ref[:half, here] = result[half:]

    def step(place, carry):
        one_part(place * size, size)
        return carry

    lax.fori_loop(0, columns // size, step, 0, unroll=2)
    if columns % size:
        one_part(columns // size * size, columns % size)


def weight_kernel(
    terms, kept_any, came_any, slot_any, slot_came_any, doc_any, doc_came_any, kept_ref, sent_ref, left_ref, right_ref,
    sems,
):
    rows = kept_any.shape[0]
    part = slot_any.shape[0]
    copies = []
    left_place, right_place = 0, 0
    for left_start, left_width, right_start, right_width in terms:
        pieces = []
        for place, ref in enumerate((kept_any, came_any)):
            source = ref.at[:, left_start : left_start + left_width]
            target = left_ref.at[place * rows : (place + 1) * rows, left_place : left_place + left_width]
            pieces.append((source, target))
        for place, ref in enumerate((slot_any, doc_any, slot_came_any, doc_came_any)):
            source = ref.at[:, right_start : right_start + right_width]
            target = right_ref.at[place * part : (place + 1) * part, right_place : right_place + right_width]
            pieces.append((source, target))
        first = sum(len(group) for group in copies)
        copies.append(
            [pltpu.make_async_copy(one, two, sems.at[first + i]) for i, (one, two) in enumerate(pieces)]
        )
        left_place += left_width
        right_place += right_width
    for group in copies:
        for copy in group:
            copy.start()
    left_place, right_place = 0, 0
    for group, (_, left_width, _, right_width) in zip(copies, terms):
        for copy in group:
            copy.wait()
        left = left_ref[:, left_place : left_place + left_width]
        right = right_ref.at[:, right_place : right_place + right_width]
        store_product(left, right, right_width, kept_ref, sent_ref, right_place)
        left_place += left_width
        right_place += right_width


def attend_weight_kernel(
    doc_ref, kept_any, came_any, slot_any, slot_came_any, grads_ref, other_ref, table_ref, other_table_ref,
    kept_out, sent_out, pair_kept, pair_sent, slot_room, slot_came_room, left_ref, right_ref, query_ref, sems,
):
    rows = slot_any.shape[0]
    width = slot_room.shape[1] // 3
    half = doc_ref.shape[1]
    length = doc_ref.shape[0]
    lanes = slice(kept_any.shape[1] - half, kept_any.shape[1])
    copies = loads(
        (slot_any, slot_came_any, kept_any.at[:rows, lanes], came_any.at[:rows, lanes]),
        (slot_room, slot_came_room, left_ref.at[length : length + rows, :], left_ref.at[length + rows :, :]),
        sems,
    )
    for copy in copies:
        copy.start()
    left_ref[:length, :] = doc_ref[...]
    for part in range(length // LANES):
        here = slice(part * LANES, (part + 1) * LANES)
        there = slice((part ^ 1) * LANES, ((part ^ 1) + 1) * LANES)
        right_ref[here, :] = add(grads_ref[here, :], other_ref[there, :]).astype(bf16)
    pair_kept[...] = right_ref[:LANES, :]
    pair_sent[...] = right_ref[2 * LANES : 3 * LANES, :]
    small = LANES // 2
    for place, ref in enumerate((grads_ref, other_ref)):
        query_ref[2 * place * small : (2 * place + 1) * small, :] = ref[length:, :width]
        query_ref[(2 * place + 1) * small : (2 * place + 2) * small, :] = ref[length:, width:]
    for copy in copies:
        copy.wait()
    right_ref[length : length + rows, :] = slot_room[:, width:]
    right_ref[length + rows :, :] = slot_came_room[:, width:]
    query_ref[2 * LANES : 2 * LANES + rows, :] = slot_room[:, :width]
    query_ref[2 * LANES + rows :, :] = slot_came_room[:, :width]
    store_product(left_ref[...], right_ref, 2 * width, kept_out, sent_out, width)
    left = jnp.concatenate([left_ref[: 2 * LANES, :], left_ref[length:, :]], 0)
    store_product(left, query_ref, width, kept_out, sent_out, 0)
    tail = sent_out.shape[0] - 16
    sent_out[tail:, :] = jnp.zeros((16, sent_out.shape[1]), bf16)
    sent_out[tail:, :LANES] = add(table_ref[...], other_table_ref[...]).astype(bf16)


def doc_input_kernel(
    tokens_ref, gain_ref, after_ref, grads_ref, kept_ref, came_ref, wq_ref, wk_ref, wv_ref, tokens_out
):
    rows, width = tokens_ref.shape
    rest = grads_ref.shape[0] - rows // 2
    query = jnp.concatenate([grads_ref[rest:, :width], grads_ref[rest:, width:]], 0)
    pair = add(kept_ref[...], came_ref[...]).astype(bf16)
    tokens_out[...] = input_back(
        tokens_ref[...].astype(f32), gain_ref, after_ref, query, pair[:, :width], pair[:, width:], wq_ref, wk_ref, wv_ref
    )


def slot_input_kernel(
    slots, rank_ref, tokens_any, gain_ref, after_ref, grads_ref, wq_ref, wk_ref, wv_ref, tokens_out, slot_room, sem
):
    narrow_size = tokens_any.shape[0] // slots
    first = (rank_ref[0] & (narrow_size - 1)) * slots
    load = pltpu.make_async_copy(tokens_any.at[pl.ds(first, slots)], slot_room, sem)
    load.start()
    load.wait()
    width = tokens_out.shape[1]
    query, key, value = (grads_ref[:, place * width : (place + 1) * width] for place in range(3))
    tokens_out[...] = input_back(
        slot_room[...].reshape(tokens_out.shape).astype(f32), gain_ref, after_ref, query, key, value, wq_ref, wk_ref,
        wv_ref,
    )


def on_device(
    doc_tokens, query_tokens, query_lengths, positive_docs, retrieved, attend_gain, query_weight, key_weight,
    value_weight, output_weight, bias_table, feed_gain, gate_weight, up_weight, down_weight, final_gain, proj_weight,
):
    narrow_size = lax.axis_size("narrow")
    bits = rank_bits()
    rank = my_rank()
    rank_word = rank.astype(jnp.int32).reshape(1)
    doc_rows, width = doc_tokens.shape[1:]
    doc_length = doc_rows * narrow_size
    doc_total = doc_tokens.shape[0] * lax.axis_size("wide")
    slots = query_tokens.shape[0] // narrow_size
    slot_length = query_tokens.shape[1]
    heads = bias_table.shape[1]
    units = gate_weight.shape[1]
    columns = proj_weight.shape[1]
    slot_rows = slots * slot_length
    rows = slot_rows + doc_rows
    blocks = doc_total * doc_length // LANES
    assert doc_tokens.shape[0] == 1 and doc_rows == LANES and slot_rows == LANES and narrow_size == 4
    assert columns == LANES and doc_total <= LANES and blocks == 1 << bits
    gains = (attend_gain, feed_gain, final_gain)
    dma = pltpu.SemaphoreType.DMA
    waxes = list(range(3, bits))

    orders = (
        waxes[:1] + [2] + [1] + waxes[1:],
        [1] + [2] + waxes[:1] + waxes[1:],
        waxes[:1] + [2] + [1] + waxes[1:],
        [2] + [1] + waxes[:1] + waxes[1:],
    )
    own_tokens = doc_tokens[0]
    y_tokens = swap(own_tokens, 2)
    core_tokens = swap(own_tokens, 1)
    pairs = heads // 2
    doc_bias, slot_bias = call(
        functools.partial(bias_kernel, doc_length),
        [shape((pairs, 2 * doc_rows, doc_length)), shape((pairs, 2 * slot_rows, slot_rows))],
        [rank_word, bias_table],
        "s",
        [pltpu.VMEM((heads, 2 * doc_length + LANES), f32)],
    )
    counts, tally = call(
        functools.partial(count_kernel, doc_length, doc_total),
        [shape((blocks, slot_rows, LANES), bf16), shape((slot_rows, LANES))],
        [rank_word, after(retrieved, slot_bias)],
        "sa",
        [
            pltpu.VMEM((slots, slot_length, retrieved.shape[2]), jnp.int32),
            pltpu.VMEM((slot_rows, retrieved.shape[2]), jnp.int32),
            pltpu.VMEM((blocks * slot_rows, LANES), f32),
            dma,
        ],
        us=5,
        wide=bits > 5,
    )
    y_tokens = after(y_tokens, doc_bias, tally)
    both_tokens = swap(y_tokens, 1)

    all_rows = slot_rows + doc_length
    forward_shapes = [
        shape((all_rows, width), bf16),
        shape((rows, width), bf16),
        shape((all_rows, width), bf16),
        shape((all_rows, width), bf16),
        shape((pairs, 2 * doc_rows, doc_length), bf16),
        shape((pairs, 2 * slot_rows, slot_rows), bf16),
        shape((rows, width), bf16),
        shape((rows, width)),
        shape((rows, width), bf16),
        shape((rows, units), bf16),
        shape((rows, units), bf16),
        shape((rows, units), bf16),
        shape((rows, width)),
        shape((rows, width), bf16),
        shape((rows, columns)),
        shape((slot_rows, columns), bf16),
        shape((doc_rows, columns), bf16),
    ]
    weights = [
        query_weight, key_weight, value_weight, output_weight, gate_weight, up_weight, down_weight, proj_weight,
    ]
    slot_room = pltpu.VMEM((slots, slot_length, width), bf16)
    (
        all_normed, query, key, value, doc_probs, slot_probs, mixed, after_attend, normed_feed, hidden, gate_slope,
        up_slope, after_feed, normed_final, embed, slot_unit, doc_unit,
    ) = call(
        functools.partial(forward_kernel, slots, slot_length),
        forward_shapes,
        [
            rank_word, query_lengths, query_tokens, own_tokens, core_tokens, y_tokens, both_tokens, doc_bias, slot_bias,
            *gains, *weights,
        ],
        "ssa" + "v" * 9 + "v" * 8 + "v" * len(forward_shapes),
        [slot_room, dma],
        vmem=VM[0],
        us=18,
    )

    phases = [list(range(high, max(high - 2, 0), -1)) for high in range(bits - 1, 0, -2)]
    gathered = []
    near_units = doc_unit[None]
    for phase, group in enumerate(phases):
        group = group[::-1]
        masks = [gather_order(place, group) for place in range(1, 1 << len(group))]
        came = [swap(near_units, mask) for mask in masks]
        if phase == 0:
            pass
        if phase == 1:
            turned_cols = 5 * width // 2 + units // 2
            turned, turned_sent, turned_docs = call(
                functools.partial(turn_kernel, orders),
                [shape((rows, turned_cols), bf16)] * 2 + [shape((doc_length, width // 2), bf16)],
                after([rank_word, all_normed, normed_feed, mixed, normed_final, hidden], near_units),
                "s",
                us=5,
                wide=bits > 5,
            )
            came = after(came, turned)
        near_units = jnp.concatenate([near_units] + came, 0)
        gathered = gathered + group
    gathered = gathered + [0]
    far_units = swap(near_units, 1)

    order = list(range(bits))
    half = blocks // 2
    losses, grad_slot_unit, kept, sent = call(
        functools.partial(loss_kernel, order, gathered, doc_total, slots),
        [
            shape((slots, LANES)),
            shape((slot_rows, columns)),
            shape((half, columns, LANES), bf16),
            shape((half, columns, LANES), bf16),
        ],
        [rank_word, query_lengths, positive_docs, counts, near_units, far_units, slot_unit, tally],
        "sss",
        [
            pltpu.VMEM((doc_total, slot_rows, columns), f32),
            pltpu.VMEM((doc_total, columns, slot_rows), bf16),
        ],
        wide=bits > 5,
    )
    back_weights = [proj_weight, down_weight, gate_weight, up_weight, output_weight]
    doc_cols = 2 * units + 2 * width + columns

    came = [swap(sent, 1)]
    rest = order[1:]
    parts = [kept]
    phase = 0
    feed_shapes = [shape((LANES, doc_cols), bf16), shape((LANES, width)), shape((LANES, width), bf16)]
    while rest:
        group, rest = rest[:2], rest[2:]
        count = 1 << len(group)
        size = parts[0].shape[0] // count
        pieces = []
        for place in range(count):
            here = slice(place * size, (place + 1) * size)
            pieces.append(add(*(part[here] for part in parts), *(one[here] for one in came)).astype(bf16))
        masks = [scatter_order(place, group) for place in range(count)]
        came = [swap(piece, mask) for piece, mask in zip(pieces[1:], masks[1:])]
        parts = [pieces[0]]
        if phase == 0:
            slot_grads, slot_after, slot_mixed = call(
                slot_feed_kernel,
                feed_shapes,
                [after(grad_slot_unit, pieces[1])]
                + [embed, after_feed, after_attend, gate_slope, up_slope, gains[1], gains[2]]
                + back_weights,
                "",
                [pltpu.VMEM((slot_rows, width), f32)],
                vmem=VM[1],
                us=7,
            )
            came = after(came, slot_after)
        if phase == 1:
            slot_came = swap(after(slot_grads, *pieces[1:]), 1)
            turned_came = swap(after(turned_sent, *pieces[1:]), 1)
            slot_thirds, slot_table = call(
                slot_attend_kernel,
                [shape((slot_rows, 3 * width), bf16), shape((heads, LANES))],
                [query, key, value, slot_probs, after(slot_mixed, *pieces[1:])],
                scratch=[pltpu.VMEM((heads * 8, 2 * LANES), f32)],
                us=4,
            )
            came = after(came, slot_table)
        phase += 1

    doc_grads, doc_after, doc_mixed = call(
        functools.partial(doc_feed_kernel, 1 + len(came)),
        feed_shapes,
        parts + after(came, slot_came, turned_came)
        + [embed, after_feed, after_attend, gate_slope, up_slope, gains[1], gains[2]]
        + back_weights,
        "",
        [pltpu.VMEM((doc_rows, width), f32)],
        vmem=VM[2],
        us=7,
    )
    thirds_came = swap(after(slot_thirds, doc_after), 1)
    doc_came = swap(doc_grads, 1)

    class Stream:
        def __init__(self, kept, sent, order):
            self.kept, self.order, self.step = kept, order, 0
            self.loaded = sent.shape[0] > kept.shape[0]
            self.small = sent[-16:] if self.loaded else None
            self.send(sent)

        def send(self, sent):
            self.came = swap(sent, 1 << self.order[self.step])
            self.step += 1

        def advance(self, *wait):
            came = after(self.came, *wait)
            if self.step == len(self.order):
                if self.loaded:
                    self.small = add(self.small, came[-16:]).astype(bf16)
                    came = came[:-16]
                self.result = add(self.kept, came)
                return self.result
            self.kept, sent, self.small = cut(self.kept, came, self.small)
            self.send(sent)
            return self.kept

    def weight_product(terms, order, *wait):
        left = sum(term[1] for term in terms)
        right = sum(term[3] for term in terms)
        tall = terms[0][1] // 2
        args = after([turned, turned_came, slot_grads, slot_came, doc_grads, doc_came], *wait)
        kept, sent = call(
            functools.partial(weight_kernel, terms),
            [shape((tall, right), bf16)] * 2,
            args,
            "a" * 6,
            [pltpu.VMEM((2 * rows, left), bf16), pltpu.VMEM((2 * rows, right), bf16), dma((6 * len(terms),))],
        )
        return Stream(kept, sent, order)

    small_half = width // 2
    att_grads, table = call(
        doc_attend_kernel,
        [shape((doc_length + doc_rows // 2, 2 * width), bf16), shape((16, LANES), bf16)],
        [rank_word, query, key, value, doc_probs, doc_mixed, slot_table],
        "s",
        [pltpu.VMEM((doc_rows, width), bf16), pltpu.VMEM((heads * 8, 2 * doc_length), f32)],
    )
    att_came, table_came = swap(att_grads, 1), swap(table, 1)
    first = weight_product(
        [(0, small_half, 0, units), (2 * small_half, small_half, 2 * units + width, width)], orders[0], table
    )
    fourth_kept, fourth_sent, pair_kept, pair_sent = call(
        attend_weight_kernel,
        [
            shape((width // 4, 3 * width), bf16),
            shape((width // 4 + 16, 3 * width), bf16),
            shape((doc_rows, 2 * width), bf16),
            shape((doc_rows, 2 * width), bf16),
        ],
        [turned_docs, turned, turned_came, slot_thirds, thirds_came, att_grads, att_came, after(table, first.kept), table_came],
        "vaaaa",
        [
            pltpu.VMEM((slot_rows, 3 * width), bf16),
            pltpu.VMEM((slot_rows, 3 * width), bf16),
            pltpu.VMEM((doc_length + 2 * slot_rows, width // 2), bf16),
            pltpu.VMEM((doc_length + 2 * slot_rows, 2 * width), bf16),
            pltpu.VMEM((2 * doc_rows + 2 * slot_rows, width), bf16),
            dma((4,)),
        ],
    )
    fourth = Stream(fourth_kept, fourth_sent, orders[3])
    second = weight_product(
        [(small_half, small_half, units, units), (3 * small_half, small_half, 2 * units + 2 * width, columns)],
        orders[1],
        fourth_kept,
    )
    third = weight_product([(4 * small_half, units // 2, 2 * units, width)], orders[2], second.kept)
    def own_rows(values):
        return lax.dynamic_slice_in_dim(values, rank * (width >> bits), width >> bits, 0).astype(f32)

    def gain_grad(gain, *pairs):
        return sum(jnp.sum(own_rows(weight) * grad, 1) for weight, grad in pairs) / own_rows(gain)

    streams = {"A": first, "B": second, "C": third, "D": fourth}
    plan = "JADBACDpBADCBCIABDCfa"
    if bits != 5:
        plan = "J" + "ADBC" + "p" + "ADBC" * (bits - 3) + "I" + "ABfDaC"
    done = third.kept
    for event in plan:
        if event in streams:
            done = streams[event].advance(done)
        elif event == "p":
            pair_came = swap(after(pair_sent, done), 2)
        elif event == "f":
            gate_grad, output_grad = first.result[:, :units], first.result[:, units:]
            up_grad, proj_grad = second.result[:, :units], second.result[:, units:]
            feed_gain_grad = gain_grad(feed_gain, (gate_weight, gate_grad), (up_weight, up_grad))
            final_gain_grad = gain_grad(final_gain, (proj_weight, proj_grad))
            done = jnp.concatenate([feed_gain_grad, final_gain_grad])
            feed_gain_grad, final_gain_grad = done[: width >> bits], done[width >> bits :]
        elif event == "a":
            query_g, key_g, value_g = (fourth.result[:, place * width : (place + 1) * width] for place in range(3))
            done = gain_grad(attend_gain, (query_weight, query_g), (key_weight, key_g), (value_weight, value_g))
            attend_gain_grad = done
        elif event == "I":
            (done,) = call(
                doc_input_kernel,
                [shape((doc_rows, width))],
                [own_tokens, gains[0], doc_after, att_grads, pair_kept, after(pair_came, done)]
                + [query_weight, key_weight, value_weight],
                us=3,
            )
            doc_grad = done
        else:
            (done,) = call(
                functools.partial(slot_input_kernel, slots),
                [shape((slot_rows, width))],
                [rank_word, query_tokens, gains[0], slot_after, after(slot_thirds, done)]
                + [query_weight, key_weight, value_weight],
                "sa",
                [slot_room, dma],
                us=3,
            )
            query_grad = done
    return (
        losses[:, 0],
        doc_grad[None],
        query_grad.reshape(slots, slot_length, width),
        attend_gain_grad,
        query_g,
        key_g,
        value_g,
        output_grad,
        fourth.small[:heads, :BUCKETS].astype(f32).T,
        feed_gain_grad,
        gate_grad,
        up_grad,
        third.result,
        final_gain_grad,
        proj_grad,
    )


def solution(mesh):
    return jax.shard_map(
        on_device,
        mesh=mesh,
        in_specs=(
            P("wide", "narrow", None),
            P("wide", None, None),
            P("wide"),
            P("wide"),
            P("wide", None, None),
            P(),
            P(),
            P(),
            P(),
            P(),
            P(),
            P(),
            P(),
            P(),
            P(),
            P(),
            P(),
        ),
        out_specs=(
            P(("wide", "narrow")),
            P("wide", "narrow", None),
            P(("wide", "narrow"), None, None),
            P(("wide", "narrow")),
            P(("wide", "narrow"), None),
            P(("wide", "narrow"), None),
            P(("wide", "narrow"), None),
            P(("wide", "narrow"), None),
            P(),
            P(("wide", "narrow")),
            P(("wide", "narrow"), None),
            P(("wide", "narrow"), None),
            P(("wide", "narrow"), None),
            P(("wide", "narrow")),
            P(("wide", "narrow"), None),
        ),
        check_vma=False,
    )
```

```python
import functools

import jax
import jax.numpy as jnp
from jax import lax
from jax.experimental import pallas as pl
from jax.experimental.pallas import tpu as pltpu
from jax.sharding import PartitionSpec as P

BUCKETS = 32
LANES = 128
CHUNK = 512
VM = (12, 12, 12, 16, 8)
COST = 1.1e9

epsilon = 1e-06
contrastive_sharpness_factor = 0.01
masked_value = -1000000000.0
bucket_edges = (12, 16, 23, 32, 46, 64, 91)
highest = lax.Precision.HIGHEST
f32 = jnp.float32
bf16 = jnp.bfloat16


def bucket_index(offset):
    distance = jnp.abs(offset)
    beyond = 8 + sum(((distance >= boundary).astype(jnp.int32) for boundary in bucket_edges))
    inside = jnp.where(distance < 8, distance, beyond)
    return inside + BUCKETS // 2 * (offset > 0).astype(jnp.int32)


def product(left, right):
    return jnp.dot(left, right, preferred_element_type=f32)


def left_product(left, right):
    return lax.dot_general(left, right, (((0,), (0,)), ((), ())), preferred_element_type=f32)


def right_product(left, right):
    return lax.dot_general(left, right, (((1,), (1,)), ((), ())), preferred_element_type=f32)


def rank_bits():
    return (lax.axis_size("wide") * lax.axis_size("narrow")).bit_length() - 1


def my_rank():
    return lax.axis_index("wide") * lax.axis_size("narrow") + lax.axis_index("narrow")


def swap(values, mask):
    ranks = 1 << rank_bits()
    pairs = [(rank, rank ^ mask) for rank in range(ranks)]
    return lax.ppermute(values, ("wide", "narrow"), pairs)


def scatter_order(position, order):
    count = len(order)
    return sum(((position >> (count - 1 - step)) & 1) << bit for step, bit in enumerate(order))


def gather_order(position, order):
    return sum(((position >> step) & 1) << bit for step, bit in enumerate(order))


def after(values, *others):
    flat, tree = jax.tree.flatten(values)
    done = lax.optimization_barrier(tuple(flat) + tuple(others))
    return jax.tree.unflatten(tree, done[: len(flat)])


def add(*values):
    total = values[0].astype(f32)
    for value in values[1:]:
        total = total + value.astype(f32)
    return total


def cut_kernel(kept_ref, came_ref, kept_out, sent_out):
    half = kept_out.shape[0]
    kept_out[...] = add(kept_ref[:half, :], came_ref[:half, :]).astype(bf16)
    sent_out[...] = add(kept_ref[half:, :], came_ref[half:, :]).astype(bf16)


def cut_loaded_kernel(kept_ref, came_ref, small_ref, kept_out, sent_out, small_out):
    half = kept_out.shape[0]
    kept_out[...] = add(kept_ref[:half, :], came_ref[:half, :]).astype(bf16)
    sent_out[:half, :] = add(kept_ref[half:, :], came_ref[half : 2 * half, :]).astype(bf16)
    small = add(small_ref[...], came_ref[2 * half :, :]).astype(bf16)
    sent_out[half:, :] = small
    small_out[...] = small


def cut(kept, came, small=None):
    half, cols = kept.shape[0] // 2, kept.shape[1]
    if half % 16 == 0 and small is None:
        return *call(cut_kernel, [shape((half, cols), bf16)] * 2, [kept, came], vmem=VM[4], us=0), None
    if half % 16 == 0:
        outs = [shape((half, cols), bf16), shape((half + 16, cols), bf16), shape((16, cols), bf16)]
        return call(cut_loaded_kernel, outs, [kept, came, small], vmem=VM[4], us=0)
    if small is not None:
        small = add(small, came[-16:]).astype(bf16)
        came = came[:-16]
    next_sent = add(kept[half:], came[half:]).astype(bf16)
    if small is not None:
        next_sent = jnp.concatenate([next_sent, small], 0)
    return add(kept[:half], came[:half]).astype(bf16), next_sent, small


def call(kernel, outs, args, spaces="", scratch=(), vmem=None, us=3, wide=False):
    kinds = {"s": pltpu.SMEM, "v": pltpu.VMEM, "a": pl.ANY, "h": pltpu.HBM}
    spaces = spaces.ljust(len(args) + len(outs), "v")
    specs = [pl.BlockSpec(memory_space=kinds[kind]) for kind in spaces]
    return pl.pallas_call(
        kernel,
        out_shape=tuple(outs),
        in_specs=specs[: len(args)],
        out_specs=tuple(specs[len(args) :]),
        scratch_shapes=list(scratch),
        compiler_params=pltpu.CompilerParams(vmem_limit_bytes=(60 if wide else vmem or VM[3]) * 1024 * 1024),
        cost_estimate=pl.CostEstimate(flops=int(us * COST), bytes_accessed=0, transcendentals=0),
    )(*args)


def shape(dims, kind=f32):
    return jax.ShapeDtypeStruct(tuple(dims), kind)


def room(values):
    return pltpu.VMEM(values.shape, values.dtype)


def loads(refs, rooms, sems):
    return [pltpu.make_async_copy(ref, place, sems.at[i]) for i, (ref, place) in enumerate(zip(refs, rooms))]


def bias_kernel(doc_length, rank_ref, table_ref, doc_bias_ref, slot_bias_ref, line_ref):
    pairs = doc_bias_ref.shape[0]
    parts = doc_length // LANES
    length = line_ref.shape[1]
    offset = lax.broadcasted_iota(jnp.int32, (BUCKETS, length), 1) - doc_length
    hot = (bucket_index(offset) == lax.broadcasted_iota(jnp.int32, (BUCKETS, length), 0)).astype(f32)
    line_ref[...] = lax.dot_general(
        table_ref[...], hot, (((0,), (0,)), ((), ())), precision=highest, preferred_element_type=f32
    )
    narrow = rank_ref[0] & (parts - 1)

    def spread(head, start):
        line = line_ref[pl.ds(head, 1), pl.ds(pl.multiple_of(start, LANES), 2 * LANES)]
        rolled = pltpu.roll(jnp.broadcast_to(line, (LANES, 2 * LANES)), 0, 1, stride=1, stride_axis=0)
        return rolled[:, LANES:]

    def one_pair(pair, carry):
        for side in range(2):
            rows = slice(side * LANES, (side + 1) * LANES)
            head = 2 * pair + side
            for part in range(parts):
                distance = (narrow ^ part) - narrow
                doc_bias_ref[pair, rows, part * LANES : (part + 1) * LANES] = spread(
                    head, doc_length - LANES + distance * LANES
                )
            slot_bias_ref[pair, rows, :] = spread(head, doc_length - LANES)
        return carry

    lax.fori_loop(0, pairs, one_pair, 0)


def count_kernel(doc_length, doc_total, rank_ref, picked_ref, counts_ref, tally_ref, load_ref, places_ref, scratch_ref, sem):
    slots, slot_length, picks = load_ref.shape
    rows = slots * slot_length
    blocks = counts_ref.shape[0]
    narrow_size = picked_ref.shape[0] // slots
    first = (rank_ref[0] & (narrow_size - 1)) * slots
    load = pltpu.make_async_copy(picked_ref.at[pl.ds(first, slots)], load_ref, sem)
    load.start()
    load.wait()

    places_ref[...] = load_ref[...].reshape(rows, picks)

    def one_row(row, carry):
        places = places_ref[pl.ds(row, 1), :]
        high = places >> 7
        low = places & 127
        high_hot = (lax.broadcasted_iota(jnp.int32, (blocks, picks), 0) == high).astype(bf16)
        low_hot = (lax.broadcasted_iota(jnp.int32, (LANES, picks), 0) == low).astype(bf16)
        scratch_ref[pl.ds(row, blocks, stride=rows), :] = right_product(high_hot, low_hot)
        return carry

    lax.fori_loop(0, rows, one_row, 0, unroll=8)

    def one_block(block, carry):
        start = pl.multiple_of(block * rows, rows)
        counts_ref[block] = scratch_ref[pl.ds(start, rows), :].astype(bf16)
        return carry

    lax.fori_loop(0, blocks, one_block, 0, unroll=4)

    owner = places_ref[...] // doc_length
    lane = lax.broadcasted_iota(jnp.int32, (rows, LANES), 1)
    tally = jnp.zeros((rows, LANES), f32)
    for doc in range(doc_total):
        number = jnp.sum((owner == doc).astype(f32), 1, keepdims=True)
        tally = jnp.where(lane == doc, number, tally)
    tally_ref[...] = tally


def rms_scale(values):
    return lax.rsqrt(jnp.mean(values * values, -1, keepdims=True) + epsilon)


def rms_back(values, gain, grad):
    scale = rms_scale(values)
    weighted = grad * gain
    inner = jnp.mean(weighted * values, -1, keepdims=True)
    return scale * weighted - values * (scale * scale * scale * inner)


def tile(index, size=LANES):
    return pl.ds(pl.multiple_of(index * size, size), size)


def halves(values, zero_row):
    return jnp.concatenate([jnp.where(zero_row, values, jnp.zeros((), values.dtype)),
                            jnp.where(zero_row, jnp.zeros((), values.dtype), values)], 0)


def joined(values, first_lanes):
    rows = values.shape[0] // 2
    return jnp.where(first_lanes, values[:rows], values[rows:])


def forward_kernel(
    slots, slot_length, rank_ref, lengths_ref, queries_ref, own_ref, near_ref, far_ref, last_ref, doc_bias_ref,
    slot_bias_ref, attend_gain_ref, feed_gain_ref, final_gain_ref,
    wq_ref, wk_ref, wv_ref, wo_ref, wg_ref, wu_ref, wd_ref, wp_ref,
    all_ref, query_ref, key_ref, value_ref, doc_probs_ref, slot_probs_ref, mixed_ref, after_attend_ref,
    normed_feed_ref, hidden_ref, gate_slope_ref, up_slope_ref, after_feed_ref, normed_final_ref, embed_ref,
    slot_unit_ref, doc_unit_ref,
    slot_ref, slot_sem,
):
    slot_rows = slots * slot_length
    rows, width = query_ref.shape
    pairs = doc_probs_ref.shape[0]
    half = LANES // 2
    narrow_size = queries_ref.shape[0] // slots
    first = (rank_ref[0] & (narrow_size - 1)) * slots
    load_slots = pltpu.make_async_copy(queries_ref.at[pl.ds(first, slots)], slot_ref, slot_sem)
    load_slots.start()
    gain = attend_gain_ref[...].reshape(1, width)
    place = slot_rows
    for ref in (own_ref, near_ref, far_ref, last_ref):
        tokens = ref[...].astype(f32)
        all_ref[place : place + ref.shape[0], :] = (tokens * rms_scale(tokens) * gain).astype(bf16)
        place += ref.shape[0]
    load_slots.wait()
    slot_tokens = slot_ref[...].reshape(slot_rows, width).astype(f32)
    all_ref[:slot_rows, :] = (slot_tokens * rms_scale(slot_tokens) * gain).astype(bf16)
    normed = all_ref[:rows, :]
    query_ref[...] = product(normed, wq_ref[...]).astype(bf16)
    key_ref[...] = product(all_ref[...], wk_ref[...]).astype(bf16)
    value_ref[...] = product(all_ref[...], wv_ref[...]).astype(bf16)

    lane = lax.broadcasted_iota(jnp.int32, (slot_rows, LANES), 1)
    row = lax.broadcasted_iota(jnp.int32, (slot_rows, slot_rows), 0)
    col = lax.broadcasted_iota(jnp.int32, (slot_rows, slot_rows), 1)
    slot_keep = row < 0
    for slot in range(slots):
        start = slot * slot_length
        inside = (row >= start) & (row < start + slot_length) & (col >= start)
        slot_keep = slot_keep | (inside & (col < start + lengths_ref[first + slot]))

    def softmax(scores):
        weights = jnp.exp(scores - jnp.max(scores, -1, keepdims=True))
        return (weights * (1.0 / jnp.sum(weights, -1, keepdims=True))).astype(bf16)

    first_lanes = lane < half
    pair_keep = jnp.concatenate([slot_keep, slot_keep], 0)

    def one_pair(pair, carry):
        lanes = tile(pair)
        slot_query = halves(query_ref[:slot_rows, lanes], first_lanes)
        scores = right_product(slot_query, key_ref[:slot_rows, lanes]) + slot_bias_ref[pair]
        probs = softmax(jnp.where(pair_keep, scores, masked_value))
        slot_probs_ref[pair] = probs
        slot_mixed = product(probs, value_ref[:slot_rows, lanes])
        mixed_ref[:slot_rows, lanes] = joined(slot_mixed, first_lanes).astype(bf16)
        doc_query = halves(query_ref[slot_rows:, lanes], first_lanes)
        scores = right_product(doc_query, key_ref[slot_rows:, lanes]) + doc_bias_ref[pair]
        probs = softmax(scores)
        doc_probs_ref[pair] = probs
        doc_mixed = product(probs, value_ref[slot_rows:, lanes])
        mixed_ref[slot_rows:, lanes] = joined(doc_mixed, first_lanes).astype(bf16)
        return carry

    lax.fori_loop(0, pairs, one_pair, 0, unroll=2)

    attended = product(mixed_ref[...], wo_ref[...])
    after_attend_ref[:slot_rows, :] = slot_ref[...].reshape(slot_rows, width).astype(f32) + attended[:slot_rows]
    after_attend_ref[slot_rows:, :] = own_ref[...].astype(f32) + attended[slot_rows:]
    after_attend = after_attend_ref[...]
    feed_gain = feed_gain_ref[...].reshape(1, width)
    normed_feed_ref[...] = (after_attend * rms_scale(after_attend) * feed_gain).astype(bf16)

    def one_part(step, carry):
        part = tile(step, CHUNK)
        gate = product(normed_feed_ref[...], wg_ref[:, part])
        upward = product(normed_feed_ref[...], wu_ref[:, part])
        factor = 0.7978845608028654
        square = gate * gate
        bent = jnp.tanh(factor * gate * (1.0 + 0.044715 * square))
        curve = 0.5 * gate * (1.0 + bent)
        slope = 0.5 * (1.0 + bent) + 0.5 * factor * gate * (1.0 - bent * bent) * (1.0 + 3 * 0.044715 * square)
        hidden_ref[:, part] = (curve * upward).astype(bf16)
        gate_slope_ref[:, part] = (upward * slope).astype(bf16)
        up_slope_ref[:, part] = curve.astype(bf16)
        return carry

    lax.fori_loop(0, hidden_ref.shape[1] // CHUNK, one_part, 0, unroll=2)
    after_feed = after_attend_ref[...] + product(hidden_ref[...], wd_ref[...])
    after_feed_ref[...] = after_feed
    final_gain = final_gain_ref[...].reshape(1, width)
    normed_final = (after_feed * rms_scale(after_feed) * final_gain).astype(bf16)
    normed_final_ref[...] = normed_final
    embed = product(normed_final, wp_ref[...])
    embed_ref[...] = embed
    unit = (embed * lax.rsqrt(jnp.sum(embed * embed, -1, keepdims=True) + epsilon)).astype(bf16)
    slot_unit_ref[...] = unit[:slot_rows]
    doc_unit_ref[...] = unit[slot_rows:]


def loss_kernel(
    order, gathered, doc_total, slots, rank_ref, lengths_ref, positives_ref, counts_ref, near_ref, far_ref, unit_ref,
    tally_ref, losses_ref, grad_ref, kept_ref, sent_ref, sum_ref, scaled_ref,
):
    rows = unit_ref.shape[0]
    blocks = counts_ref.shape[0]
    per_doc = blocks // doc_total
    rank = rank_ref[0]
    half = blocks // 2
    sum_ref[...] = jnp.zeros_like(sum_ref)

    def gather_step(place, carry):
        near = rank ^ gather_order(place, gathered)
        far = near ^ (1 << gathered[-1])
        sum_ref[near // per_doc] += product(counts_ref[near], near_ref[place])
        sum_ref[far // per_doc] += product(counts_ref[far], far_ref[place])
        return carry

    lax.fori_loop(0, half, gather_step, 0, unroll=4)

    unit = unit_ref[...].astype(f32)
    lane = lax.broadcasted_iota(jnp.int32, (rows, LANES), 1)
    summed = jnp.zeros((rows, LANES), f32)
    for doc in range(doc_total):
        number = jnp.sum(sum_ref[doc] * unit, 1, keepdims=True)
        summed = jnp.where(lane == doc, number, summed)
    tally = tally_ref[...]
    most = jnp.maximum(tally, 1.0)
    slot_length = rows // slots
    narrow_size = lengths_ref.shape[0] // slots
    first = (rank & (narrow_size - 1)) * slots
    row = lax.broadcasted_iota(jnp.int32, (rows, LANES), 0)
    slot_row = lax.broadcasted_iota(jnp.int32, (slots, LANES), 0)
    valid = row < 0
    positive = jnp.zeros((slots, LANES), jnp.int32)
    for slot in range(slots):
        start = slot * slot_length
        valid = valid | ((row >= start) & (row < start + lengths_ref[first + slot]))
        positive = jnp.where(slot_row == slot, positives_ref[first + slot], positive)
    weight = jnp.where(valid, jnp.minimum(tally, 1.0), 0.0)
    pooled = (weight * (summed / most)).reshape(slots, slot_length, LANES)
    weight_sum = jnp.maximum(jnp.sum(weight.reshape(slots, slot_length, LANES), 1), 1.0)
    scores = jnp.sum(pooled, 1) / weight_sum / contrastive_sharpness_factor
    slot_lane = lax.broadcasted_iota(jnp.int32, (slots, LANES), 1)
    inside = slot_lane < doc_total
    scores = jnp.where(inside, scores, -jnp.inf)
    top = jnp.max(scores, -1, keepdims=True)
    powers = jnp.exp(scores - top)
    total = jnp.sum(powers, -1, keepdims=True)
    chosen = (slot_lane == positive).astype(f32)
    picked = jnp.sum(jnp.where(slot_lane == positive, scores, 0.0), -1, keepdims=True)
    losses_ref[...] = jnp.broadcast_to(top + jnp.log(total) - picked, (slots, LANES))
    slope = (powers / total - chosen) / contrastive_sharpness_factor / weight_sum
    slope = jnp.where(inside, slope, 0.0)
    slope = jnp.broadcast_to(slope[:, None, :], (slots, slot_length, LANES)).reshape(rows, LANES)
    slope = slope * weight / most

    grad = jnp.zeros((rows, unit.shape[1]), f32)
    for doc in range(doc_total):
        column = jnp.sum(jnp.where(lane == doc, slope, 0.0), 1, keepdims=True)
        grad = grad + column * sum_ref[doc]
        scaled_ref[doc] = (column * unit).T.astype(bf16)
    grad_ref[...] = grad

    def scatter_step(place, carry):
        kept = rank ^ scatter_order(place, order)
        sent = kept ^ (1 << order[0])
        kept_ref[place] = product(scaled_ref[kept // per_doc], counts_ref[kept]).astype(bf16)
        sent_ref[place] = product(scaled_ref[sent // per_doc], counts_ref[sent]).astype(bf16)
        return carry

    lax.fori_loop(0, half, scatter_step, 0, unroll=4)


def feed_back(
    part, grad_unit, embed_ref, after_feed_ref, after_attend_ref, gate_slope_ref, up_slope_ref, feed_gain_ref,
    final_gain_ref, wo_ref, wg_ref, wu_ref, wd_ref, wp_ref, grads_out, after_out, mixed_out, more_ref,
):
    units, width = wd_ref.shape
    up_start, feed_start = units, 2 * units
    attend_start, embed_start = 2 * units + width, 2 * units + 2 * width
    embed = embed_ref[part, :]
    scale = lax.rsqrt(jnp.sum(embed * embed, -1, keepdims=True) + epsilon)
    inner = jnp.sum(grad_unit * embed, -1, keepdims=True)
    grad_embed = (scale * grad_unit - embed * (scale * scale * scale * inner)).astype(bf16)
    grads_out[:, embed_start : embed_start + embed.shape[1]] = grad_embed
    grad_after_feed = rms_back(
        after_feed_ref[part, :], final_gain_ref[...].reshape(1, -1), right_product(grad_embed, wp_ref[...])
    )
    after_out[...] = grad_after_feed
    grad_feed = grad_after_feed.astype(bf16)
    grads_out[:, feed_start:attend_start] = grad_feed
    def one_part(step, total):
        cols = tile(step, CHUNK)
        grad_hidden = right_product(grads_out[:, feed_start:attend_start], wd_ref[cols, :])
        grad_gate = (grad_hidden * gate_slope_ref[part, cols].astype(f32)).astype(bf16)
        grad_up = (grad_hidden * up_slope_ref[part, cols].astype(f32)).astype(bf16)
        grads_out[:, cols] = grad_gate
        grads_out[:, pl.ds(pl.multiple_of(up_start + step * CHUNK, CHUNK), CHUNK)] = grad_up
        more_ref[...] += right_product(grad_gate, wg_ref[:, cols]) + right_product(grad_up, wu_ref[:, cols])
        return total

    more_ref[...] = jnp.zeros_like(more_ref)
    lax.fori_loop(0, units // CHUNK, one_part, 0, unroll=2)
    total = more_ref[...]
    more = rms_back(after_attend_ref[part, :], feed_gain_ref[...].reshape(1, -1), total)
    grad_after_attend = after_out[...] + more
    after_out[...] = grad_after_attend
    grad_attend = grad_after_attend.astype(bf16)
    grads_out[:, attend_start:embed_start] = grad_attend
    mixed_out[...] = right_product(grad_attend, wo_ref[...]).astype(bf16)


def attend_back(
    far_parts, queries, keys, query_ref, key_ref, value_ref, probs_ref, mixed_ref, query_out, key_out, value_out,
    sums_out,
):
    rows = mixed_ref.shape[0]
    length = probs_ref.shape[2]
    half = LANES // 2
    first_lanes = lax.broadcasted_iota(jnp.int32, (rows, LANES), 1) < half
    row = lax.broadcasted_iota(jnp.int32, (rows, rows), 0)
    col = lax.broadcasted_iota(jnp.int32, (rows, rows), 1)
    flip = (row + col == rows - 1).astype(bf16)
    nothing = jnp.zeros((rows, LANES), f32)

    def one_pair(pair, carry):
        lanes = tile(pair)
        grad_mixed = halves(mixed_ref[:, lanes], first_lanes)
        query = halves(query_ref[queries, lanes], first_lanes)
        probs = probs_ref[pair]
        grad_probs = right_product(grad_mixed, value_ref[keys, lanes])
        exact = probs.astype(f32)
        inner = jnp.sum(exact * grad_probs, -1, keepdims=True)
        grad_scores = (exact * (grad_probs - inner)).astype(bf16)
        query_out(joined(product(grad_scores, key_ref[keys, lanes]), first_lanes).astype(bf16), pair)
        key_out(left_product(grad_scores, query).astype(bf16), pair)
        value_out(left_product(probs, grad_mixed).astype(bf16), pair)
        for side in range(2):
            head = 2 * pair + side
            own = grad_scores[side * rows : (side + 1) * rows, :]
            for part in range(length // LANES):
                piece = own[:, part * LANES : (part + 1) * LANES]
                if part in far_parts:
                    line = jnp.concatenate([piece.astype(f32), nothing], 1)
                else:
                    line = pltpu.roll(
                        jnp.concatenate([product(flip, piece), nothing], 1), 0, 1, stride=1, stride_axis=0
                    )
                sums_out[tile(head, 8), part * 2 * LANES : (part + 1) * 2 * LANES] = jnp.sum(
                    line.reshape(rows // 8, 8, 2 * LANES), 0
                )
        return carry

    lax.fori_loop(0, probs_ref.shape[0], one_pair, 0, unroll=2)


def input_back(tokens, gain_ref, after_ref, query, key, value, wq_ref, wk_ref, wv_ref):
    grad_normed = right_product(query, wq_ref[...])
    grad_normed = grad_normed + right_product(key, wk_ref[...])
    grad_normed = grad_normed + right_product(value, wv_ref[...])
    return after_ref[...] + rms_back(tokens, gain_ref[...].reshape(1, -1), grad_normed)


def table_sums(sums_ref, distances):
    heads = sums_ref.shape[0] // 8
    span = lax.broadcasted_iota(jnp.int32, (2 * LANES, LANES), 0) - (LANES - 1)
    bucket = lax.broadcasted_iota(jnp.int32, (2 * LANES, LANES), 1)
    total = jnp.zeros((heads, LANES), f32)
    for part, distance in enumerate(distances):
        lines = jnp.sum(sums_ref[:, part * 2 * LANES : (part + 1) * 2 * LANES].reshape(heads, 8, 2 * LANES), 1)
        hot = (bucket_index(span + distance * LANES) == bucket).astype(f32)
        total = total + lax.dot_general(
            lines, hot, (((1,), (0,)), ((), ())), precision=highest, preferred_element_type=f32
        )
    return total


def slot_feed_kernel(
    grad_unit_ref, embed_ref, after_feed_ref, after_attend_ref, gate_slope_ref, up_slope_ref, feed_gain_ref,
    final_gain_ref, wp_ref, wd_ref, wg_ref, wu_ref, wo_ref,
    grads_out, after_out, mixed_out, more_ref,
):
    feed_back(
        slice(0, after_out.shape[0]), grad_unit_ref[...], embed_ref, after_feed_ref, after_attend_ref,
        gate_slope_ref, up_slope_ref, feed_gain_ref, final_gain_ref, wo_ref, wg_ref, wu_ref, wd_ref, wp_ref, grads_out,
        after_out, mixed_out, more_ref,
    )


def slot_attend_kernel(
    query_ref, key_ref, value_ref, probs_ref, mixed_ref, grads_out, table_out, sums_ref
):
    rows, width = mixed_ref.shape

    def out(place):
        def store(values, pair):
            grads_out[:, pl.ds(pl.multiple_of(place * width + pair * LANES, LANES), LANES)] = values

        return store

    part = slice(0, rows)
    attend_back(
        (), part, part, query_ref, key_ref, value_ref, probs_ref, mixed_ref, out(0), out(1), out(2), sums_ref
    )
    table_out[...] = table_sums(sums_ref, [0])


def doc_feed_kernel(came, *refs):
    parts, refs = refs[:came], refs[came:]
    (
        embed_ref, after_feed_ref, after_attend_ref, gate_slope_ref, up_slope_ref, feed_gain_ref, final_gain_ref,
        wp_ref, wd_ref, wg_ref, wu_ref, wo_ref,
        grads_out, after_out, mixed_out, more_ref,
    ) = refs
    rows = after_out.shape[0]
    grad_unit = add(*(part[0] for part in parts)).T
    feed_back(
        slice(embed_ref.shape[0] - rows, embed_ref.shape[0]), grad_unit, embed_ref, after_feed_ref,
        after_attend_ref, gate_slope_ref, up_slope_ref, feed_gain_ref, final_gain_ref, wo_ref, wg_ref, wu_ref, wd_ref,
        wp_ref, grads_out, after_out, mixed_out, more_ref,
    )


def doc_attend_kernel(
    rank_ref, query_ref, key_ref, value_ref, probs_ref, mixed_ref, slot_table_ref, grads_out, table_out, query_room,
    sums_ref,
):
    rows, width = query_room.shape
    length = probs_ref.shape[2]
    first = key_ref.shape[0] - length

    def query_out(values, pair):
        query_room[:, tile(pair)] = values

    def key_out(values, pair):
        grads_out[:length, tile(pair)] = values

    def value_out(values, pair):
        grads_out[:length, pl.ds(pl.multiple_of(width + pair * LANES, LANES), LANES)] = values

    attend_back(
        (2,), slice(first, first + rows), slice(first, key_ref.shape[0]), query_ref, key_ref, value_ref, probs_ref,
        mixed_ref, query_out, key_out, value_out, sums_ref,
    )
    grads_out[length:, :width] = query_room[: rows // 2, :]
    grads_out[length:, width:] = query_room[rows // 2 :, :]
    parts = length // LANES
    narrow = rank_ref[0] & (parts - 1)
    table = table_sums(sums_ref, [(narrow ^ part) - narrow for part in range(parts)]) + slot_table_ref[...]
    heads = table.shape[0]
    table_out[...] = jnp.concatenate([table, jnp.zeros((16 - heads, LANES), f32)], 0).astype(bf16)


def pick_columns(values, total, order, flipped, rank):
    count = 1 << len(order) + 1
    size = total // count
    row = lax.broadcasted_iota(jnp.int32, (total, total // 2), 0)
    col = lax.broadcasted_iota(jnp.int32, (total, total // 2), 1)
    source = (scatter_order(col // size, order) ^ rank ^ flipped) * size + col % size
    return product(values, (row == source).astype(bf16)).astype(bf16)


def pick_tiles(values_ref, order, flipped, rank, store):
    rows = values_ref.shape[0]
    half = LANES // 2
    first_lanes = lax.broadcasted_iota(jnp.int32, (rows, LANES), 1) < half
    upper = ((rank ^ flipped) & 1) == 1

    def one_tile(step, carry):
        place = 2 * step
        sides = []
        for side in range(2):
            tile = (rank ^ scatter_order(place + side, order)) >> 1
            values = values_ref[:, pl.ds(pl.multiple_of(tile * LANES, LANES), LANES)].astype(f32)
            turned = pltpu.roll(values, half, 1)
            sides.append(jnp.where(upper, turned, values) if side == 0 else jnp.where(upper, values, turned))
        store(step, jnp.where(first_lanes, sides[0], sides[1]).astype(bf16))
        return carry

    lax.fori_loop(0, 1 << len(order) - 1, one_tile, 0)


def turn_kernel(
    orders, rank_ref, all_ref, normed_feed_ref, mixed_ref, normed_final_ref, hidden_ref, kept_out, sent_out, doc_out,
):
    first, second, third, fourth = orders
    rank = rank_ref[0]
    rows, width = normed_feed_ref.shape
    units = hidden_ref.shape[1]
    slots = all_ref.shape[0] - doc_out.shape[0]
    half = width // 2
    for out, flipped in ((kept_out, 0), (sent_out, 1)):
        out[:, :half] = pick_columns(normed_feed_ref[...], width, first, flipped, rank)
        out[:, half : 2 * half] = pick_columns(normed_feed_ref[...], width, second, flipped, rank)
        out[:, 2 * half : 3 * half] = pick_columns(mixed_ref[...], width, first, flipped, rank)
        out[:, 3 * half : 4 * half] = pick_columns(normed_final_ref[...], width, second, flipped, rank)
        start = 4 * half
        if units >> (len(third) + 1) == LANES // 2:

            def store(place, values):
                out[:, pl.ds(pl.multiple_of(start + place * LANES, LANES), LANES)] = values

            pick_tiles(hidden_ref, third, flipped, rank, store)
        else:
            out[:, start : start + units // 2] = pick_columns(hidden_ref[...], units, third, flipped, rank)
        start = start + units // 2
        out[slots:, start:] = jnp.zeros((rows - slots, half), bf16)
        if flipped:
            out[:slots, start:] = pick_columns(all_ref[:slots, :], width, fourth, flipped, rank)
        else:
            both = pick_columns(all_ref[...], width, fourth, flipped, rank)
            out[:slots, start:] = both[:slots]
            doc_out[...] = both[slots:]


def store_product(left, right_ref, columns, kept_ref, sent_ref, start):
    half = left.shape[1] // 2
    size = 2 * LANES

    def one_part(first, size):
        here = pl.ds(pl.multiple_of(start + first, LANES), size)
        result = left_product(left, right_ref[:, pl.ds(pl.multiple_of(first, LANES), size)]).astype(bf16)
        kept_ref[:half, here] = result[:half]
        sent_ref[:half, here] = result[half:]

    def step(place, carry):
        one_part(place * size, size)
        return carry

    lax.fori_loop(0, columns // size, step, 0, unroll=2)
    if columns % size:
        one_part(columns // size * size, columns % size)


def weight_kernel(
    terms, kept_any, came_any, slot_any, slot_came_any, doc_any, doc_came_any, kept_ref, sent_ref, left_ref, right_ref,
    sems,
):
    rows = kept_any.shape[0]
    part = slot_any.shape[0]
    copies = []
    left_place, right_place = 0, 0
    for left_start, left_width, right_start, right_width in terms:
        pieces = []
        for place, ref in enumerate((kept_any, came_any)):
            source = ref.at[:, left_start : left_start + left_width]
            target = left_ref.at[place * rows : (place + 1) * rows, left_place : left_place + left_width]
            pieces.append((source, target))
        for place, ref in enumerate((slot_any, doc_any, slot_came_any, doc_came_any)):
            source = ref.at[:, right_start : right_start + right_width]
            target = right_ref.at[place * part : (place + 1) * part, right_place : right_place + right_width]
            pieces.append((source, target))
        first = sum(len(group) for group in copies)
        copies.append(
            [pltpu.make_async_copy(one, two, sems.at[first + i]) for i, (one, two) in enumerate(pieces)]
        )
        left_place += left_width
        right_place += right_width
    for group in copies:
        for copy in group:
            copy.start()
    left_place, right_place = 0, 0
    for group, (_, left_width, _, right_width) in zip(copies, terms):
        for copy in group:
            copy.wait()
        left = left_ref[:, left_place : left_place + left_width]
        right = right_ref.at[:, right_place : right_place + right_width]
        store_product(left, right, right_width, kept_ref, sent_ref, right_place)
        left_place += left_width
        right_place += right_width


def attend_weight_kernel(
    doc_ref, kept_any, came_any, slot_any, slot_came_any, grads_ref, other_ref, table_ref, other_table_ref,
    kept_out, sent_out, pair_kept, pair_sent, slot_room, slot_came_room, left_ref, right_ref, query_ref, sems,
):
    rows = slot_any.shape[0]
    width = slot_room.shape[1] // 3
    half = doc_ref.shape[1]
    length = doc_ref.shape[0]
    lanes = slice(kept_any.shape[1] - half, kept_any.shape[1])
    copies = loads(
        (slot_any, slot_came_any, kept_any.at[:rows, lanes], came_any.at[:rows, lanes]),
        (slot_room, slot_came_room, left_ref.at[length : length + rows, :], left_ref.at[length + rows :, :]),
        sems,
    )
    for copy in copies:
        copy.start()
    left_ref[:length, :] = doc_ref[...]
    for part in range(length // LANES):
        here = slice(part * LANES, (part + 1) * LANES)
        there = slice((part ^ 1) * LANES, ((part ^ 1) + 1) * LANES)
        right_ref[here, :] = add(grads_ref[here, :], other_ref[there, :]).astype(bf16)
    pair_kept[...] = right_ref[:LANES, :]
    pair_sent[...] = right_ref[2 * LANES : 3 * LANES, :]
    small = LANES // 2
    for place, ref in enumerate((grads_ref, other_ref)):
        query_ref[2 * place * small : (2 * place + 1) * small, :] = ref[length:, :width]
        query_ref[(2 * place + 1) * small : (2 * place + 2) * small, :] = ref[length:, width:]
    for copy in copies:
        copy.wait()
    right_ref[length : length + rows, :] = slot_room[:, width:]
    right_ref[length + rows :, :] = slot_came_room[:, width:]
    query_ref[2 * LANES : 2 * LANES + rows, :] = slot_room[:, :width]
    query_ref[2 * LANES + rows :, :] = slot_came_room[:, :width]
    store_product(left_ref[...], right_ref, 2 * width, kept_out, sent_out, width)
    left = jnp.concatenate([left_ref[: 2 * LANES, :], left_ref[length:, :]], 0)
    store_product(left, query_ref, width, kept_out, sent_out, 0)
    tail = sent_out.shape[0] - 16
    sent_out[tail:, :] = jnp.zeros((16, sent_out.shape[1]), bf16)
    sent_out[tail:, :LANES] = add(table_ref[...], other_table_ref[...]).astype(bf16)


def doc_input_kernel(
    tokens_ref, gain_ref, after_ref, grads_ref, kept_ref, came_ref, wq_ref, wk_ref, wv_ref, tokens_out
):
    rows, width = tokens_ref.shape
    rest = grads_ref.shape[0] - rows // 2
    query = jnp.concatenate([grads_ref[rest:, :width], grads_ref[rest:, width:]], 0)
    pair = add(kept_ref[...], came_ref[...]).astype(bf16)
    tokens_out[...] = input_back(
        tokens_ref[...].astype(f32), gain_ref, after_ref, query, pair[:, :width], pair[:, width:], wq_ref, wk_ref, wv_ref
    )


def slot_input_kernel(
    slots, rank_ref, tokens_any, gain_ref, after_ref, grads_ref, wq_ref, wk_ref, wv_ref, tokens_out, slot_room, sem
):
    narrow_size = tokens_any.shape[0] // slots
    first = (rank_ref[0] & (narrow_size - 1)) * slots
    load = pltpu.make_async_copy(tokens_any.at[pl.ds(first, slots)], slot_room, sem)
    load.start()
    load.wait()
    width = tokens_out.shape[1]
    query, key, value = (grads_ref[:, place * width : (place + 1) * width] for place in range(3))
    tokens_out[...] = input_back(
        slot_room[...].reshape(tokens_out.shape).astype(f32), gain_ref, after_ref, query, key, value, wq_ref, wk_ref,
        wv_ref,
    )


def on_device(
    doc_tokens, query_tokens, query_lengths, positive_docs, retrieved, attend_gain, query_weight, key_weight,
    value_weight, output_weight, bias_table, feed_gain, gate_weight, up_weight, down_weight, final_gain, proj_weight,
):
    narrow_size = lax.axis_size("narrow")
    bits = rank_bits()
    rank = my_rank()
    rank_word = rank.astype(jnp.int32).reshape(1)
    doc_rows, width = doc_tokens.shape[1:]
    doc_length = doc_rows * narrow_size
    doc_total = doc_tokens.shape[0] * lax.axis_size("wide")
    slots = query_tokens.shape[0] // narrow_size
    slot_length = query_tokens.shape[1]
    heads = bias_table.shape[1]
    units = gate_weight.shape[1]
    columns = proj_weight.shape[1]
    slot_rows = slots * slot_length
    rows = slot_rows + doc_rows
    blocks = doc_total * doc_length // LANES
    assert doc_tokens.shape[0] == 1 and doc_rows == LANES and slot_rows == LANES and narrow_size == 4
    assert columns == LANES and doc_total <= LANES and blocks == 1 << bits
    gains = (attend_gain, feed_gain, final_gain)
    dma = pltpu.SemaphoreType.DMA
    waxes = list(range(3, bits))

    orders = (
        [2] + [1] + waxes[:1] + waxes[1:],
        waxes[:1] + [1] + [2] + waxes[1:],
        [2] + [1] + waxes[:1] + waxes[1:],
        [1] + waxes[:1] + [2] + waxes[1:],
    )
    own_tokens = doc_tokens[0]
    y_tokens = swap(own_tokens, 2)
    core_tokens = swap(own_tokens, 1)
    pairs = heads // 2
    doc_bias, slot_bias = call(
        functools.partial(bias_kernel, doc_length),
        [shape((pairs, 2 * doc_rows, doc_length)), shape((pairs, 2 * slot_rows, slot_rows))],
        [rank_word, bias_table],
        "s",
        [pltpu.VMEM((heads, 2 * doc_length + LANES), f32)],
    )
    counts, tally = call(
        functools.partial(count_kernel, doc_length, doc_total),
        [shape((blocks, slot_rows, LANES), bf16), shape((slot_rows, LANES))],
        [rank_word, after(retrieved, slot_bias)],
        "sa",
        [
            pltpu.VMEM((slots, slot_length, retrieved.shape[2]), jnp.int32),
            pltpu.VMEM((slot_rows, retrieved.shape[2]), jnp.int32),
            pltpu.VMEM((blocks * slot_rows, LANES), f32),
            dma,
        ],
        us=5,
        wide=bits > 5,
    )
    y_tokens = after(y_tokens, doc_bias, tally)
    both_tokens = swap(y_tokens, 1)

    all_rows = slot_rows + doc_length
    forward_shapes = [
        shape((all_rows, width), bf16),
        shape((rows, width), bf16),
        shape((all_rows, width), bf16),
        shape((all_rows, width), bf16),
        shape((pairs, 2 * doc_rows, doc_length), bf16),
        shape((pairs, 2 * slot_rows, slot_rows), bf16),
        shape((rows, width), bf16),
        shape((rows, width)),
        shape((rows, width), bf16),
        shape((rows, units), bf16),
        shape((rows, units), bf16),
        shape((rows, units), bf16),
        shape((rows, width)),
        shape((rows, width), bf16),
        shape((rows, columns)),
        shape((slot_rows, columns), bf16),
        shape((doc_rows, columns), bf16),
    ]
    weights = [
        query_weight, key_weight, value_weight, output_weight, gate_weight, up_weight, down_weight, proj_weight,
    ]
    slot_room = pltpu.VMEM((slots, slot_length, width), bf16)
    (
        all_normed, query, key, value, doc_probs, slot_probs, mixed, after_attend, normed_feed, hidden, gate_slope,
        up_slope, after_feed, normed_final, embed, slot_unit, doc_unit,
    ) = call(
        functools.partial(forward_kernel, slots, slot_length),
        forward_shapes,
        [
            rank_word, query_lengths, query_tokens, own_tokens, core_tokens, y_tokens, both_tokens, doc_bias, slot_bias,
            *gains, *weights,
        ],
        "ssa" + "v" * 9 + "v" * 8 + "v" * len(forward_shapes),
        [slot_room, dma],
        vmem=VM[0],
        us=18,
    )

    phases = [list(range(high, max(high - 2, 0), -1)) for high in range(bits - 1, 0, -2)]
    gathered = []
    near_units = doc_unit[None]
    for phase, group in enumerate(phases):
        group = group[::-1]
        masks = [gather_order(place, group) for place in range(1, 1 << len(group))]
        came = [swap(near_units, mask) for mask in masks]
        if phase == 0:
            pass
        if phase == 1:
            turned_cols = 5 * width // 2 + units // 2
            turned, turned_sent, turned_docs = call(
                functools.partial(turn_kernel, orders),
                [shape((rows, turned_cols), bf16)] * 2 + [shape((doc_length, width // 2), bf16)],
                after([rank_word, all_normed, normed_feed, mixed, normed_final, hidden], near_units),
                "s",
                us=5,
                wide=bits > 5,
            )
            came = after(came, turned)
        near_units = jnp.concatenate([near_units] + came, 0)
        gathered = gathered + group
    gathered = gathered + [0]
    far_units = swap(near_units, 1)

    order = list(range(bits))
    half = blocks // 2
    losses, grad_slot_unit, kept, sent = call(
        functools.partial(loss_kernel, order, gathered, doc_total, slots),
        [
            shape((slots, LANES)),
            shape((slot_rows, columns)),
            shape((half, columns, LANES), bf16),
            shape((half, columns, LANES), bf16),
        ],
        [rank_word, query_lengths, positive_docs, counts, near_units, far_units, slot_unit, tally],
        "sss",
        [
            pltpu.VMEM((doc_total, slot_rows, columns), f32),
            pltpu.VMEM((doc_total, columns, slot_rows), bf16),
        ],
        wide=bits > 5,
    )
    back_weights = [proj_weight, down_weight, gate_weight, up_weight, output_weight]
    doc_cols = 2 * units + 2 * width + columns

    came = [swap(sent, 1)]
    rest = order[1:]
    parts = [kept]
    phase = 0
    feed_shapes = [shape((LANES, doc_cols), bf16), shape((LANES, width)), shape((LANES, width), bf16)]
    while rest:
        group, rest = rest[:2], rest[2:]
        count = 1 << len(group)
        size = parts[0].shape[0] // count
        pieces = []
        for place in range(count):
            here = slice(place * size, (place + 1) * size)
            pieces.append(add(*(part[here] for part in parts), *(one[here] for one in came)).astype(bf16))
        masks = [scatter_order(place, group) for place in range(count)]
        came = [swap(piece, mask) for piece, mask in zip(pieces[1:], masks[1:])]
        parts = [pieces[0]]
        if phase == 0:
            slot_grads, slot_after, slot_mixed = call(
                slot_feed_kernel,
                feed_shapes,
                [after(grad_slot_unit, pieces[1])]
                + [embed, after_feed, after_attend, gate_slope, up_slope, gains[1], gains[2]]
                + back_weights,
                "",
                [pltpu.VMEM((slot_rows, width), f32)],
                vmem=VM[1],
                us=7,
            )
            came = after(came, slot_after)
        if phase == 1:
            slot_came = swap(after(slot_grads, *pieces[1:]), 1)
            turned_came = swap(after(turned_sent, *pieces[1:]), 1)
            slot_thirds, slot_table = call(
                slot_attend_kernel,
                [shape((slot_rows, 3 * width), bf16), shape((heads, LANES))],
                [query, key, value, slot_probs, after(slot_mixed, *pieces[1:])],
                scratch=[pltpu.VMEM((heads * 8, 2 * LANES), f32)],
                us=4,
            )
            came = after(came, slot_table)
        phase += 1

    doc_grads, doc_after, doc_mixed = call(
        functools.partial(doc_feed_kernel, 1 + len(came)),
        feed_shapes,
        parts + after(came, slot_came, turned_came)
        + [embed, after_feed, after_attend, gate_slope, up_slope, gains[1], gains[2]]
        + back_weights,
        "",
        [pltpu.VMEM((doc_rows, width), f32)],
        vmem=VM[2],
        us=7,
    )
    thirds_came = swap(after(slot_thirds, doc_after), 1)
    doc_came = swap(doc_grads, 1)

    class Stream:
        def __init__(self, kept, sent, order):
            self.kept, self.order, self.step = kept, order, 0
            self.loaded = sent.shape[0] > kept.shape[0]
            self.small = sent[-16:] if self.loaded else None
            self.send(sent)

        def send(self, sent):
            self.came = swap(sent, 1 << self.order[self.step])
            self.step += 1

        def advance(self, *wait):
            came = after(self.came, *wait)
            if self.step == len(self.order):
                if self.loaded:
                    self.small = add(self.small, came[-16:]).astype(bf16)
                    came = came[:-16]
                self.result = add(self.kept, came)
                return self.result
            self.kept, sent, self.small = cut(self.kept, came, self.small)
            self.send(sent)
            return self.kept

    def weight_product(terms, order, *wait):
        left = sum(term[1] for term in terms)
        right = sum(term[3] for term in terms)
        tall = terms[0][1] // 2
        args = after([turned, turned_came, slot_grads, slot_came, doc_grads, doc_came], *wait)
        kept, sent = call(
            functools.partial(weight_kernel, terms),
            [shape((tall, right), bf16)] * 2,
            args,
            "a" * 6,
            [pltpu.VMEM((2 * rows, left), bf16), pltpu.VMEM((2 * rows, right), bf16), dma((6 * len(terms),))],
        )
        return Stream(kept, sent, order)

    small_half = width // 2
    att_grads, table = call(
        doc_attend_kernel,
        [shape((doc_length + doc_rows // 2, 2 * width), bf16), shape((16, LANES), bf16)],
        [rank_word, query, key, value, doc_probs, doc_mixed, slot_table],
        "s",
        [pltpu.VMEM((doc_rows, width), bf16), pltpu.VMEM((heads * 8, 2 * doc_length), f32)],
    )
    att_came, table_came = swap(att_grads, 1), swap(table, 1)
    first = weight_product(
        [(0, small_half, 0, units), (2 * small_half, small_half, 2 * units + width, width)], orders[0], table
    )
    fourth_kept, fourth_sent, pair_kept, pair_sent = call(
        attend_weight_kernel,
        [
            shape((width // 4, 3 * width), bf16),
            shape((width // 4 + 16, 3 * width), bf16),
            shape((doc_rows, 2 * width), bf16),
            shape((doc_rows, 2 * width), bf16),
        ],
        [turned_docs, turned, turned_came, slot_thirds, thirds_came, att_grads, att_came, after(table, first.kept), table_came],
        "vaaaa",
        [
            pltpu.VMEM((slot_rows, 3 * width), bf16),
            pltpu.VMEM((slot_rows, 3 * width), bf16),
            pltpu.VMEM((doc_length + 2 * slot_rows, width // 2), bf16),
            pltpu.VMEM((doc_length + 2 * slot_rows, 2 * width), bf16),
            pltpu.VMEM((2 * doc_rows + 2 * slot_rows, width), bf16),
            dma((4,)),
        ],
    )
    fourth = Stream(fourth_kept, fourth_sent, orders[3])
    second = weight_product(
        [(small_half, small_half, units, units), (3 * small_half, small_half, 2 * units + 2 * width, columns)],
        orders[1],
        fourth_kept,
    )
    third = weight_product([(4 * small_half, units // 2, 2 * units, width)], orders[2], second.kept)
    def own_rows(values):
        return lax.dynamic_slice_in_dim(values, rank * (width >> bits), width >> bits, 0).astype(f32)

    def gain_grad(gain, *pairs):
        return sum(jnp.sum(own_rows(weight) * grad, 1) for weight, grad in pairs) / own_rows(gain)

    streams = {"A": first, "B": second, "C": third, "D": fourth}
    plan = "JADBACDpBADCBCIABDCfa"
    if bits != 5:
        plan = "J" + "ADBC" + "p" + "ADBC" * (bits - 3) + "I" + "ABfDaC"
    done = third.kept
    for event in plan:
        if event in streams:
            done = streams[event].advance(done)
        elif event == "p":
            pair_came = swap(after(pair_sent, done), 2)
        elif event == "f":
            gate_grad, output_grad = first.result[:, :units], first.result[:, units:]
            up_grad, proj_grad = second.result[:, :units], second.result[:, units:]
            feed_gain_grad = gain_grad(feed_gain, (gate_weight, gate_grad), (up_weight, up_grad))
            final_gain_grad = gain_grad(final_gain, (proj_weight, proj_grad))
            done = jnp.concatenate([feed_gain_grad, final_gain_grad])
            feed_gain_grad, final_gain_grad = done[: width >> bits], done[width >> bits :]
        elif event == "a":
            query_g, key_g, value_g = (fourth.result[:, place * width : (place + 1) * width] for place in range(3))
            done = gain_grad(attend_gain, (query_weight, query_g), (key_weight, key_g), (value_weight, value_g))
            attend_gain_grad = done
        elif event == "I":
            (done,) = call(
                doc_input_kernel,
                [shape((doc_rows, width))],
                [own_tokens, gains[0], doc_after, att_grads, pair_kept, after(pair_came, done)]
                + [query_weight, key_weight, value_weight],
                us=3,
            )
            doc_grad = done
        else:
            (done,) = call(
                functools.partial(slot_input_kernel, slots),
                [shape((slot_rows, width))],
                [rank_word, query_tokens, gains[0], slot_after, after(slot_thirds, done)]
                + [query_weight, key_weight, value_weight],
                "sa",
                [slot_room, dma],
                us=3,
            )
            query_grad = done
    return (
        losses[:, 0],
        doc_grad[None],
        query_grad.reshape(slots, slot_length, width),
        attend_gain_grad,
        query_g,
        key_g,
        value_g,
        output_grad,
        fourth.small[:heads, :BUCKETS].astype(f32).T,
        feed_gain_grad,
        gate_grad,
        up_grad,
        third.result,
        final_gain_grad,
        proj_grad,
    )


def solution(mesh):
    return jax.shard_map(
        on_device,
        mesh=mesh,
        in_specs=(
            P("wide", "narrow", None),
            P("wide", None, None),
            P("wide"),
            P("wide"),
            P("wide", None, None),
            P(),
            P(),
            P(),
            P(),
            P(),
            P(),
            P(),
            P(),
            P(),
            P(),
            P(),
            P(),
        ),
        out_specs=(
            P(("wide", "narrow")),
            P("wide", "narrow", None),
            P(("wide", "narrow"), None, None),
            P(("wide", "narrow")),
            P(("wide", "narrow"), None),
            P(("wide", "narrow"), None),
            P(("wide", "narrow"), None),
            P(("wide", "narrow"), None),
            P(),
            P(("wide", "narrow")),
            P(("wide", "narrow"), None),
            P(("wide", "narrow"), None),
            P(("wide", "narrow"), None),
            P(("wide", "narrow")),
            P(("wide", "narrow"), None),
        ),
        check_vma=False,
    )
```

```python
import functools

import jax
import jax.numpy as jnp
from jax import lax
from jax.experimental import pallas as pl
from jax.experimental.pallas import tpu as pltpu
from jax.sharding import PartitionSpec as P

BUCKETS = 32
LANES = 128
CHUNK = 512
VM = (12, 12, 12, 16, 8)
COST = 1.1e9

epsilon = 1e-06
contrastive_sharpness_factor = 0.01
masked_value = -1000000000.0
bucket_edges = (12, 16, 23, 32, 46, 64, 91)
highest = lax.Precision.HIGHEST
f32 = jnp.float32
bf16 = jnp.bfloat16


def bucket_index(offset):
    distance = jnp.abs(offset)
    beyond = 8 + sum(((distance >= boundary).astype(jnp.int32) for boundary in bucket_edges))
    inside = jnp.where(distance < 8, distance, beyond)
    return inside + BUCKETS // 2 * (offset > 0).astype(jnp.int32)


def product(left, right):
    return jnp.dot(left, right, preferred_element_type=f32)


def left_product(left, right):
    return lax.dot_general(left, right, (((0,), (0,)), ((), ())), preferred_element_type=f32)


def right_product(left, right):
    return lax.dot_general(left, right, (((1,), (1,)), ((), ())), preferred_element_type=f32)


def rank_bits():
    return (lax.axis_size("wide") * lax.axis_size("narrow")).bit_length() - 1


def my_rank():
    return lax.axis_index("wide") * lax.axis_size("narrow") + lax.axis_index("narrow")


def swap(values, mask):
    ranks = 1 << rank_bits()
    pairs = [(rank, rank ^ mask) for rank in range(ranks)]
    return lax.ppermute(values, ("wide", "narrow"), pairs)


def scatter_order(position, order):
    count = len(order)
    return sum(((position >> (count - 1 - step)) & 1) << bit for step, bit in enumerate(order))


def gather_order(position, order):
    return sum(((position >> step) & 1) << bit for step, bit in enumerate(order))


def after(values, *others):
    flat, tree = jax.tree.flatten(values)
    done = lax.optimization_barrier(tuple(flat) + tuple(others))
    return jax.tree.unflatten(tree, done[: len(flat)])


def add(*values):
    total = values[0].astype(f32)
    for value in values[1:]:
        total = total + value.astype(f32)
    return total


def cut_kernel(kept_ref, came_ref, kept_out, sent_out):
    half = kept_out.shape[0]
    kept_out[...] = add(kept_ref[:half, :], came_ref[:half, :]).astype(bf16)
    sent_out[...] = add(kept_ref[half:, :], came_ref[half:, :]).astype(bf16)


def cut_loaded_kernel(kept_ref, came_ref, small_ref, kept_out, sent_out, small_out):
    half = kept_out.shape[0]
    kept_out[...] = add(kept_ref[:half, :], came_ref[:half, :]).astype(bf16)
    sent_out[:half, :] = add(kept_ref[half:, :], came_ref[half : 2 * half, :]).astype(bf16)
    small = add(small_ref[...], came_ref[2 * half :, :]).astype(bf16)
    sent_out[half:, :] = small
    small_out[...] = small


def cut(kept, came, small=None):
    half, cols = kept.shape[0] // 2, kept.shape[1]
    if half % 16 == 0 and small is None:
        return *call(cut_kernel, [shape((half, cols), bf16)] * 2, [kept, came], vmem=VM[4], us=0), None
    if half % 16 == 0:
        outs = [shape((half, cols), bf16), shape((half + 16, cols), bf16), shape((16, cols), bf16)]
        return call(cut_loaded_kernel, outs, [kept, came, small], vmem=VM[4], us=0)
    if small is not None:
        small = add(small, came[-16:]).astype(bf16)
        came = came[:-16]
    next_sent = add(kept[half:], came[half:]).astype(bf16)
    if small is not None:
        next_sent = jnp.concatenate([next_sent, small], 0)
    return add(kept[:half], came[:half]).astype(bf16), next_sent, small


def call(kernel, outs, args, spaces="", scratch=(), vmem=None, us=3, wide=False):
    kinds = {"s": pltpu.SMEM, "v": pltpu.VMEM, "a": pl.ANY, "h": pltpu.HBM}
    spaces = spaces.ljust(len(args) + len(outs), "v")
    specs = [pl.BlockSpec(memory_space=kinds[kind]) for kind in spaces]
    return pl.pallas_call(
        kernel,
        out_shape=tuple(outs),
        in_specs=specs[: len(args)],
        out_specs=tuple(specs[len(args) :]),
        scratch_shapes=list(scratch),
        compiler_params=pltpu.CompilerParams(vmem_limit_bytes=(60 if wide else vmem or VM[3]) * 1024 * 1024),
        cost_estimate=pl.CostEstimate(flops=int(us * COST), bytes_accessed=0, transcendentals=0),
    )(*args)


def shape(dims, kind=f32):
    return jax.ShapeDtypeStruct(tuple(dims), kind)


def room(values):
    return pltpu.VMEM(values.shape, values.dtype)


def loads(refs, rooms, sems):
    return [pltpu.make_async_copy(ref, place, sems.at[i]) for i, (ref, place) in enumerate(zip(refs, rooms))]


def bias_kernel(doc_length, rank_ref, table_ref, doc_bias_ref, slot_bias_ref, line_ref):
    pairs = doc_bias_ref.shape[0]
    parts = doc_length // LANES
    length = line_ref.shape[1]
    offset = lax.broadcasted_iota(jnp.int32, (BUCKETS, length), 1) - doc_length
    hot = (bucket_index(offset) == lax.broadcasted_iota(jnp.int32, (BUCKETS, length), 0)).astype(f32)
    line_ref[...] = lax.dot_general(
        table_ref[...], hot, (((0,), (0,)), ((), ())), precision=highest, preferred_element_type=f32
    )
    narrow = rank_ref[0] & (parts - 1)

    def spread(head, start):
        line = line_ref[pl.ds(head, 1), pl.ds(pl.multiple_of(start, LANES), 2 * LANES)]
        rolled = pltpu.roll(jnp.broadcast_to(line, (LANES, 2 * LANES)), 0, 1, stride=1, stride_axis=0)
        return rolled[:, LANES:]

    def one_pair(pair, carry):
        for side in range(2):
            rows = slice(side * LANES, (side + 1) * LANES)
            head = 2 * pair + side
            for part in range(parts):
                distance = (narrow ^ part) - narrow
                doc_bias_ref[pair, rows, part * LANES : (part + 1) * LANES] = spread(
                    head, doc_length - LANES + distance * LANES
                )
            slot_bias_ref[pair, rows, :] = spread(head, doc_length - LANES)
        return carry

    lax.fori_loop(0, pairs, one_pair, 0)


def count_kernel(doc_length, doc_total, rank_ref, picked_ref, counts_ref, tally_ref, load_ref, places_ref, scratch_ref, sem):
    slots, slot_length, picks = load_ref.shape
    rows = slots * slot_length
    blocks = counts_ref.shape[0]
    narrow_size = picked_ref.shape[0] // slots
    first = (rank_ref[0] & (narrow_size - 1)) * slots
    load = pltpu.make_async_copy(picked_ref.at[pl.ds(first, slots)], load_ref, sem)
    load.start()
    load.wait()

    places_ref[...] = load_ref[...].reshape(rows, picks)

    def one_row(row, carry):
        places = places_ref[pl.ds(row, 1), :]
        high = places >> 7
        low = places & 127
        high_hot = (lax.broadcasted_iota(jnp.int32, (blocks, picks), 0) == high).astype(bf16)
        low_hot = (lax.broadcasted_iota(jnp.int32, (LANES, picks), 0) == low).astype(bf16)
        scratch_ref[pl.ds(row, blocks, stride=rows), :] = right_product(high_hot, low_hot)
        return carry

    lax.fori_loop(0, rows, one_row, 0, unroll=8)

    def one_block(block, carry):
        start = pl.multiple_of(block * rows, rows)
        counts_ref[block] = scratch_ref[pl.ds(start, rows), :].astype(bf16)
        return carry

    lax.fori_loop(0, blocks, one_block, 0, unroll=4)

    owner = places_ref[...] // doc_length
    lane = lax.broadcasted_iota(jnp.int32, (rows, LANES), 1)
    tally = jnp.zeros((rows, LANES), f32)
    for doc in range(doc_total):
        number = jnp.sum((owner == doc).astype(f32), 1, keepdims=True)
        tally = jnp.where(lane == doc, number, tally)
    tally_ref[...] = tally


def rms_scale(values):
    return lax.rsqrt(jnp.mean(values * values, -1, keepdims=True) + epsilon)


def rms_back(values, gain, grad):
    scale = rms_scale(values)
    weighted = grad * gain
    inner = jnp.mean(weighted * values, -1, keepdims=True)
    return scale * weighted - values * (scale * scale * scale * inner)


def tile(index, size=LANES):
    return pl.ds(pl.multiple_of(index * size, size), size)


def halves(values, zero_row):
    return jnp.concatenate([jnp.where(zero_row, values, jnp.zeros((), values.dtype)),
                            jnp.where(zero_row, jnp.zeros((), values.dtype), values)], 0)


def joined(values, first_lanes):
    rows = values.shape[0] // 2
    return jnp.where(first_lanes, values[:rows], values[rows:])


def forward_kernel(
    slots, slot_length, rank_ref, lengths_ref, queries_ref, own_ref, near_ref, far_ref, last_ref, doc_bias_ref,
    slot_bias_ref, attend_gain_ref, feed_gain_ref, final_gain_ref,
    wq_ref, wk_ref, wv_ref, wo_ref, wg_ref, wu_ref, wd_ref, wp_ref,
    all_ref, query_ref, key_ref, value_ref, doc_probs_ref, slot_probs_ref, mixed_ref, after_attend_ref,
    normed_feed_ref, hidden_ref, gate_slope_ref, up_slope_ref, after_feed_ref, normed_final_ref, embed_ref,
    slot_unit_ref, doc_unit_ref,
    slot_ref, slot_sem,
):
    slot_rows = slots * slot_length
    rows, width = query_ref.shape
    pairs = doc_probs_ref.shape[0]
    half = LANES // 2
    narrow_size = queries_ref.shape[0] // slots
    first = (rank_ref[0] & (narrow_size - 1)) * slots
    load_slots = pltpu.make_async_copy(queries_ref.at[pl.ds(first, slots)], slot_ref, slot_sem)
    load_slots.start()
    gain = attend_gain_ref[...].reshape(1, width)
    place = slot_rows
    for ref in (own_ref, near_ref, far_ref, last_ref):
        tokens = ref[...].astype(f32)
        all_ref[place : place + ref.shape[0], :] = (tokens * rms_scale(tokens) * gain).astype(bf16)
        place += ref.shape[0]
    load_slots.wait()
    slot_tokens = slot_ref[...].reshape(slot_rows, width).astype(f32)
    all_ref[:slot_rows, :] = (slot_tokens * rms_scale(slot_tokens) * gain).astype(bf16)
    normed = all_ref[:rows, :]
    query_ref[...] = product(normed, wq_ref[...]).astype(bf16)
    key_ref[...] = product(all_ref[...], wk_ref[...]).astype(bf16)
    value_ref[...] = product(all_ref[...], wv_ref[...]).astype(bf16)

    lane = lax.broadcasted_iota(jnp.int32, (slot_rows, LANES), 1)
    row = lax.broadcasted_iota(jnp.int32, (slot_rows, slot_rows), 0)
    col = lax.broadcasted_iota(jnp.int32, (slot_rows, slot_rows), 1)
    slot_keep = row < 0
    for slot in range(slots):
        start = slot * slot_length
        inside = (row >= start) & (row < start + slot_length) & (col >= start)
        slot_keep = slot_keep | (inside & (col < start + lengths_ref[first + slot]))

    def softmax(scores):
        weights = jnp.exp(scores - jnp.max(scores, -1, keepdims=True))
        return (weights * (1.0 / jnp.sum(weights, -1, keepdims=True))).astype(bf16)

    first_lanes = lane < half
    pair_keep = jnp.concatenate([slot_keep, slot_keep], 0)

    def one_pair(pair, carry):
        lanes = tile(pair)
        slot_query = halves(query_ref[:slot_rows, lanes], first_lanes)
        scores = right_product(slot_query, key_ref[:slot_rows, lanes]) + slot_bias_ref[pair]
        probs = softmax(jnp.where(pair_keep, scores, masked_value))
        slot_probs_ref[pair] = probs
        slot_mixed = product(probs, value_ref[:slot_rows, lanes])
        mixed_ref[:slot_rows, lanes] = joined(slot_mixed, first_lanes).astype(bf16)
        doc_query = halves(query_ref[slot_rows:, lanes], first_lanes)
        scores = right_product(doc_query, key_ref[slot_rows:, lanes]) + doc_bias_ref[pair]
        probs = softmax(scores)
        doc_probs_ref[pair] = probs
        doc_mixed = product(probs, value_ref[slot_rows:, lanes])
        mixed_ref[slot_rows:, lanes] = joined(doc_mixed, first_lanes).astype(bf16)
        return carry

    lax.fori_loop(0, pairs, one_pair, 0, unroll=2)

    attended = product(mixed_ref[...], wo_ref[...])
    after_attend_ref[:slot_rows, :] = slot_ref[...].reshape(slot_rows, width).astype(f32) + attended[:slot_rows]
    after_attend_ref[slot_rows:, :] = own_ref[...].astype(f32) + attended[slot_rows:]
    after_attend = after_attend_ref[...]
    feed_gain = feed_gain_ref[...].reshape(1, width)
    normed_feed_ref[...] = (after_attend * rms_scale(after_attend) * feed_gain).astype(bf16)

    def one_part(step, carry):
        part = tile(step, CHUNK)
        gate = product(normed_feed_ref[...], wg_ref[:, part])
        upward = product(normed_feed_ref[...], wu_ref[:, part])
        factor = 0.7978845608028654
        square = gate * gate
        bent = jnp.tanh(factor * gate * (1.0 + 0.044715 * square))
        curve = 0.5 * gate * (1.0 + bent)
        slope = 0.5 * (1.0 + bent) + 0.5 * factor * gate * (1.0 - bent * bent) * (1.0 + 3 * 0.044715 * square)
        hidden_ref[:, part] = (curve * upward).astype(bf16)
        gate_slope_ref[:, part] = (upward * slope).astype(bf16)
        up_slope_ref[:, part] = curve.astype(bf16)
        return carry

    lax.fori_loop(0, hidden_ref.shape[1] // CHUNK, one_part, 0, unroll=2)
    after_feed = after_attend_ref[...] + product(hidden_ref[...], wd_ref[...])
    after_feed_ref[...] = after_feed
    final_gain = final_gain_ref[...].reshape(1, width)
    normed_final = (after_feed * rms_scale(after_feed) * final_gain).astype(bf16)
    normed_final_ref[...] = normed_final
    embed = product(normed_final, wp_ref[...])
    embed_ref[...] = embed
    unit = (embed * lax.rsqrt(jnp.sum(embed * embed, -1, keepdims=True) + epsilon)).astype(bf16)
    slot_unit_ref[...] = unit[:slot_rows]
    doc_unit_ref[...] = unit[slot_rows:]


def loss_kernel(
    order, gathered, doc_total, slots, rank_ref, lengths_ref, positives_ref, counts_ref, near_ref, far_ref, unit_ref,
    tally_ref, losses_ref, grad_ref, kept_ref, sent_ref, sum_ref, scaled_ref,
):
    rows = unit_ref.shape[0]
    blocks = counts_ref.shape[0]
    per_doc = blocks // doc_total
    rank = rank_ref[0]
    half = blocks // 2
    sum_ref[...] = jnp.zeros_like(sum_ref)

    def gather_step(place, carry):
        near = rank ^ gather_order(place, gathered)
        far = near ^ (1 << gathered[-1])
        sum_ref[near // per_doc] += product(counts_ref[near], near_ref[place])
        sum_ref[far // per_doc] += product(counts_ref[far], far_ref[place])
        return carry

    lax.fori_loop(0, half, gather_step, 0, unroll=4)

    unit = unit_ref[...].astype(f32)
    lane = lax.broadcasted_iota(jnp.int32, (rows, LANES), 1)
    summed = jnp.zeros((rows, LANES), f32)
    for doc in range(doc_total):
        number = jnp.sum(sum_ref[doc] * unit, 1, keepdims=True)
        summed = jnp.where(lane == doc, number, summed)
    tally = tally_ref[...]
    most = jnp.maximum(tally, 1.0)
    slot_length = rows // slots
    narrow_size = lengths_ref.shape[0] // slots
    first = (rank & (narrow_size - 1)) * slots
    row = lax.broadcasted_iota(jnp.int32, (rows, LANES), 0)
    slot_row = lax.broadcasted_iota(jnp.int32, (slots, LANES), 0)
    valid = row < 0
    positive = jnp.zeros((slots, LANES), jnp.int32)
    for slot in range(slots):
        start = slot * slot_length
        valid = valid | ((row >= start) & (row < start + lengths_ref[first + slot]))
        positive = jnp.where(slot_row == slot, positives_ref[first + slot], positive)
    weight = jnp.where(valid, jnp.minimum(tally, 1.0), 0.0)
    pooled = (weight * (summed / most)).reshape(slots, slot_length, LANES)
    weight_sum = jnp.maximum(jnp.sum(weight.reshape(slots, slot_length, LANES), 1), 1.0)
    scores = jnp.sum(pooled, 1) / weight_sum / contrastive_sharpness_factor
    slot_lane = lax.broadcasted_iota(jnp.int32, (slots, LANES), 1)
    inside = slot_lane < doc_total
    scores = jnp.where(inside, scores, -jnp.inf)
    top = jnp.max(scores, -1, keepdims=True)
    powers = jnp.exp(scores - top)
    total = jnp.sum(powers, -1, keepdims=True)
    chosen = (slot_lane == positive).astype(f32)
    picked = jnp.sum(jnp.where(slot_lane == positive, scores, 0.0), -1, keepdims=True)
    losses_ref[...] = jnp.broadcast_to(top + jnp.log(total) - picked, (slots, LANES))
    slope = (powers / total - chosen) / contrastive_sharpness_factor / weight_sum
    slope = jnp.where(inside, slope, 0.0)
    slope = jnp.broadcast_to(slope[:, None, :], (slots, slot_length, LANES)).reshape(rows, LANES)
    slope = slope * weight / most

    grad = jnp.zeros((rows, unit.shape[1]), f32)
    for doc in range(doc_total):
        column = jnp.sum(jnp.where(lane == doc, slope, 0.0), 1, keepdims=True)
        grad = grad + column * sum_ref[doc]
        scaled_ref[doc] = (column * unit).T.astype(bf16)
    grad_ref[...] = grad

    def scatter_step(place, carry):
        kept = rank ^ scatter_order(place, order)
        sent = kept ^ (1 << order[0])
        kept_ref[place] = product(scaled_ref[kept // per_doc], counts_ref[kept]).astype(bf16)
        sent_ref[place] = product(scaled_ref[sent // per_doc], counts_ref[sent]).astype(bf16)
        return carry

    lax.fori_loop(0, half, scatter_step, 0, unroll=4)


def feed_back(
    part, grad_unit, embed_ref, after_feed_ref, after_attend_ref, gate_slope_ref, up_slope_ref, feed_gain_ref,
    final_gain_ref, wo_ref, wg_ref, wu_ref, wd_ref, wp_ref, grads_out, after_out, mixed_out, more_ref,
):
    units, width = wd_ref.shape
    up_start, feed_start = units, 2 * units
    attend_start, embed_start = 2 * units + width, 2 * units + 2 * width
    embed = embed_ref[part, :]
    scale = lax.rsqrt(jnp.sum(embed * embed, -1, keepdims=True) + epsilon)
    inner = jnp.sum(grad_unit * embed, -1, keepdims=True)
    grad_embed = (scale * grad_unit - embed * (scale * scale * scale * inner)).astype(bf16)
    grads_out[:, embed_start : embed_start + embed.shape[1]] = grad_embed
    grad_after_feed = rms_back(
        after_feed_ref[part, :], final_gain_ref[...].reshape(1, -1), right_product(grad_embed, wp_ref[...])
    )
    after_out[...] = grad_after_feed
    grad_feed = grad_after_feed.astype(bf16)
    grads_out[:, feed_start:attend_start] = grad_feed
    def one_part(step, total):
        cols = tile(step, CHUNK)
        grad_hidden = right_product(grads_out[:, feed_start:attend_start], wd_ref[cols, :])
        grad_gate = (grad_hidden * gate_slope_ref[part, cols].astype(f32)).astype(bf16)
        grad_up = (grad_hidden * up_slope_ref[part, cols].astype(f32)).astype(bf16)
        grads_out[:, cols] = grad_gate
        grads_out[:, pl.ds(pl.multiple_of(up_start + step * CHUNK, CHUNK), CHUNK)] = grad_up
        more_ref[...] += right_product(grad_gate, wg_ref[:, cols]) + right_product(grad_up, wu_ref[:, cols])
        return total

    more_ref[...] = jnp.zeros_like(more_ref)
    lax.fori_loop(0, units // CHUNK, one_part, 0, unroll=2)
    total = more_ref[...]
    more = rms_back(after_attend_ref[part, :], feed_gain_ref[...].reshape(1, -1), total)
    grad_after_attend = after_out[...] + more
    after_out[...] = grad_after_attend
    grad_attend = grad_after_attend.astype(bf16)
    grads_out[:, attend_start:embed_start] = grad_attend
    mixed_out[...] = right_product(grad_attend, wo_ref[...]).astype(bf16)


def attend_back(
    far_parts, queries, keys, query_ref, key_ref, value_ref, probs_ref, mixed_ref, query_out, key_out, value_out,
    sums_out,
):
    rows = mixed_ref.shape[0]
    length = probs_ref.shape[2]
    half = LANES // 2
    first_lanes = lax.broadcasted_iota(jnp.int32, (rows, LANES), 1) < half
    row = lax.broadcasted_iota(jnp.int32, (rows, rows), 0)
    col = lax.broadcasted_iota(jnp.int32, (rows, rows), 1)
    flip = (row + col == rows - 1).astype(bf16)
    nothing = jnp.zeros((rows, LANES), f32)

    def one_pair(pair, carry):
        lanes = tile(pair)
        grad_mixed = halves(mixed_ref[:, lanes], first_lanes)
        query = halves(query_ref[queries, lanes], first_lanes)
        probs = probs_ref[pair]
        grad_probs = right_product(grad_mixed, value_ref[keys, lanes])
        exact = probs.astype(f32)
        inner = jnp.sum(exact * grad_probs, -1, keepdims=True)
        grad_scores = (exact * (grad_probs - inner)).astype(bf16)
        query_out(joined(product(grad_scores, key_ref[keys, lanes]), first_lanes).astype(bf16), pair)
        key_out(left_product(grad_scores, query).astype(bf16), pair)
        value_out(left_product(probs, grad_mixed).astype(bf16), pair)
        for side in range(2):
            head = 2 * pair + side
            own = grad_scores[side * rows : (side + 1) * rows, :]
            for part in range(length // LANES):
                piece = own[:, part * LANES : (part + 1) * LANES]
                if part in far_parts:
                    line = jnp.concatenate([piece.astype(f32), nothing], 1)
                else:
                    line = pltpu.roll(
                        jnp.concatenate([product(flip, piece), nothing], 1), 0, 1, stride=1, stride_axis=0
                    )
                sums_out[tile(head, 8), part * 2 * LANES : (part + 1) * 2 * LANES] = jnp.sum(
                    line.reshape(rows // 8, 8, 2 * LANES), 0
                )
        return carry

    lax.fori_loop(0, probs_ref.shape[0], one_pair, 0, unroll=2)


def input_back(tokens, gain_ref, after_ref, query, key, value, wq_ref, wk_ref, wv_ref):
    grad_normed = right_product(query, wq_ref[...])
    grad_normed = grad_normed + right_product(key, wk_ref[...])
    grad_normed = grad_normed + right_product(value, wv_ref[...])
    return after_ref[...] + rms_back(tokens, gain_ref[...].reshape(1, -1), grad_normed)


def table_sums(sums_ref, distances):
    heads = sums_ref.shape[0] // 8
    span = lax.broadcasted_iota(jnp.int32, (2 * LANES, LANES), 0) - (LANES - 1)
    bucket = lax.broadcasted_iota(jnp.int32, (2 * LANES, LANES), 1)
    total = jnp.zeros((heads, LANES), f32)
    for part, distance in enumerate(distances):
        lines = jnp.sum(sums_ref[:, part * 2 * LANES : (part + 1) * 2 * LANES].reshape(heads, 8, 2 * LANES), 1)
        hot = (bucket_index(span + distance * LANES) == bucket).astype(f32)
        total = total + lax.dot_general(
            lines, hot, (((1,), (0,)), ((), ())), precision=highest, preferred_element_type=f32
        )
    return total


def slot_feed_kernel(
    grad_unit_ref, embed_ref, after_feed_ref, after_attend_ref, gate_slope_ref, up_slope_ref, feed_gain_ref,
    final_gain_ref, wp_ref, wd_ref, wg_ref, wu_ref, wo_ref,
    grads_out, after_out, mixed_out, more_ref,
):
    feed_back(
        slice(0, after_out.shape[0]), grad_unit_ref[...], embed_ref, after_feed_ref, after_attend_ref,
        gate_slope_ref, up_slope_ref, feed_gain_ref, final_gain_ref, wo_ref, wg_ref, wu_ref, wd_ref, wp_ref, grads_out,
        after_out, mixed_out, more_ref,
    )


def slot_attend_kernel(
    query_ref, key_ref, value_ref, probs_ref, mixed_ref, grads_out, table_out, sums_ref
):
    rows, width = mixed_ref.shape

    def out(place):
        def store(values, pair):
            grads_out[:, pl.ds(pl.multiple_of(place * width + pair * LANES, LANES), LANES)] = values

        return store

    part = slice(0, rows)
    attend_back(
        (), part, part, query_ref, key_ref, value_ref, probs_ref, mixed_ref, out(0), out(1), out(2), sums_ref
    )
    table_out[...] = table_sums(sums_ref, [0])


def doc_feed_kernel(came, *refs):
    parts, refs = refs[:came], refs[came:]
    (
        embed_ref, after_feed_ref, after_attend_ref, gate_slope_ref, up_slope_ref, feed_gain_ref, final_gain_ref,
        wp_ref, wd_ref, wg_ref, wu_ref, wo_ref,
        grads_out, after_out, mixed_out, more_ref,
    ) = refs
    rows = after_out.shape[0]
    grad_unit = add(*(part[0] for part in parts)).T
    feed_back(
        slice(embed_ref.shape[0] - rows, embed_ref.shape[0]), grad_unit, embed_ref, after_feed_ref,
        after_attend_ref, gate_slope_ref, up_slope_ref, feed_gain_ref, final_gain_ref, wo_ref, wg_ref, wu_ref, wd_ref,
        wp_ref, grads_out, after_out, mixed_out, more_ref,
    )


def doc_attend_kernel(
    rank_ref, query_ref, key_ref, value_ref, probs_ref, mixed_ref, slot_table_ref, grads_out, table_out, query_room,
    sums_ref,
):
    rows, width = query_room.shape
    length = probs_ref.shape[2]
    first = key_ref.shape[0] - length

    def query_out(values, pair):
        query_room[:, tile(pair)] = values

    def key_out(values, pair):
        grads_out[:length, tile(pair)] = values

    def value_out(values, pair):
        grads_out[:length, pl.ds(pl.multiple_of(width + pair * LANES, LANES), LANES)] = values

    attend_back(
        (2,), slice(first, first + rows), slice(first, key_ref.shape[0]), query_ref, key_ref, value_ref, probs_ref,
        mixed_ref, query_out, key_out, value_out, sums_ref,
    )
    grads_out[length:, :width] = query_room[: rows // 2, :]
    grads_out[length:, width:] = query_room[rows // 2 :, :]
    parts = length // LANES
    narrow = rank_ref[0] & (parts - 1)
    table = table_sums(sums_ref, [(narrow ^ part) - narrow for part in range(parts)]) + slot_table_ref[...]
    heads = table.shape[0]
    table_out[...] = jnp.concatenate([table, jnp.zeros((16 - heads, LANES), f32)], 0).astype(bf16)


def pick_columns(values, total, order, flipped, rank):
    count = 1 << len(order) + 1
    size = total // count
    row = lax.broadcasted_iota(jnp.int32, (total, total // 2), 0)
    col = lax.broadcasted_iota(jnp.int32, (total, total // 2), 1)
    source = (scatter_order(col // size, order) ^ rank ^ flipped) * size + col % size
    return product(values, (row == source).astype(bf16)).astype(bf16)


def pick_tiles(values_ref, order, flipped, rank, store):
    rows = values_ref.shape[0]
    half = LANES // 2
    first_lanes = lax.broadcasted_iota(jnp.int32, (rows, LANES), 1) < half
    upper = ((rank ^ flipped) & 1) == 1

    def one_tile(step, carry):
        place = 2 * step
        sides = []
        for side in range(2):
            tile = (rank ^ scatter_order(place + side, order)) >> 1
            values = values_ref[:, pl.ds(pl.multiple_of(tile * LANES, LANES), LANES)].astype(f32)
            turned = pltpu.roll(values, half, 1)
            sides.append(jnp.where(upper, turned, values) if side == 0 else jnp.where(upper, values, turned))
        store(step, jnp.where(first_lanes, sides[0], sides[1]).astype(bf16))
        return carry

    lax.fori_loop(0, 1 << len(order) - 1, one_tile, 0)


def turn_kernel(
    orders, rank_ref, all_ref, normed_feed_ref, mixed_ref, normed_final_ref, hidden_ref, kept_out, sent_out, doc_out,
):
    first, second, third, fourth = orders
    rank = rank_ref[0]
    rows, width = normed_feed_ref.shape
    units = hidden_ref.shape[1]
    slots = all_ref.shape[0] - doc_out.shape[0]
    half = width // 2
    for out, flipped in ((kept_out, 0), (sent_out, 1)):
        out[:, :half] = pick_columns(normed_feed_ref[...], width, first, flipped, rank)
        out[:, half : 2 * half] = pick_columns(normed_feed_ref[...], width, second, flipped, rank)
        out[:, 2 * half : 3 * half] = pick_columns(mixed_ref[...], width, first, flipped, rank)
        out[:, 3 * half : 4 * half] = pick_columns(normed_final_ref[...], width, second, flipped, rank)
        start = 4 * half
        if units >> (len(third) + 1) == LANES // 2:

            def store(place, values):
                out[:, pl.ds(pl.multiple_of(start + place * LANES, LANES), LANES)] = values

            pick_tiles(hidden_ref, third, flipped, rank, store)
        else:
            out[:, start : start + units // 2] = pick_columns(hidden_ref[...], units, third, flipped, rank)
        start = start + units // 2
        out[slots:, start:] = jnp.zeros((rows - slots, half), bf16)
        if flipped:
            out[:slots, start:] = pick_columns(all_ref[:slots, :], width, fourth, flipped, rank)
        else:
            both = pick_columns(all_ref[...], width, fourth, flipped, rank)
            out[:slots, start:] = both[:slots]
            doc_out[...] = both[slots:]


def store_product(left, right_ref, columns, kept_ref, sent_ref, start):
    half = left.shape[1] // 2
    size = 2 * LANES

    def one_part(first, size):
        here = pl.ds(pl.multiple_of(start + first, LANES), size)
        result = left_product(left, right_ref[:, pl.ds(pl.multiple_of(first, LANES), size)]).astype(bf16)
        kept_ref[:half, here] = result[:half]
        sent_ref[:half, here] = result[half:]

    def step(place, carry):
        one_part(place * size, size)
        return carry

    lax.fori_loop(0, columns // size, step, 0, unroll=2)
    if columns % size:
        one_part(columns // size * size, columns % size)


def weight_kernel(
    terms, kept_any, came_any, slot_any, slot_came_any, doc_any, doc_came_any, kept_ref, sent_ref, left_ref, right_ref,
    sems,
):
    rows = kept_any.shape[0]
    part = slot_any.shape[0]
    copies = []
    left_place, right_place = 0, 0
    for left_start, left_width, right_start, right_width in terms:
        pieces = []
        for place, ref in enumerate((kept_any, came_any)):
            source = ref.at[:, left_start : left_start + left_width]
            target = left_ref.at[place * rows : (place + 1) * rows, left_place : left_place + left_width]
            pieces.append((source, target))
        for place, ref in enumerate((slot_any, doc_any, slot_came_any, doc_came_any)):
            source = ref.at[:, right_start : right_start + right_width]
            target = right_ref.at[place * part : (place + 1) * part, right_place : right_place + right_width]
            pieces.append((source, target))
        first = sum(len(group) for group in copies)
        copies.append(
            [pltpu.make_async_copy(one, two, sems.at[first + i]) for i, (one, two) in enumerate(pieces)]
        )
        left_place += left_width
        right_place += right_width
    for group in copies:
        for copy in group:
            copy.start()
    left_place, right_place = 0, 0
    for group, (_, left_width, _, right_width) in zip(copies, terms):
        for copy in group:
            copy.wait()
        left = left_ref[:, left_place : left_place + left_width]
        right = right_ref.at[:, right_place : right_place + right_width]
        store_product(left, right, right_width, kept_ref, sent_ref, right_place)
        left_place += left_width
        right_place += right_width


def attend_weight_kernel(
    doc_ref, kept_any, came_any, slot_any, slot_came_any, grads_ref, other_ref, table_ref, other_table_ref,
    kept_out, sent_out, pair_kept, pair_sent, slot_room, slot_came_room, left_ref, right_ref, query_ref, sems,
):
    rows = slot_any.shape[0]
    width = slot_room.shape[1] // 3
    half = doc_ref.shape[1]
    length = doc_ref.shape[0]
    lanes = slice(kept_any.shape[1] - half, kept_any.shape[1])
    copies = loads(
        (slot_any, slot_came_any, kept_any.at[:rows, lanes], came_any.at[:rows, lanes]),
        (slot_room, slot_came_room, left_ref.at[length : length + rows, :], left_ref.at[length + rows :, :]),
        sems,
    )
    for copy in copies:
        copy.start()
    left_ref[:length, :] = doc_ref[...]
    for part in range(length // LANES):
        here = slice(part * LANES, (part + 1) * LANES)
        there = slice((part ^ 1) * LANES, ((part ^ 1) + 1) * LANES)
        right_ref[here, :] = add(grads_ref[here, :], other_ref[there, :]).astype(bf16)
    pair_kept[...] = right_ref[:LANES, :]
    pair_sent[...] = right_ref[2 * LANES : 3 * LANES, :]
    small = LANES // 2
    for place, ref in enumerate((grads_ref, other_ref)):
        query_ref[2 * place * small : (2 * place + 1) * small, :] = ref[length:, :width]
        query_ref[(2 * place + 1) * small : (2 * place + 2) * small, :] = ref[length:, width:]
    for copy in copies:
        copy.wait()
    right_ref[length : length + rows, :] = slot_room[:, width:]
    right_ref[length + rows :, :] = slot_came_room[:, width:]
    query_ref[2 * LANES : 2 * LANES + rows, :] = slot_room[:, :width]
    query_ref[2 * LANES + rows :, :] = slot_came_room[:, :width]
    store_product(left_ref[...], right_ref, 2 * width, kept_out, sent_out, width)
    left = jnp.concatenate([left_ref[: 2 * LANES, :], left_ref[length:, :]], 0)
    store_product(left, query_ref, width, kept_out, sent_out, 0)
    tail = sent_out.shape[0] - 16
    sent_out[tail:, :] = jnp.zeros((16, sent_out.shape[1]), bf16)
    sent_out[tail:, :LANES] = add(table_ref[...], other_table_ref[...]).astype(bf16)


def doc_input_kernel(
    tokens_ref, gain_ref, after_ref, grads_ref, kept_ref, came_ref, wq_ref, wk_ref, wv_ref, tokens_out
):
    rows, width = tokens_ref.shape
    rest = grads_ref.shape[0] - rows // 2
    query = jnp.concatenate([grads_ref[rest:, :width], grads_ref[rest:, width:]], 0)
    pair = add(kept_ref[...], came_ref[...]).astype(bf16)
    tokens_out[...] = input_back(
        tokens_ref[...].astype(f32), gain_ref, after_ref, query, pair[:, :width], pair[:, width:], wq_ref, wk_ref, wv_ref
    )


def slot_input_kernel(
    slots, rank_ref, tokens_any, gain_ref, after_ref, grads_ref, wq_ref, wk_ref, wv_ref, tokens_out, slot_room, sem
):
    narrow_size = tokens_any.shape[0] // slots
    first = (rank_ref[0] & (narrow_size - 1)) * slots
    load = pltpu.make_async_copy(tokens_any.at[pl.ds(first, slots)], slot_room, sem)
    load.start()
    load.wait()
    width = tokens_out.shape[1]
    query, key, value = (grads_ref[:, place * width : (place + 1) * width] for place in range(3))
    tokens_out[...] = input_back(
        slot_room[...].reshape(tokens_out.shape).astype(f32), gain_ref, after_ref, query, key, value, wq_ref, wk_ref,
        wv_ref,
    )


def on_device(
    doc_tokens, query_tokens, query_lengths, positive_docs, retrieved, attend_gain, query_weight, key_weight,
    value_weight, output_weight, bias_table, feed_gain, gate_weight, up_weight, down_weight, final_gain, proj_weight,
):
    narrow_size = lax.axis_size("narrow")
    bits = rank_bits()
    rank = my_rank()
    rank_word = rank.astype(jnp.int32).reshape(1)
    doc_rows, width = doc_tokens.shape[1:]
    doc_length = doc_rows * narrow_size
    doc_total = doc_tokens.shape[0] * lax.axis_size("wide")
    slots = query_tokens.shape[0] // narrow_size
    slot_length = query_tokens.shape[1]
    heads = bias_table.shape[1]
    units = gate_weight.shape[1]
    columns = proj_weight.shape[1]
    slot_rows = slots * slot_length
    rows = slot_rows + doc_rows
    blocks = doc_total * doc_length // LANES
    assert doc_tokens.shape[0] == 1 and doc_rows == LANES and slot_rows == LANES and narrow_size == 4
    assert columns == LANES and doc_total <= LANES and blocks == 1 << bits
    gains = (attend_gain, feed_gain, final_gain)
    dma = pltpu.SemaphoreType.DMA
    waxes = list(range(3, bits))

    orders = (
        [2] + [1] + waxes[:1] + waxes[1:],
        waxes[:1] + [1] + [2] + waxes[1:],
        [2] + [1] + waxes[:1] + waxes[1:],
        [1] + waxes[:1] + [2] + waxes[1:],
    )
    own_tokens = doc_tokens[0]
    y_tokens = swap(own_tokens, 2)
    core_tokens = swap(own_tokens, 1)
    pairs = heads // 2
    doc_bias, slot_bias = call(
        functools.partial(bias_kernel, doc_length),
        [shape((pairs, 2 * doc_rows, doc_length)), shape((pairs, 2 * slot_rows, slot_rows))],
        [rank_word, bias_table],
        "s",
        [pltpu.VMEM((heads, 2 * doc_length + LANES), f32)],
    )
    counts, tally = call(
        functools.partial(count_kernel, doc_length, doc_total),
        [shape((blocks, slot_rows, LANES), bf16), shape((slot_rows, LANES))],
        [rank_word, after(retrieved, slot_bias)],
        "sa",
        [
            pltpu.VMEM((slots, slot_length, retrieved.shape[2]), jnp.int32),
            pltpu.VMEM((slot_rows, retrieved.shape[2]), jnp.int32),
            pltpu.VMEM((blocks * slot_rows, LANES), f32),
            dma,
        ],
        us=5,
        wide=bits > 5,
    )
    y_tokens = after(y_tokens, doc_bias, tally)
    both_tokens = swap(y_tokens, 1)

    all_rows = slot_rows + doc_length
    forward_shapes = [
        shape((all_rows, width), bf16),
        shape((rows, width), bf16),
        shape((all_rows, width), bf16),
        shape((all_rows, width), bf16),
        shape((pairs, 2 * doc_rows, doc_length), bf16),
        shape((pairs, 2 * slot_rows, slot_rows), bf16),
        shape((rows, width), bf16),
        shape((rows, width)),
        shape((rows, width), bf16),
        shape((rows, units), bf16),
        shape((rows, units), bf16),
        shape((rows, units), bf16),
        shape((rows, width)),
        shape((rows, width), bf16),
        shape((rows, columns)),
        shape((slot_rows, columns), bf16),
        shape((doc_rows, columns), bf16),
    ]
    weights = [
        query_weight, key_weight, value_weight, output_weight, gate_weight, up_weight, down_weight, proj_weight,
    ]
    slot_room = pltpu.VMEM((slots, slot_length, width), bf16)
    (
        all_normed, query, key, value, doc_probs, slot_probs, mixed, after_attend, normed_feed, hidden, gate_slope,
        up_slope, after_feed, normed_final, embed, slot_unit, doc_unit,
    ) = call(
        functools.partial(forward_kernel, slots, slot_length),
        forward_shapes,
        [
            rank_word, query_lengths, query_tokens, own_tokens, core_tokens, y_tokens, both_tokens, doc_bias, slot_bias,
            *gains, *weights,
        ],
        "ssa" + "v" * 9 + "v" * 8 + "v" * len(forward_shapes),
        [slot_room, dma],
        vmem=VM[0],
        us=18,
    )

    phases = [list(range(high, max(high - 2, 0), -1)) for high in range(bits - 1, 0, -2)]
    gathered = []
    near_units = doc_unit[None]
    for phase, group in enumerate(phases):
        group = group[::-1]
        masks = [gather_order(place, group) for place in range(1, 1 << len(group))]
        came = [swap(near_units, mask) for mask in masks]
        if phase == 0:
            pass
        if phase == 1:
            turned_cols = 5 * width // 2 + units // 2
            turned, turned_sent, turned_docs = call(
                functools.partial(turn_kernel, orders),
                [shape((rows, turned_cols), bf16)] * 2 + [shape((doc_length, width // 2), bf16)],
                after([rank_word, all_normed, normed_feed, mixed, normed_final, hidden], near_units),
                "s",
                us=5,
                wide=bits > 5,
            )
            came = after(came, turned)
        near_units = jnp.concatenate([near_units] + came, 0)
        gathered = gathered + group
    gathered = gathered + [0]
    far_units = swap(near_units, 1)

    order = list(range(bits))
    half = blocks // 2
    losses, grad_slot_unit, kept, sent = call(
        functools.partial(loss_kernel, order, gathered, doc_total, slots),
        [
            shape((slots, LANES)),
            shape((slot_rows, columns)),
            shape((half, columns, LANES), bf16),
            shape((half, columns, LANES), bf16),
        ],
        [rank_word, query_lengths, positive_docs, counts, near_units, far_units, slot_unit, tally],
        "sss",
        [
            pltpu.VMEM((doc_total, slot_rows, columns), f32),
            pltpu.VMEM((doc_total, columns, slot_rows), bf16),
        ],
        wide=bits > 5,
    )
    back_weights = [proj_weight, down_weight, gate_weight, up_weight, output_weight]
    doc_cols = 2 * units + 2 * width + columns

    came = [swap(sent, 1)]
    rest = order[1:]
    parts = [kept]
    phase = 0
    feed_shapes = [shape((LANES, doc_cols), bf16), shape((LANES, width)), shape((LANES, width), bf16)]
    while rest:
        group, rest = rest[:2], rest[2:]
        count = 1 << len(group)
        size = parts[0].shape[0] // count
        pieces = []
        for place in range(count):
            here = slice(place * size, (place + 1) * size)
            pieces.append(add(*(part[here] for part in parts), *(one[here] for one in came)).astype(bf16))
        masks = [scatter_order(place, group) for place in range(count)]
        came = [swap(piece, mask) for piece, mask in zip(pieces[1:], masks[1:])]
        parts = [pieces[0]]
        if phase == 0:
            slot_grads, slot_after, slot_mixed = call(
                slot_feed_kernel,
                feed_shapes,
                [after(grad_slot_unit, pieces[1])]
                + [embed, after_feed, after_attend, gate_slope, up_slope, gains[1], gains[2]]
                + back_weights,
                "",
                [pltpu.VMEM((slot_rows, width), f32)],
                vmem=VM[1],
                us=7,
            )
            came = after(came, slot_after)
        if phase == 1:
            slot_came = swap(after(slot_grads, *pieces[1:]), 1)
            turned_came = swap(after(turned_sent, *pieces[1:]), 1)
            slot_thirds, slot_table = call(
                slot_attend_kernel,
                [shape((slot_rows, 3 * width), bf16), shape((heads, LANES))],
                [query, key, value, slot_probs, after(slot_mixed, *pieces[1:])],
                scratch=[pltpu.VMEM((heads * 8, 2 * LANES), f32)],
                us=4,
            )
            came = after(came, slot_table)
        phase += 1

    doc_grads, doc_after, doc_mixed = call(
        functools.partial(doc_feed_kernel, 1 + len(came)),
        feed_shapes,
        parts + after(came, slot_came, turned_came)
        + [embed, after_feed, after_attend, gate_slope, up_slope, gains[1], gains[2]]
        + back_weights,
        "",
        [pltpu.VMEM((doc_rows, width), f32)],
        vmem=VM[2],
        us=7,
    )
    thirds_came = swap(after(slot_thirds, doc_after), 1)
    doc_came = swap(doc_grads, 1)

    class Stream:
        def __init__(self, kept, sent, order):
            self.kept, self.order, self.step = kept, order, 0
            self.loaded = sent.shape[0] > kept.shape[0]
            self.small = sent[-16:] if self.loaded else None
            self.send(sent)

        def send(self, sent):
            self.came = swap(sent, 1 << self.order[self.step])
            self.step += 1

        def advance(self, *wait):
            came = after(self.came, *wait)
            if self.step == len(self.order):
                if self.loaded:
                    self.small = add(self.small, came[-16:]).astype(bf16)
                    came = came[:-16]
                self.result = add(self.kept, came)
                return self.result
            self.kept, sent, self.small = cut(self.kept, came, self.small)
            self.send(sent)
            return self.kept

    def weight_product(terms, order, *wait):
        left = sum(term[1] for term in terms)
        right = sum(term[3] for term in terms)
        tall = terms[0][1] // 2
        args = after([turned, turned_came, slot_grads, slot_came, doc_grads, doc_came], *wait)
        kept, sent = call(
            functools.partial(weight_kernel, terms),
            [shape((tall, right), bf16)] * 2,
            args,
            "a" * 6,
            [pltpu.VMEM((2 * rows, left), bf16), pltpu.VMEM((2 * rows, right), bf16), dma((6 * len(terms),))],
        )
        return Stream(kept, sent, order)

    small_half = width // 2
    att_grads, table = call(
        doc_attend_kernel,
        [shape((doc_length + doc_rows // 2, 2 * width), bf16), shape((16, LANES), bf16)],
        [rank_word, query, key, value, doc_probs, doc_mixed, slot_table],
        "s",
        [pltpu.VMEM((doc_rows, width), bf16), pltpu.VMEM((heads * 8, 2 * doc_length), f32)],
    )
    att_came, table_came = swap(att_grads, 1), swap(table, 1)
    first = weight_product(
        [(0, small_half, 0, units), (2 * small_half, small_half, 2 * units + width, width)], orders[0], table
    )
    fourth_kept, fourth_sent, pair_kept, pair_sent = call(
        attend_weight_kernel,
        [
            shape((width // 4, 3 * width), bf16),
            shape((width // 4 + 16, 3 * width), bf16),
            shape((doc_rows, 2 * width), bf16),
            shape((doc_rows, 2 * width), bf16),
        ],
        [turned_docs, turned, turned_came, slot_thirds, thirds_came, att_grads, att_came, after(table, first.kept), table_came],
        "vaaaa",
        [
            pltpu.VMEM((slot_rows, 3 * width), bf16),
            pltpu.VMEM((slot_rows, 3 * width), bf16),
            pltpu.VMEM((doc_length + 2 * slot_rows, width // 2), bf16),
            pltpu.VMEM((doc_length + 2 * slot_rows, 2 * width), bf16),
            pltpu.VMEM((2 * doc_rows + 2 * slot_rows, width), bf16),
            dma((4,)),
        ],
    )
    fourth = Stream(fourth_kept, fourth_sent, orders[3])
    second = weight_product(
        [(small_half, small_half, units, units), (3 * small_half, small_half, 2 * units + 2 * width, columns)],
        orders[1],
        fourth_kept,
    )
    third = weight_product([(4 * small_half, units // 2, 2 * units, width)], orders[2], second.kept)
    def own_rows(values):
        return lax.dynamic_slice_in_dim(values, rank * (width >> bits), width >> bits, 0).astype(f32)

    def gain_grad(gain, *pairs):
        return sum(jnp.sum(own_rows(weight) * grad, 1) for weight, grad in pairs) / own_rows(gain)

    streams = {"A": first, "B": second, "C": third, "D": fourth}
    plan = "JADBACDpBADCBICABDCfa"
    if bits != 5:
        plan = "J" + "ADBC" + "p" + "ADBC" * (bits - 3) + "I" + "ABfDaC"
    done = third.kept
    for event in plan:
        if event in streams:
            done = streams[event].advance(done)
        elif event == "p":
            pair_came = swap(after(pair_sent, done), 2)
        elif event == "f":
            gate_grad, output_grad = first.result[:, :units], first.result[:, units:]
            up_grad, proj_grad = second.result[:, :units], second.result[:, units:]
            feed_gain_grad = gain_grad(feed_gain, (gate_weight, gate_grad), (up_weight, up_grad))
            final_gain_grad = gain_grad(final_gain, (proj_weight, proj_grad))
            done = jnp.concatenate([feed_gain_grad, final_gain_grad])
            feed_gain_grad, final_gain_grad = done[: width >> bits], done[width >> bits :]
        elif event == "a":
            query_g, key_g, value_g = (fourth.result[:, place * width : (place + 1) * width] for place in range(3))
            done = gain_grad(attend_gain, (query_weight, query_g), (key_weight, key_g), (value_weight, value_g))
            attend_gain_grad = done
        elif event == "I":
            (done,) = call(
                doc_input_kernel,
                [shape((doc_rows, width))],
                [own_tokens, gains[0], doc_after, att_grads, pair_kept, after(pair_came, done)]
                + [query_weight, key_weight, value_weight],
                us=3,
            )
            doc_grad = done
        else:
            (done,) = call(
                functools.partial(slot_input_kernel, slots),
                [shape((slot_rows, width))],
                [rank_word, query_tokens, gains[0], slot_after, after(slot_thirds, done)]
                + [query_weight, key_weight, value_weight],
                "sa",
                [slot_room, dma],
                us=3,
            )
            query_grad = done
    return (
        losses[:, 0],
        doc_grad[None],
        query_grad.reshape(slots, slot_length, width),
        attend_gain_grad,
        query_g,
        key_g,
        value_g,
        output_grad,
        fourth.small[:heads, :BUCKETS].astype(f32).T,
        feed_gain_grad,
        gate_grad,
        up_grad,
        third.result,
        final_gain_grad,
        proj_grad,
    )


def solution(mesh):
    return jax.shard_map(
        on_device,
        mesh=mesh,
        in_specs=(
            P("wide", "narrow", None),
            P("wide", None, None),
            P("wide"),
            P("wide"),
            P("wide", None, None),
            P(),
            P(),
            P(),
            P(),
            P(),
            P(),
            P(),
            P(),
            P(),
            P(),
            P(),
            P(),
        ),
        out_specs=(
            P(("wide", "narrow")),
            P("wide", "narrow", None),
            P(("wide", "narrow"), None, None),
            P(("wide", "narrow")),
            P(("wide", "narrow"), None),
            P(("wide", "narrow"), None),
            P(("wide", "narrow"), None),
            P(("wide", "narrow"), None),
            P(),
            P(("wide", "narrow")),
            P(("wide", "narrow"), None),
            P(("wide", "narrow"), None),
            P(("wide", "narrow"), None),
            P(("wide", "narrow")),
            P(("wide", "narrow"), None),
        ),
        check_vma=False,
    )
```
